256 devices in a mesh: grp: 4 (over z_hi, core), seq: 64 (over x, z_lo, y).
Axes of the slice: x: 4, y: 4, z: 8 (z_hi: 2, z_lo: 4; z = z_hi * 4 + z_lo), core: 2. Of those that a mesh axis runs over, the one named last changes fastest.
Arguments:
- queries: bfloat16 [524288, 128], P(('grp', 'seq')), may hold values from -6 to 6
- keys: bfloat16 [524288, 128], P(('grp', 'seq')), may hold values from -6 to 6
- values: bfloat16 [524288, 128], P(('grp', 'seq')), may hold values from -6 to 6
- cotangent: bfloat16 [524288, 128], P(('grp', 'seq')), may hold values from -640 to 640
Outputs:
- grad_queries: float32 [524288, 128], P(('grp', 'seq'))
- grad_keys: float32 [524288, 128], P(('grp', 'seq'))
- grad_values: float32 [524288, 128], P(('grp', 'seq'))
The draws below stay inside these ranges and needn't reach their ends.
All inputs are finite; a program needn't handle non-finite values.
Results may differ from the reference program's by a relative error of at most 0.0057.
Values may be sent and summed in bfloat16 or wider, within the bound.
No kernel may reach another device: no remote copies, remote signals or barrier semaphores. Data moves between devices by JAX's collectives and lax.ppermute only.
A program may use at most 128 MiB of HBM per device.

```python
import jax
import jax.numpy as jnp
from jax import lax

HEAD = 128
SEG = 2048
LEVELS = 5
TOKENS = 524288


def paired_rows(key, shift):
    directions = jax.random.uniform(jax.random.fold_in(key, 601), (SEG, HEAD), minval=-1.0, maxval=1.0)
    gap = TOKENS // SEG
    position = jnp.arange(TOKENS)
    chosen = (position % gap == 0)[:, None]
    index_rows = (position // gap + shift) % SEG
    return (chosen, 1.2 * directions[index_rows])


def draw_queries(key, part):
    chosen, added = paired_rows(key, 0)
    drawn_key = jax.random.fold_in(key, 11)
    field_rows = jax.random.truncated_normal(drawn_key, -4.5, 4.5, (TOKENS, HEAD))
    field_rows = jnp.where(chosen, field_rows + added, field_rows)
    return jnp.clip(field_rows, -6.0, 6.0).astype(jnp.bfloat16)


def draw_keys(key, part):
    chosen, added = paired_rows(key, SEG - SEG // 2)
    drawn_key = jax.random.fold_in(key, 12)
    field_rows = jax.random.truncated_normal(drawn_key, -4.5, 4.5, (TOKENS, HEAD))
    field_rows = jnp.where(chosen, field_rows + added, field_rows)
    return jnp.clip(field_rows, -6.0, 6.0).astype(jnp.bfloat16)


def steps_of(own_key, extent, pieces, smallest, top_value):
    gain, own = 1.0, jax.random.fold_in(own_key, 6)
    for axis_at, parts in pieces:
        heights = jnp.exp(jax.random.uniform(jax.random.fold_in(own, axis_at), (parts,), jnp.float32, smallest / len(pieces), top_value / len(pieces)))
        gain = gain * jnp.repeat(heights, extent[axis_at] // parts).reshape([-1 if axis == axis_at else 1 for axis in range(len(extent))])
    return gain


def scatter_about(rng, dims, deviation, limit, split=(), dtype=jnp.bfloat16):
    drawn = jax.random.normal(rng, dims, jnp.float32) * deviation
    if len(split) > 0:
        drawn = steps_of(rng, dims, split, -0.22, 0.18) * drawn
    return jnp.clip(drawn, min=-limit, max=limit).astype(dtype)


def setup_inputs(seed: int = 0) -> dict:
    arg_keys = jax.random.split(jax.random.key(seed), 5)
    queries = draw_queries(jax.random.fold_in(arg_keys[4], 71), 0)
    keys = draw_keys(jax.random.fold_in(arg_keys[4], 71), 0)
    values = scatter_about(arg_keys[2], (TOKENS, HEAD), 1.0, 6.0, ((0, 256),))
    cotangent = scatter_about(arg_keys[3], (TOKENS, HEAD), ((LEVELS * SEG) ** 0.5), 640.0, ((0, 256),))
    return dict(queries=queries, keys=keys, values=values, cotangent=cotangent)


NEG_FILL = -1.0e30


def level_rows(field_rows, stride):
    row_count = field_rows.shape[0] // stride
    return field_rows.reshape((row_count, stride) + field_rows.shape[1:])[:, 0]


def spread_rows(part_rows, stride, fill_value):
    row_count = part_rows.shape[0]
    widths = ((0, 0), (0, stride - 1)) + ((0, 0),) * (part_rows.ndim - 1)
    widened = jnp.pad(part_rows[:, None], widths, constant_values=fill_value)
    return widened.reshape((row_count * stride,) + part_rows.shape[1:])


def reference(queries, keys, values, cotangent):
    total_rows, head_dim = queries.shape
    score_scale = head_dim ** -0.5
    strides = [2 ** level_idx for level_idx in range(LEVELS - 1)] + [total_rows // SEG]

    def segments(field_rows, stride):
        picked = level_rows(field_rows, stride)
        return picked.reshape((picked.shape[0] // SEG, SEG) + picked.shape[1:])

    def forward_segment(members):
        query_seg, key_seg, value_seg = members
        scores = score_scale * jnp.dot(query_seg, key_seg.T, preferred_element_type=jnp.float32)
        row_peak = jnp.max(scores, axis=1, keepdims=True)
        log_norm = row_peak[:, 0] + jnp.log(jnp.sum(jnp.exp(scores - row_peak), axis=1))
        prob_low = jnp.exp(scores - log_norm[:, None]).astype(jnp.bfloat16)
        return log_norm, jnp.dot(prob_low, value_seg, preferred_element_type=jnp.float32)

    def backward_segment(members):
        query_seg, key_seg, value_seg, grad_seg, total_seg, delta_seg = members
        scores = score_scale * jnp.dot(query_seg, key_seg.T, preferred_element_type=jnp.float32)
        weights = jnp.exp(scores - total_seg[:, None])
        grad_probs = jnp.dot(grad_seg, value_seg.T, preferred_element_type=jnp.float32)
        grad_scores = (weights * (grad_probs - delta_seg[:, None])).astype(jnp.bfloat16)
        grad_query = score_scale * jnp.dot(grad_scores, key_seg, preferred_element_type=jnp.float32)
        grad_key = score_scale * jnp.dot(grad_scores.T, query_seg, preferred_element_type=jnp.float32)
        grad_value = jnp.dot(weights.astype(jnp.bfloat16).T, grad_seg, preferred_element_type=jnp.float32)
        return grad_query, grad_key, grad_value

    log_norms = []
    level_outs = []
    for stride in strides:
        log_norm, level_out = lax.map(forward_segment, (segments(queries, stride), segments(keys, stride), segments(values, stride)))
        log_norms.append(log_norm.reshape(-1))
        level_outs.append(level_out.reshape(-1, head_dim))

    spread_norms = [spread_rows(log_norms[level_idx], strides[level_idx], NEG_FILL) for level_idx in range(LEVELS)]
    top_norm = spread_norms[0]
    for norm_field in spread_norms[1:]:
        top_norm = jnp.maximum(top_norm, norm_field)
    norm_sum = jnp.zeros((total_rows,), jnp.float32)
    for norm_field in spread_norms:
        norm_sum = norm_sum + jnp.exp(norm_field - top_norm)
    log_total = top_norm + jnp.log(norm_sum)

    combined = jnp.zeros((total_rows, head_dim), jnp.float32)
    for level_idx in range(LEVELS):
        stride = strides[level_idx]
        level_share = jnp.exp(log_norms[level_idx] - level_rows(log_total, stride))
        combined = combined + spread_rows(level_share[:, None] * level_outs[level_idx], stride, 0.0)
    row_delta = jnp.sum(cotangent.astype(jnp.float32) * combined, axis=1)

    grad_queries = jnp.zeros((total_rows, head_dim), jnp.float32)
    grad_keys = jnp.zeros((total_rows, head_dim), jnp.float32)
    grad_values = jnp.zeros((total_rows, head_dim), jnp.float32)
    for stride in strides:
        members = (segments(queries, stride), segments(keys, stride), segments(values, stride),
                   segments(cotangent, stride), segments(log_total, stride), segments(row_delta, stride))
        grad_query, grad_key, grad_value = lax.map(backward_segment, members)
        grad_queries = grad_queries + spread_rows(grad_query.reshape(-1, head_dim), stride, 0.0)
        grad_keys = grad_keys + spread_rows(grad_key.reshape(-1, head_dim), stride, 0.0)
        grad_values = grad_values + spread_rows(grad_value.reshape(-1, head_dim), stride, 0.0)
    return grad_queries, grad_keys, grad_values
```

```python
import functools
import math

import jax
import jax.numpy as jnp
import numpy as np
from jax import lax
from jax.experimental import pallas as pl
from jax.experimental.pallas import tpu as pltpu
from jax.sharding import PartitionSpec as P

ROWS = 2048
HEAD = 128
UNIT = 256
ORDER = (0, 4, 2, 6, 1, 3, 5, 7)
SCALE = HEAD**-0.5
SCALE2 = SCALE * math.log2(math.e)
NEG = -1e30
REMOTE = 5120
SETS = ((0, 1024, 1024), (1024, 1024, 512), (2048, 1024, 256), (3072, 2048, 256))
VMEM = 56 * 1024 * 1024


def unit_level(unit):
    return 3 if unit == 0 else 2 if unit == 1 else 1 if unit < 4 else 0


def own_bias():
    table = np.zeros((8, ROWS), np.float32)
    for key_unit in range(8):
        for query_unit in range(8):
            shared = 1 + min(unit_level(key_unit), unit_level(query_unit))
            table[key_unit, query_unit * UNIT : (query_unit + 1) * UNIT] = math.log2(shared)
    return table


def remote_bias():
    table = np.full((20, 1024), NEG, np.float32)
    for query_unit in range(4):
        lanes = slice(query_unit * UNIT, (query_unit + 1) * UNIT)
        level = unit_level(query_unit)
        for unit in range(4):
            table[unit, lanes] = math.log2(min(unit_level(unit), level))
        for unit in range(4):
            shared = min(unit_level(unit % 2), level) - 1
            if shared > 0:
                table[4 + unit, lanes] = math.log2(shared)
        if level == 3:
            table[8:12, lanes] = 0.0
    table[12:20, :8] = 0.0
    return np.concatenate([table, np.full((4, 1024), NEG, np.float32)], 0)


def dot_nt(left, right):
    return lax.dot_general(left, right, (((1,), (1,)), ((), ())), preferred_element_type=jnp.float32)


def dot_nn(left, right):
    return lax.dot_general(left, right, (((1,), (0,)), ((), ())), preferred_element_type=jnp.float32)


def dot_tn(left, right):
    return lax.dot_general(left, right, (((0,), (0,)), ((), ())), preferred_element_type=jnp.float32)


def call(kernel, outs, args, scratch=(), flops=0, nbytes=0, exps=0, any_inputs=()):
    specs = [
        pl.BlockSpec(memory_space=pl.ANY if at in any_inputs else pltpu.VMEM)
        for at in range(len(args))
    ]
    return pl.pallas_call(
        kernel,
        out_shape=[jax.ShapeDtypeStruct(shape, dtype) for shape, dtype in outs],
        in_specs=specs,
        out_specs=[pl.BlockSpec(memory_space=pltpu.VMEM)] * len(outs),
        scratch_shapes=list(scratch),
        compiler_params=pltpu.CompilerParams(vmem_limit_bytes=VMEM),
        cost_estimate=pl.CostEstimate(flops=flops, bytes_accessed=nbytes, transcendentals=exps),
    )(*args)


def prepare_kernel(q_ref, k_ref, v_ref, g_ref, qp_ref, kv_ref, gp_ref, s1_ref, s2_ref, s3_ref, s4_ref, wide):
    def sort_rows(source, target, lane):
        wide[...] = source[...].astype(jnp.float32)
        for unit, residue in enumerate(ORDER):
            for pair in range(16):
                parts = [
                    wide[pl.ds(8 * (2 * pair + half) + residue, 8, stride=256), :]
                    for half in range(2)
                ]
                rows = slice(unit * UNIT + 16 * pair, unit * UNIT + 16 * pair + 16)
                target[rows, lane : lane + HEAD] = jnp.concatenate(parts, 0).astype(jnp.bfloat16)

    sort_rows(k_ref, kv_ref, 0)
    sort_rows(v_ref, kv_ref, HEAD)
    sort_rows(q_ref, qp_ref, 0)
    sort_rows(g_ref, gp_ref, 0)
    s1_ref[...] = kv_ref[:1024]
    s2_ref[...] = kv_ref[:512]
    s3_ref[...] = kv_ref[:256]
    s4_ref[...] = kv_ref[:16]


def forward_block(q_block, kv_ref, first, units, bias_ref, bias_row, lanes, score_ref):
    count = q_block.shape[0]

    def scores(unit, peak):
        rows = pl.multiple_of(first + unit * UNIT, UNIT)
        block = dot_nt(kv_ref[pl.ds(rows, UNIT), :HEAD], q_block) * SCALE2
        block = block + bias_ref[pl.ds(bias_row + unit, 1), lanes]
        score_ref[pl.ds(pl.multiple_of(unit * UNIT, UNIT), UNIT), :count] = block
        return jnp.maximum(peak, jnp.max(block, axis=0, keepdims=True))

    peak = lax.fori_loop(0, units, scores, jnp.full((1, count), NEG, jnp.float32))

    def values(unit, state):
        total, out = state
        rows = pl.multiple_of(first + unit * UNIT, UNIT)
        block = score_ref[pl.ds(pl.multiple_of(unit * UNIT, UNIT), UNIT), :count]
        prob = jnp.exp2(block - peak)
        total = total + jnp.sum(prob, axis=0, keepdims=True)
        out = out + dot_tn(kv_ref[pl.ds(rows, UNIT), HEAD:], prob.astype(jnp.bfloat16))
        return total, out

    zero = (jnp.zeros((1, count), jnp.float32), jnp.zeros((HEAD, count), jnp.float32))
    total, out = lax.fori_loop(0, units, values, zero)
    return peak, total, out


def own_forward_kernel(q_ref, kv_ref, bias_ref, stat_ref, out_ref, score_ref):
    stat_ref[...] = jnp.zeros_like(stat_ref)

    def block(at, carry):
        start = pl.multiple_of(at * UNIT, UNIT)
        lanes = pl.ds(start, UNIT)
        peak, total, out = forward_block(
            q_ref[pl.ds(start, UNIT), :], kv_ref, 0, 8, bias_ref, 0, lanes, score_ref
        )
        stat_ref[0:1, lanes] = peak
        stat_ref[1:2, lanes] = total
        out_ref[:, lanes] = out
        return carry

    lax.fori_loop(0, ROWS // UNIT, block, 0)


def gather_rows(refs, held, sem):
    copies = []
    at = 0
    for index, ref in enumerate(refs):
        rows = ref.shape[0]
        copies.append(pltpu.make_async_copy(ref, held.at[pl.ds(at, rows)], sem.at[index]))
        at += rows
    for copy in copies:
        copy.start()
    for copy in copies:
        copy.wait()


def remote_forward_kernel(q_ref, g_ref, bias_ref, stat_ref, out_ref, *rest):
    kv_refs, (row_ref, held, score_ref, sem) = rest[:8], rest[8:]
    gather_rows(kv_refs, held, sem)
    row_ref[...] = jnp.zeros_like(row_ref)
    for start, count, units in ((0, 256, 20), (256, 256, 8), (512, 256, 4), (768, 256, 4), (1024, 1024, 0)):
        lanes = slice(start, start + count)
        peak = stat_ref[0:1, lanes]
        total = stat_ref[1:2, lanes]
        out = out_ref[:, lanes]
        if units:
            far_peak, far_total, far_out = forward_block(
                q_ref[lanes, :], held, 0, units, bias_ref, 0, lanes, score_ref
            )
            top = jnp.maximum(peak, far_peak)
            near, far = jnp.exp2(peak - top), jnp.exp2(far_peak - top)
            total = near * total + far * far_total
            out = near * out + far * far_out
            peak = top
        row_ref[0:1, lanes] = peak + jnp.log2(total)
        grad = g_ref[lanes, :].astype(jnp.float32).T
        row_ref[1:2, lanes] = jnp.sum(grad * out, axis=0, keepdims=True) / total


def backward_unit(kv_unit, q_ref, g_ref, row_ref, bias_ref, bias_row, count, step, dq_ref):
    key, value = kv_unit[:, :HEAD], kv_unit[:, HEAD:]
    grad_key = jnp.zeros((UNIT, HEAD), jnp.float32)
    grad_value = jnp.zeros((UNIT, HEAD), jnp.float32)
    for start in range(0, count, step):
        lanes = slice(start, start + step)
        query, grad = q_ref[lanes, :], g_ref[lanes, :]
        offset = bias_ref[pl.ds(bias_row, 1), lanes] - row_ref[0:1, lanes]
        weights = jnp.exp2(dot_nt(key, query) * SCALE2 + offset)
        grad_probs = dot_nt(value, grad)
        grad_scores = (weights * (grad_probs - row_ref[1:2, lanes])).astype(jnp.bfloat16)
        grad_value = grad_value + dot_nn(weights.astype(jnp.bfloat16), grad)
        grad_key = grad_key + dot_nn(grad_scores, query)
        dq_ref[:, lanes] += dot_tn(key, grad_scores)
    return jnp.concatenate([SCALE * grad_key, grad_value], 1)


def remote_backward_kernel(q_ref, g_ref, bias_ref, row_ref, *rest):
    kv_refs, rest = rest[:8], rest[8:]
    out_refs, dq_ref = rest[:8], rest[8]
    dq_ref[...] = jnp.zeros_like(dq_ref)
    bias_row = 0
    for kv_ref, out_ref, count in zip(kv_refs, out_refs, (1024, 512, 512, 256, 256, 256, 256, 256)):
        units = kv_ref.shape[0] // UNIT

        def one(unit, carry, kv_ref=kv_ref, out_ref=out_ref, count=count, bias_row=bias_row):
            rows = pl.ds(pl.multiple_of(unit * UNIT, UNIT), UNIT)
            both = backward_unit(
                kv_ref[rows, :], q_ref, g_ref, row_ref, bias_ref, bias_row + unit, count, min(count, 512), dq_ref
            )
            out_ref[rows, :] = both.astype(jnp.bfloat16)
            return carry

        lax.fori_loop(0, units, one, 0)
        bias_row += units


def own_backward_kernel(q_ref, g_ref, bias_ref, row_ref, kv_ref, far_ref, dq_ref, dkv_ref, acc_ref, tall_ref):
    acc_ref[:, :1024] = far_ref[...]
    acc_ref[:, 1024:] = jnp.zeros((HEAD, 1024), jnp.float32)

    def one(unit, carry):
        rows = pl.ds(pl.multiple_of(unit * UNIT, UNIT), UNIT)
        dkv_ref[rows, :] = backward_unit(
            kv_ref[rows, :], q_ref, g_ref, row_ref, bias_ref, unit, ROWS, 512, acc_ref
        )
        return carry

    lax.fori_loop(0, ROWS // UNIT, one, 0)
    for unit in range(8):
        lanes = slice(unit * UNIT, (unit + 1) * UNIT)
        tall_ref[lanes, :] = acc_ref[:, lanes].T * SCALE
    restore_rows(lambda rows: tall_ref[rows, :], dq_ref)


def restore_rows(read, target):
    for unit, residue in enumerate(ORDER):
        for block in range(32):
            start = unit * UNIT + 8 * block
            target[pl.ds(8 * block + residue, 8, stride=256), :] = read(slice(start, start + 8))


def join_kernel(dkv_ref, *rest):
    far_refs, (dk_ref, dv_ref, sum_ref) = rest[:8], rest[8:]
    sum_ref[...] = dkv_ref[...]
    for ref in far_refs[:7]:
        rows = ref.shape[0]
        sum_ref[:rows, :] += ref[...].astype(jnp.float32)
    whole = far_refs[7]

    def add(at, total):
        piece = whole[pl.ds(pl.multiple_of(at * 16, 16), 16), :].astype(jnp.float32)
        return total + piece[:8] + piece[8:]

    total = lax.fori_loop(0, 128, add, jnp.zeros((8, 2 * HEAD), jnp.float32))
    sum_ref[:8, :] += total
    restore_rows(lambda rows: sum_ref[rows, :HEAD], dk_ref)
    restore_rows(lambda rows: sum_ref[rows, HEAD:], dv_ref)


def swap(block, mask):
    return lax.ppermute(block, "seq", [(at, at ^ mask) for at in range(lax.axis_size("seq"))])


def on_device(queries, keys, values, cotangent):
    f32, bf16 = jnp.float32, jnp.bfloat16
    near_bias = jnp.asarray(own_bias())
    far_bias = jnp.asarray(remote_bias())
    q, kv, g, s1, s2, s3, s4 = call(
        prepare_kernel,
        [((ROWS, HEAD), bf16), ((ROWS, 256), bf16), ((ROWS, HEAD), bf16)]
        + [((rows, 256), bf16) for rows in (1024, 512, 256, 16)],
        (queries, keys, values, cotangent),
        [pltpu.VMEM((ROWS, HEAD), f32)],
        nbytes=5 << 20,
    )
    far = [swap(s1, 1)] + [swap(s2, mask) for mask in (2, 3)] + [swap(s3, mask) for mask in (4, 5, 6, 7)]
    spread = jnp.broadcast_to(s4[None, :8], (256, 8, 256))
    whole = lax.all_to_all(spread, ("grp", "seq"), 0, 0)
    far.append(whole.reshape(2048, 256))
    stat, out = call(
        own_forward_kernel,
        [((8, ROWS), f32), ((HEAD, ROWS), f32)],
        (q, kv, near_bias),
        [pltpu.VMEM((ROWS, UNIT), f32)],
        flops=4 * HEAD * ROWS * ROWS,
        nbytes=3 << 20,
        exps=ROWS * ROWS,
    )
    (row,) = call(
        remote_forward_kernel,
        [((8, ROWS), f32)],
        (q, g, far_bias, stat, out, *far),
        [pltpu.VMEM((REMOTE, 256), bf16), pltpu.VMEM((REMOTE, UNIT), f32), pltpu.SemaphoreType.DMA((8,))],
        flops=2 * HEAD * ROWS * ROWS,
        nbytes=6 << 20,
        exps=ROWS * ROWS // 2,
        any_inputs=range(5, 13),
    )
    *sends, far_dq = call(
        remote_backward_kernel,
        [((block.shape[0], 256), bf16) for block in far] + [((HEAD, 1024), f32)],
        (q, g, far_bias, row, *far),
        flops=5 * HEAD * ROWS * ROWS,
        nbytes=8 << 20,
        exps=ROWS * ROWS // 2,
    )
    back = [swap(block, mask) for block, mask in zip(sends[:7], (1, 2, 3, 4, 5, 6, 7))]
    back.append(lax.all_to_all(sends[7].reshape(256, 8, 256), ("grp", "seq"), 0, 0).reshape(2048, 256))
    dq, dkv = call(
        own_backward_kernel,
        [((ROWS, HEAD), f32), ((ROWS, 256), f32)],
        (q, g, near_bias, row, kv, far_dq),
        [pltpu.VMEM((HEAD, ROWS), f32), pltpu.VMEM((ROWS, HEAD), f32)],
        flops=10 * HEAD * ROWS * ROWS,
        nbytes=8 << 20,
        exps=ROWS * ROWS,
    )
    dk, dv = call(
        join_kernel,
        [((ROWS, HEAD), f32)] * 2,
        (dkv, *back),
        [pltpu.VMEM((ROWS, 256), f32)],
        nbytes=8 << 20,
    )
    return dq, dk, dv


def solution(mesh):
    spec = P(("grp", "seq"), None)
    return jax.shard_map(
        on_device, mesh=mesh, in_specs=(spec,) * 4, out_specs=(spec,) * 3, check_vma=False
    )
```

```python
import functools
import math

import jax
import jax.numpy as jnp
import numpy as np
from jax import lax
from jax.experimental import pallas as pl
from jax.experimental.pallas import tpu as pltpu
from jax.sharding import PartitionSpec as P

ROWS = 2048
HEAD = 128
UNIT = 256
ORDER = (0, 4, 2, 6, 1, 3, 5, 7)
SCALE = HEAD**-0.5
SCALE2 = SCALE * math.log2(math.e)
NEG = -1e30
REMOTE = 5120
BLOCK = 512
VMEM = 58 * 1024 * 1024


def unit_level(unit):
    return 3 if unit == 0 else 2 if unit == 1 else 1 if unit < 4 else 0


def own_bias():
    table = np.zeros((8, ROWS), np.float32)
    for key_unit in range(8):
        for query_unit in range(8):
            shared = 1 + min(unit_level(key_unit), unit_level(query_unit))
            table[key_unit, query_unit * UNIT : (query_unit + 1) * UNIT] = math.log2(shared)
    return table


def far_bias():
    table = np.zeros((8, 1024), np.float32)
    for query_unit in range(4):
        lanes = slice(query_unit * UNIT, (query_unit + 1) * UNIT)
        level = unit_level(query_unit)
        table[0, lanes] = math.log2(min(3, level))
        table[1, lanes] = math.log2(min(2, level))
        if level >= 2:
            table[2, lanes] = math.log2(level - 1)
    table[3, 8:] = NEG
    return table


def dot_nt(left, right):
    return lax.dot_general(left, right, (((1,), (1,)), ((), ())), preferred_element_type=jnp.float32)


def dot_nn(left, right):
    return lax.dot_general(left, right, (((1,), (0,)), ((), ())), preferred_element_type=jnp.float32)


def dot_tn(left, right):
    return lax.dot_general(left, right, (((0,), (0,)), ((), ())), preferred_element_type=jnp.float32)


def call(kernel, outs, args, scratch=(), flops=0, nbytes=0, exps=0, any_inputs=(), smem_inputs=()):
    specs = [
        pl.BlockSpec(memory_space=pl.ANY if at in any_inputs else pltpu.SMEM if at in smem_inputs else pltpu.VMEM)
        for at in range(len(args))
    ]
    return pl.pallas_call(
        kernel,
        out_shape=[jax.ShapeDtypeStruct(shape, dtype) for shape, dtype in outs],
        in_specs=specs,
        out_specs=[pl.BlockSpec(memory_space=pltpu.VMEM)] * len(outs),
        scratch_shapes=list(scratch),
        compiler_params=pltpu.CompilerParams(vmem_limit_bytes=VMEM),
        cost_estimate=pl.CostEstimate(flops=flops, bytes_accessed=nbytes, transcendentals=exps),
    )(*args)


def prepare_kernel(q_ref, k_ref, v_ref, g_ref, qp_ref, kv_ref, gp_ref, s1_ref, s4_ref, s8_ref, whole_ref, wide):
    def sort_rows(source, target, lane):
        wide[...] = source[...].astype(jnp.float32)
        for unit, residue in enumerate(ORDER):
            for pair in range(16):
                parts = [
                    wide[pl.ds(8 * (2 * pair + half) + residue, 8, stride=256), :]
                    for half in range(2)
                ]
                rows = slice(unit * UNIT + 16 * pair, unit * UNIT + 16 * pair + 16)
                target[rows, lane : lane + HEAD] = jnp.concatenate(parts, 0).astype(jnp.bfloat16)

    sort_rows(k_ref, kv_ref, 0)
    sort_rows(v_ref, kv_ref, HEAD)
    first = kv_ref[:16].astype(jnp.float32)[:8]
    pair = jnp.concatenate([first, first], 0).astype(jnp.bfloat16)
    for at in range(128):
        whole_ref[16 * at : 16 * at + 16] = pair
    for at in range(8):
        s8_ref[at] = kv_ref[:256]
    for at in range(4):
        s4_ref[at] = kv_ref[256:512]
    s1_ref[...] = kv_ref[512:1024]
    sort_rows(q_ref, qp_ref, 0)
    sort_rows(g_ref, gp_ref, 0)


def add_bias(block, rows):
    if all(row is None for row in rows):
        return block
    parts = []
    for at, row in enumerate(rows):
        part = block[at * UNIT : (at + 1) * UNIT]
        parts.append(part if row is None else part + row)
    return jnp.concatenate(parts, 0)


def attend(query, keys, values, biases):
    scores = [add_bias(dot_nt(key, query) * SCALE2, bias) for key, bias in zip(keys, biases)]
    peak = functools.reduce(jnp.maximum, [jnp.max(block, 0, keepdims=True) for block in scores])
    probs = [jnp.exp2(block - peak) for block in scores]
    total = sum([jnp.sum(block, 0, keepdims=True) for block in probs])
    out = sum([value(block.astype(jnp.bfloat16)) for value, block in zip(values, probs)])
    return peak, total, out


def own_forward_kernel(q_ref, kv_ref, bias_ref, stat_ref, out_ref, vt_ref):
    stat_ref[...] = jnp.zeros_like(stat_ref)
    for unit in range(8):
        rows = slice(unit * UNIT, (unit + 1) * UNIT)
        vt_ref[:, rows] = kv_ref[rows, HEAD:].astype(jnp.float32).T.astype(jnp.bfloat16)
    for start in (0, 1024):
        lanes = slice(start, start + 1024)
        keys, values, biases = [], [], []
        for at in range(0, ROWS, BLOCK):
            rows = slice(at, at + BLOCK)
            keys.append(kv_ref[rows, :HEAD])
            values.append(lambda prob, rows=rows: dot_nn(vt_ref[:, rows], prob))
            unit = at // UNIT
            counted = start == 0 and at < 1024
            biases.append([bias_ref[unit + half : unit + half + 1, lanes] if counted else None for half in (0, 1)])
        peak, total, out = attend(q_ref[lanes, :], keys, values, biases)
        stat_ref[0:1, lanes] = peak
        stat_ref[1:2, lanes] = total
        out_ref[:, lanes] = out


def gather_far(me_ref, s1, s4, s8, whole, held, sem):
    at8, at4 = me_ref[0] % 8, me_ref[0] % 4
    copies = []

    def bring(source, row):
        copies.append(pltpu.make_async_copy(source, held.at[pl.ds(row, source.shape[0])], sem.at[len(copies)]))

    bring(s8.at[at8 ^ 1], 0)
    bring(s4.at[at4 ^ 1], 256)
    bring(s1, 512)
    for peer in (2, 3):
        bring(s8.at[at8 ^ peer], 1024 + 512 * (peer - 2))
        bring(s4.at[at4 ^ peer], 1280 + 512 * (peer - 2))
    for peer in (4, 5, 6, 7):
        bring(s8.at[at8 ^ peer], 1024 + 256 * peer)
    bring(whole, 3072)
    for copy in copies:
        copy.start()
    for copy in copies:
        copy.wait()


SETS = (
    (0, 1024, 1024, ((0, 1), (None, None))),
    (1024, 1024, 512, ((2, None), (2, None))),
    (2048, 1024, 256, ((None, None), (None, None))),
    (3072, 2048, 128, ((3, 3),) * 4),
)


def bias_rows(bias_ref, picks, lanes):
    return [None if pick is None else bias_ref[pick : pick + 1, lanes] for pick in picks]


def remote_forward_kernel(me_ref, q_ref, g_ref, bias_ref, stat_ref, out_ref, s1, s4, s8, whole, row_ref, held, sums, acc, sem):
    gather_far(me_ref, s1, s4, s8, whole, held, sem)
    row_ref[...] = jnp.zeros_like(row_ref)
    sums[...] = stat_ref[...]
    acc[...] = out_ref[...]
    for first, keys, count, picks in SETS:
        lanes = slice(0, count)
        blocks = [slice(first + at, first + at + BLOCK) for at in range(0, keys, BLOCK)]
        far_peak, far_total, far_out = attend(
            q_ref[lanes, :],
            [held[rows, :HEAD] for rows in blocks],
            [lambda prob, rows=rows: dot_tn(held[rows, HEAD:], prob) for rows in blocks],
            [bias_rows(bias_ref, pick, lanes) for pick in picks],
        )
        peak = sums[0:1, lanes]
        top = jnp.maximum(peak, far_peak)
        near, far = jnp.exp2(peak - top), jnp.exp2(far_peak - top)
        sums[0:1, lanes] = top
        sums[1:2, lanes] = near * sums[1:2, lanes] + far * far_total
        acc[:, lanes] = near * acc[:, lanes] + far * far_out
    for unit in range(8):
        lanes = slice(unit * UNIT, (unit + 1) * UNIT)
        total = sums[1:2, lanes]
        row_ref[0:1, lanes] = sums[0:1, lanes] + jnp.log2(total)
        grad = g_ref[lanes, :].astype(jnp.float32).T
        row_ref[1:2, lanes] = jnp.sum(grad * acc[:, lanes], axis=0, keepdims=True) / total


def backward_block(kv_block, q_ref, g_ref, row_ref, bias, count, dq_ref):
    key, value = kv_block[:, :HEAD], kv_block[:, HEAD:]
    lanes = slice(0, count)
    query, grad = q_ref[lanes, :], g_ref[lanes, :]
    scores = add_bias(dot_nt(key, query) * SCALE2, bias)
    weights = jnp.exp2(scores - row_ref[0:1, lanes])
    grad_probs = dot_nt(value, grad)
    grad_scores = (weights * (grad_probs - row_ref[1:2, lanes])).astype(jnp.bfloat16)
    grad_value = dot_nn(weights.astype(jnp.bfloat16), grad)
    grad_key = dot_nn(grad_scores, query)
    dq_ref[:, lanes] += dot_tn(key, grad_scores)
    return SCALE * grad_key, grad_value


def remote_backward_kernel(me_ref, q_ref, g_ref, bias_ref, row_ref, s1, s4, s8, whole, o1, o4, o8, owhole, dq_ref, held, sem):
    gather_far(me_ref, s1, s4, s8, whole, held, sem)
    at8, at4 = me_ref[0] % 8, me_ref[0] % 4
    dq_ref[...] = jnp.zeros_like(dq_ref)
    o8[at8] = jnp.zeros((UNIT, 256), jnp.bfloat16)
    o4[at4] = jnp.zeros((UNIT, 256), jnp.bfloat16)

    def block(first, picks, count):
        bias = bias_rows(bias_ref, picks, slice(0, count))
        rows = pl.ds(pl.multiple_of(first, BLOCK), BLOCK)
        both = backward_block(held[rows, :], q_ref, g_ref, row_ref, bias, count, dq_ref)
        return jnp.concatenate(both, 1).astype(jnp.bfloat16)

    def far(at, carry):
        owhole[pl.ds(pl.multiple_of(at * BLOCK, BLOCK), BLOCK), :] = block(3072 + at * BLOCK, (3, 3), 128)
        return carry

    lax.fori_loop(0, 4, far, 0)

    def third(at, carry):
        both = block(2048 + at * BLOCK, (None, None), 256)
        o8[at8 ^ (4 + 2 * at)] = both[:UNIT]
        o8[at8 ^ (5 + 2 * at)] = both[UNIT:]
        return carry

    lax.fori_loop(0, 2, third, 0)

    def second(at, carry):
        both = block(1024 + at * BLOCK, (2, None), 512)
        o8[at8 ^ (2 + at)] = both[:UNIT]
        o4[at4 ^ (2 + at)] = both[UNIT:]
        return carry

    lax.fori_loop(0, 2, second, 0)
    both = block(0, (0, 1), 1024)
    o8[at8 ^ 1] = both[:UNIT]
    o4[at4 ^ 1] = both[UNIT:]
    o1[...] = block(512, (None, None), 1024)


def own_backward_kernel(q_ref, g_ref, bias_ref, row_ref, kv_ref, far_ref, dq_ref, dkv_ref, acc_ref, tall_ref):
    acc_ref[:, :1024] = far_ref[...]
    acc_ref[:, 1024:] = jnp.zeros((HEAD, 1024), jnp.float32)

    def one(at, carry):
        rows = pl.ds(pl.multiple_of(at * BLOCK, BLOCK), BLOCK)
        bias = [bias_ref[pl.ds(2 * at + half, 1), :] for half in (0, 1)]
        grad_key, grad_value = backward_block(kv_ref[rows, :], q_ref, g_ref, row_ref, bias, ROWS, acc_ref)
        dkv_ref[rows, :HEAD] = grad_key
        dkv_ref[rows, HEAD:] = grad_value
        return carry

    lax.fori_loop(0, ROWS // BLOCK, one, 0)
    for unit in range(8):
        lanes = slice(unit * UNIT, (unit + 1) * UNIT)
        tall_ref[lanes, :] = acc_ref[:, lanes].T * SCALE
    restore_rows(lambda rows: tall_ref[rows, :], dq_ref)


def restore_rows(read, target):
    for unit, residue in enumerate(ORDER):
        for block in range(32):
            start = unit * UNIT + 8 * block
            target[pl.ds(8 * block + residue, 8, stride=256), :] = read(slice(start, start + 8))


def join_kernel(dkv_ref, s1, s4, s8, whole, dk_ref, dv_ref, sum_ref):
    first = dkv_ref[:256, :]
    for at in range(8):
        first = first + s8[at].astype(jnp.float32)
    sum_ref[:256, :] = first
    second = dkv_ref[256:512, :]
    for at in range(4):
        second = second + s4[at].astype(jnp.float32)
    sum_ref[256:512, :] = second
    sum_ref[512:1024, :] = dkv_ref[512:1024, :] + s1[...].astype(jnp.float32)
    sum_ref[1024:, :] = dkv_ref[1024:, :]

    def add(at, total):
        piece = whole[pl.ds(pl.multiple_of(at * 128, 128), 128), :].astype(jnp.float32)
        return total + jnp.sum(piece.reshape(16, 8, 256), 0)

    total = lax.fori_loop(0, 16, add, jnp.zeros((8, 256), jnp.float32))
    sum_ref[:8, :] += total
    restore_rows(lambda rows: sum_ref[rows, :HEAD], dk_ref)
    restore_rows(lambda rows: sum_ref[rows, HEAD:], dv_ref)


def exchange(s1, s4, s8, whole):
    count = lax.axis_size("seq")
    groups = [[list(range(low, low + size)) for low in range(0, count, size)] for size in (4, 8)]
    n1 = lax.ppermute(s1, "seq", [(at, at ^ 1) for at in range(count)])
    n4 = lax.all_to_all(s4, "seq", 0, 0, axis_index_groups=groups[0])
    n8 = lax.all_to_all(s8, "seq", 0, 0, axis_index_groups=groups[1])
    far = lax.all_to_all(whole.reshape(256, 8, 256), ("grp", "seq"), 0, 0).reshape(2048, 256)
    return n1, n4, n8, far


def on_device(queries, keys, values, cotangent):
    f32, bf16 = jnp.float32, jnp.bfloat16
    near_bias, other_bias = jnp.asarray(own_bias()), jnp.asarray(far_bias())
    me = lax.axis_index("seq").astype(jnp.int32).reshape(1)
    parts = [((512, 256), bf16), ((4, 256, 256), bf16), ((8, 256, 256), bf16), ((2048, 256), bf16)]
    q, kv, g, *sends = call(
        prepare_kernel,
        [((ROWS, HEAD), bf16), ((ROWS, 256), bf16), ((ROWS, HEAD), bf16)] + parts,
        (queries, keys, values, cotangent),
        [pltpu.VMEM((ROWS, HEAD), f32)],
        nbytes=5 << 20,
    )
    far = exchange(*sends)
    stat, out = call(
        own_forward_kernel,
        [((8, ROWS), f32), ((HEAD, ROWS), f32)],
        (q, kv, near_bias),
        [pltpu.VMEM((HEAD, ROWS), bf16)],
        flops=4 * HEAD * ROWS * ROWS,
        nbytes=3 << 20,
        exps=ROWS * ROWS,
    )
    (row,) = call(
        remote_forward_kernel,
        [((8, ROWS), f32)],
        (me, q, g, other_bias, stat, out, *far),
        [
            pltpu.VMEM((REMOTE, 256), bf16),
            pltpu.VMEM((8, ROWS), f32),
            pltpu.VMEM((HEAD, ROWS), f32),
            pltpu.SemaphoreType.DMA((12,)),
        ],
        flops=2 * HEAD * ROWS * ROWS,
        nbytes=6 << 20,
        exps=ROWS * ROWS // 2,
        any_inputs=range(6, 10),
        smem_inputs=(0,),
    )
    *sends, far_dq = call(
        remote_backward_kernel,
        parts + [((HEAD, 1024), f32)],
        (me, q, g, other_bias, row, *far),
        [pltpu.VMEM((REMOTE, 256), bf16), pltpu.SemaphoreType.DMA((12,))],
        flops=5 * HEAD * ROWS * ROWS,
        nbytes=8 << 20,
        exps=ROWS * ROWS // 2,
        any_inputs=range(5, 9),
        smem_inputs=(0,),
    )
    back = exchange(*sends)
    dq, dkv = call(
        own_backward_kernel,
        [((ROWS, HEAD), f32), ((ROWS, 256), f32)],
        (q, g, near_bias, row, kv, far_dq),
        [pltpu.VMEM((HEAD, ROWS), f32), pltpu.VMEM((ROWS, HEAD), f32)],
        flops=10 * HEAD * ROWS * ROWS,
        nbytes=8 << 20,
        exps=ROWS * ROWS,
    )
    dk, dv = call(
        join_kernel,
        [((ROWS, HEAD), f32)] * 2,
        (dkv, *back),
        [pltpu.VMEM((ROWS, 256), f32)],
        nbytes=8 << 20,
    )
    return dq, dk, dv


def solution(mesh):
    spec = P(("grp", "seq"), None)
    return jax.shard_map(
        on_device, mesh=mesh, in_specs=(spec,) * 4, out_specs=(spec,) * 3, check_vma=False
    )
```

```python
import functools
import math

import jax
import jax.numpy as jnp
import numpy as np
from jax import lax
from jax.experimental import pallas as pl
from jax.experimental.pallas import tpu as pltpu
from jax.sharding import PartitionSpec as P

ROWS = 2048
HEAD = 128
UNIT = 256
ORDER = (0, 4, 2, 6, 1, 3, 5, 7)
SCALE = HEAD**-0.5
SCALE2 = SCALE * math.log2(math.e)
NEG = -1e30
BLOCK = 512


def unit_level(unit):
    return 3 if unit == 0 else 2 if unit == 1 else 1 if unit < 4 else 0


def own_bias():
    table = np.zeros((8, ROWS), np.float32)
    for key_unit in range(8):
        for query_unit in range(8):
            shared = 1 + min(unit_level(key_unit), unit_level(query_unit))
            table[key_unit, query_unit * UNIT : (query_unit + 1) * UNIT] = math.log2(shared)
    return table


def far_bias():
    table = np.zeros((8, 1024), np.float32)
    for query_unit in range(4):
        lanes = slice(query_unit * UNIT, (query_unit + 1) * UNIT)
        level = unit_level(query_unit)
        table[0, lanes] = math.log2(min(3, level))
        table[1, lanes] = math.log2(min(2, level))
        if level >= 2:
            table[2, lanes] = math.log2(level - 1)
    table[3, 8:] = NEG
    return table


def dot_nt(left, right):
    return lax.dot_general(left, right, (((1,), (1,)), ((), ())), preferred_element_type=jnp.float32)


def dot_nn(left, right):
    return lax.dot_general(left, right, (((1,), (0,)), ((), ())), preferred_element_type=jnp.float32)


def dot_tn(left, right):
    return lax.dot_general(left, right, (((0,), (0,)), ((), ())), preferred_element_type=jnp.float32)


def call(kernel, outs, args, scratch=(), flops=0, nbytes=0, exps=0, vmem=24):
    specs = [pl.BlockSpec(memory_space=pltpu.VMEM)] * len(args)
    return pl.pallas_call(
        kernel,
        out_shape=[jax.ShapeDtypeStruct(shape, dtype) for shape, dtype in outs],
        in_specs=specs,
        out_specs=[pl.BlockSpec(memory_space=pltpu.VMEM)] * len(outs),
        scratch_shapes=list(scratch),
        compiler_params=pltpu.CompilerParams(vmem_limit_bytes=vmem << 20),
        cost_estimate=pl.CostEstimate(flops=flops, bytes_accessed=nbytes, transcendentals=exps),
    )(*args)


def sort_rows(source, target, lane, wide):
    wide[...] = source[...].astype(jnp.float32)
    for unit, residue in enumerate(ORDER):
        for pair in range(16):
            parts = [
                wide[pl.ds(8 * (2 * pair + half) + residue, 8, stride=256), :] for half in range(2)
            ]
            rows = slice(unit * UNIT + 16 * pair, unit * UNIT + 16 * pair + 16)
            target[rows, lane : lane + HEAD] = jnp.concatenate(parts, 0).astype(jnp.bfloat16)


def prepare_keys_kernel(k_ref, v_ref, kv_ref, s1_ref, s2_ref, wide):
    sort_rows(k_ref, kv_ref, 0, wide)
    sort_rows(v_ref, kv_ref, HEAD, wide)
    s1_ref[...] = kv_ref[:1024]
    s2_ref[...] = kv_ref[:512]


def prepare_queries_kernel(q_ref, g_ref, s2_ref, qp_ref, gp_ref, whole_ref, wide):
    first = s2_ref[:16].astype(jnp.float32)[:8]
    pair = jnp.concatenate([first, first], 0).astype(jnp.bfloat16)
    for at in range(128):
        whole_ref[16 * at : 16 * at + 16] = pair
    sort_rows(q_ref, qp_ref, 0, wide)
    sort_rows(g_ref, gp_ref, 0, wide)


def add_bias(block, rows):
    if all(row is None for row in rows):
        return block
    parts = []
    for at, row in enumerate(rows):
        part = block[at * UNIT : (at + 1) * UNIT]
        parts.append(part if row is None else part + row)
    return jnp.concatenate(parts, 0)


def attend(query, keys, values, biases):
    scores = [add_bias(dot_nt(key, query) * SCALE2, bias) for key, bias in zip(keys, biases)]
    peak = functools.reduce(jnp.maximum, [jnp.max(block, 0, keepdims=True) for block in scores])
    probs = [jnp.exp2(block - peak) for block in scores]
    total = sum([jnp.sum(block, 0, keepdims=True) for block in probs])
    out = sum([value(block.astype(jnp.bfloat16)) for value, block in zip(values, probs)])
    return peak, total, out


def own_forward_kernel(q_ref, kv_ref, bias_ref, stat_ref, out_ref, vt_ref):
    stat_ref[...] = jnp.zeros_like(stat_ref)
    for unit in range(8):
        rows = slice(unit * UNIT, (unit + 1) * UNIT)
        vt_ref[:, rows] = kv_ref[rows, HEAD:].astype(jnp.float32).T.astype(jnp.bfloat16)
    for start in (0, 1024):
        lanes = slice(start, start + 1024)
        keys, values, biases = [], [], []
        for at in range(0, ROWS, BLOCK):
            rows = slice(at, at + BLOCK)
            keys.append(kv_ref[rows, :HEAD])
            values.append(lambda prob, rows=rows: dot_nn(vt_ref[:, rows], prob))
            unit = at // UNIT
            counted = start == 0 and at < 1024
            biases.append([bias_ref[unit + half : unit + half + 1, lanes] if counted else None for half in (0, 1)])
        peak, total, out = attend(q_ref[lanes, :], keys, values, biases)
        stat_ref[0:1, lanes] = peak
        stat_ref[1:2, lanes] = total
        out_ref[:, lanes] = out


def bias_rows(bias_ref, picks, count):
    return [None if pick is None else bias_ref[pick : pick + 1, :count] for pick in picks]


PARTNER, PARTNER_REST, SECOND, THIRD, WHOLE = (0, 1), (None, None), (2, None), (None, None), (3, 3)


def attend_far(q_ref, bias_ref, blocks, count, sums, acc):
    lanes = slice(0, count)
    far_peak, far_total, far_out = attend(
        q_ref[lanes, :],
        [ref[first : first + BLOCK, :HEAD] for ref, first, _ in blocks],
        [
            lambda prob, ref=ref, first=first: dot_tn(ref[first : first + BLOCK, HEAD:], prob)
            for ref, first, _ in blocks
        ],
        [bias_rows(bias_ref, picks, count) for _, _, picks in blocks],
    )
    peak = sums[0:1, lanes]
    top = jnp.maximum(peak, far_peak)
    near, far = jnp.exp2(peak - top), jnp.exp2(far_peak - top)
    sums[0:1, lanes] = top
    sums[1:2, lanes] = near * sums[1:2, lanes] + far * far_total
    acc[:, lanes] = near * acc[:, lanes] + far * far_out


def middle_forward_kernel(q_ref, bias_ref, stat_ref, out_ref, r1, r2, r3, sums, acc):
    sums[...] = stat_ref[...]
    acc[...] = out_ref[...]
    attend_far(q_ref, bias_ref, [(r1, 0, PARTNER), (r1, BLOCK, PARTNER_REST)], 1024, sums, acc)
    attend_far(q_ref, bias_ref, [(r2, 0, SECOND), (r3, 0, SECOND)], 512, sums, acc)


def last_forward_kernel(q_ref, g_ref, bias_ref, stat_ref, out_ref, r4, r6, whole, row_ref, sums, acc):
    row_ref[...] = jnp.zeros_like(row_ref)
    sums[...] = stat_ref[:, :256]
    acc[...] = out_ref[:, :256]
    attend_far(q_ref, bias_ref, [(r4, 0, THIRD), (r6, 0, THIRD)], 256, sums, acc)
    attend_far(q_ref, bias_ref, [(whole, at, WHOLE) for at in range(0, ROWS, BLOCK)], 128, sums, acc)
    for unit in range(8):
        lanes = slice(unit * UNIT, (unit + 1) * UNIT)
        peak, total = (sums if unit == 0 else stat_ref)[0:1, lanes], (sums if unit == 0 else stat_ref)[1:2, lanes]
        out = (acc if unit == 0 else out_ref)[:, lanes]
        row_ref[0:1, lanes] = peak + jnp.log2(total)
        grad = g_ref[lanes, :].astype(jnp.float32).T
        row_ref[1:2, lanes] = jnp.sum(grad * out, axis=0, keepdims=True) / total


def backward_block(kv_block, q_ref, g_ref, row_ref, bias, count, dq_ref):
    key, value = kv_block[:, :HEAD], kv_block[:, HEAD:]
    lanes = slice(0, count)
    query, grad = q_ref[lanes, :], g_ref[lanes, :]
    scores = add_bias(dot_nt(key, query) * SCALE2, bias)
    weights = jnp.exp2(scores - row_ref[0:1, lanes])
    grad_probs = dot_nt(value, grad)
    grad_scores = (weights * (grad_probs - row_ref[1:2, lanes])).astype(jnp.bfloat16)
    grad_value = dot_nn(weights.astype(jnp.bfloat16), grad)
    grad_key = dot_nn(grad_scores, query)
    dq_ref[:, lanes] += dot_tn(key, grad_scores)
    return SCALE * grad_key, grad_value


def backward_far(refs, source, first, picks, count, dq_ref):
    q_ref, g_ref, bias_ref, row_ref = refs
    bias = bias_rows(bias_ref, picks, count)
    both = backward_block(source[first : first + BLOCK, :], q_ref, g_ref, row_ref, bias, count, dq_ref)
    return jnp.concatenate(both, 1)


def third_backward_kernel(q_ref, g_ref, bias_ref, row_ref, r4, r6, o4, o6, dq_ref):
    refs = (q_ref, g_ref, bias_ref, row_ref)
    dq_ref[...] = jnp.zeros_like(dq_ref)
    for source, target in ((r4, o4), (r6, o6)):
        target[...] = backward_far(refs, source, 0, THIRD, 256, dq_ref).astype(jnp.bfloat16)


def second_backward_kernel(q_ref, g_ref, bias_ref, row_ref, r2, r3, o2, o3, dq_ref):
    refs = (q_ref, g_ref, bias_ref, row_ref)
    dq_ref[...] = jnp.zeros_like(dq_ref)
    for source, target in ((r2, o2), (r3, o3)):
        target[...] = backward_far(refs, source, 0, SECOND, 512, dq_ref).astype(jnp.bfloat16)


def first_backward_kernel(q_ref, g_ref, bias_ref, row_ref, r1, o1, dq_ref):
    refs = (q_ref, g_ref, bias_ref, row_ref)
    dq_ref[...] = jnp.zeros_like(dq_ref)
    o1[:BLOCK, :] = backward_far(refs, r1, 0, PARTNER, 1024, dq_ref).astype(jnp.bfloat16)
    o1[BLOCK:, :] = backward_far(refs, r1, BLOCK, PARTNER_REST, 1024, dq_ref).astype(jnp.bfloat16)


def relay_kernel(o1, b4, b6, out_ref):
    first = [ref[rows, :].astype(jnp.float32) for ref, rows in ((o1, slice(0, 256)), (b4, slice(256, 512)), (b6, slice(256, 512)))]
    out_ref[:256, :] = sum(first).astype(jnp.bfloat16)
    out_ref[256:, :] = o1[256:, :]


def whole_backward_kernel(q_ref, g_ref, bias_ref, row_ref, whole, dq1, dq2, dq3, out_ref, dq_ref):
    refs = (q_ref, g_ref, bias_ref, row_ref)
    dq_ref[...] = dq1[...]
    dq_ref[:, :512] += dq2[...]
    dq_ref[:, :256] += dq3[...]
    for first in range(0, ROWS, BLOCK):
        both = backward_far(refs, whole, first, WHOLE, 128, dq_ref)
        out_ref[first : first + BLOCK, :] = both.astype(jnp.bfloat16)


def own_backward_kernel(q_ref, g_ref, bias_ref, row_ref, kv_ref, far_ref, dq_ref, dkv_ref, acc_ref, tall_ref):
    acc_ref[:, :1024] = far_ref[...]
    acc_ref[:, 1024:] = jnp.zeros((HEAD, 1024), jnp.float32)

    def one(at, carry):
        rows = pl.ds(pl.multiple_of(at * BLOCK, BLOCK), BLOCK)
        bias = [bias_ref[pl.ds(2 * at + half, 1), :] for half in (0, 1)]
        grad_key, grad_value = backward_block(kv_ref[rows, :], q_ref, g_ref, row_ref, bias, ROWS, acc_ref)
        dkv_ref[rows, :HEAD] = grad_key
        dkv_ref[rows, HEAD:] = grad_value
        return carry

    lax.fori_loop(0, ROWS // BLOCK, one, 0)
    for unit in range(8):
        lanes = slice(unit * UNIT, (unit + 1) * UNIT)
        tall_ref[lanes, :] = acc_ref[:, lanes].T * SCALE
    restore_rows(lambda rows: tall_ref[rows, :], dq_ref)


def restore_rows(read, target):
    for unit, residue in enumerate(ORDER):
        for block in range(32):
            start = unit * UNIT + 8 * block
            target[pl.ds(8 * block + residue, 8, stride=256), :] = read(slice(start, start + 8))


def join_kernel(dkv_ref, b1, b2, b3, b4, b6, whole, dk_ref, dv_ref, sum_ref):
    def wide(ref, rows):
        return ref[rows, :].astype(jnp.float32)

    top, mid, low = slice(0, 256), slice(256, 512), slice(512, 1024)
    near = wide(b1, top) + wide(b2, top) + wide(b3, top)
    sum_ref[top, :] = dkv_ref[top, :] + near + wide(b4, top) + wide(b6, top)
    sum_ref[mid, :] = dkv_ref[mid, :] + wide(b1, mid) + wide(b2, mid) + wide(b3, mid)
    sum_ref[low, :] = dkv_ref[low, :] + wide(b1, low)
    sum_ref[1024:, :] = dkv_ref[1024:, :]

    def add(at, total):
        piece = wide(whole, pl.ds(pl.multiple_of(at * 128, 128), 128))
        return total + jnp.sum(piece.reshape(16, 8, 256), 0)

    total = lax.fori_loop(0, 16, add, jnp.zeros((8, 256), jnp.float32))
    sum_ref[:8, :] += total
    restore_rows(lambda rows: sum_ref[rows, :HEAD], dk_ref)
    restore_rows(lambda rows: sum_ref[rows, HEAD:], dv_ref)


def swap(block, mask):
    return lax.ppermute(block, "seq", [(at, at ^ mask) for at in range(lax.axis_size("seq"))])


def swap_whole(block):
    return lax.all_to_all(block.reshape(256, 8, 256), ("grp", "seq"), 0, 0).reshape(ROWS, 256)


def on_device(queries, keys, values, cotangent):
    f32, bf16 = jnp.float32, jnp.bfloat16
    near_bias, other_bias = jnp.asarray(own_bias()), jnp.asarray(far_bias())

    def both(*rows):
        return [((count, 256), bf16) for count in rows]

    def cost(pairs, products):
        return dict(flops=2 * HEAD * products * pairs, exps=pairs, nbytes=4 << 20)

    kv, s1, s2 = call(
        prepare_keys_kernel, both(ROWS, 1024, 512), (keys, values), [pltpu.VMEM((ROWS, HEAD), f32)], nbytes=8 << 20, vmem=12
    )
    r1, r2, r3 = swap(s1, 1), swap(s2, 2), swap(s2, 3)
    q, g, whole = call(
        prepare_queries_kernel,
        [((ROWS, HEAD), bf16), ((ROWS, HEAD), bf16), *both(ROWS)],
        (queries, cotangent, s2),
        [pltpu.VMEM((ROWS, HEAD), f32)],
        nbytes=8 << 20,
        vmem=12,
    )
    stat, out = call(
        own_forward_kernel,
        [((8, ROWS), f32), ((HEAD, ROWS), f32)],
        (q, kv, near_bias),
        [pltpu.VMEM((HEAD, ROWS), bf16)],
        vmem=28,
        **cost(ROWS * ROWS, 2),
    )
    pair = jnp.concatenate([s2[:256], r1[:256]], 0)
    r1, r2, r3, stat, pair, whole = lax.optimization_barrier((r1, r2, r3, stat, pair, whole))
    r4, r6 = swap(pair, 4), swap(pair, 6)
    whole = swap_whole(whole)
    stat, out = call(
        middle_forward_kernel,
        [((8, ROWS), f32), ((HEAD, ROWS), f32)],
        (q, other_bias, stat, out, r1, r2, r3),
        vmem=20,
        **cost(1536 * 1024, 2),
    )
    (row,) = call(
        last_forward_kernel,
        [((8, ROWS), f32)],
        (q, g, other_bias, stat, out, r4, r6, whole),
        [pltpu.VMEM((8, 256), f32), pltpu.VMEM((HEAD, 256), f32)],
        vmem=16,
        **cost(512 * 1024, 2),
    )
    rows = (q, g, other_bias, row)
    o4, o6, dq3 = call(
        third_backward_kernel, [*both(512, 512), ((HEAD, 256), f32)], (*rows, r4, r6), vmem=12, **cost(256 * 1024, 5)
    )
    b4, b6 = swap(o4, 4), swap(o6, 6)
    o2, o3, dq2 = call(
        second_backward_kernel, [*both(512, 512), ((HEAD, 512), f32)], (*rows, r2, r3), vmem=12, **cost(512 * 1024, 5)
    )
    b2, b3 = swap(o2, 2), swap(o3, 3)
    o1, dq1 = call(
        first_backward_kernel, [*both(1024), ((HEAD, 1024), f32)], (*rows, r1), vmem=16, **cost(1024 * 1024, 5)
    )
    (o1,) = call(relay_kernel, both(1024), (o1, b4, b6), vmem=8, nbytes=1 << 20)
    o1, whole = lax.optimization_barrier((o1, whole))
    b1 = swap(o1, 1)
    whole, far_dq = call(
        whole_backward_kernel,
        [*both(ROWS), ((HEAD, 1024), f32)],
        (*rows, whole, dq1, dq2, dq3),
        vmem=12,
        **cost(256 * 1024, 5),
    )
    b2, b3, whole = lax.optimization_barrier((b2, b3, whole))
    whole = swap_whole(whole)
    dq, dkv = call(
        own_backward_kernel,
        [((ROWS, HEAD), f32), *[((ROWS, 256), f32)]],
        (q, g, near_bias, row, kv, far_dq),
        [pltpu.VMEM((HEAD, ROWS), f32), pltpu.VMEM((ROWS, HEAD), f32)],
        vmem=32,
        **cost(ROWS * ROWS, 5),
    )
    dk, dv = call(
        join_kernel, [((ROWS, HEAD), f32)] * 2, (dkv, b1, b2, b3, b4, b6, whole), [pltpu.VMEM((ROWS, 256), f32)], nbytes=8 << 20, vmem=16
    )
    return dq, dk, dv


def solution(mesh):
    spec = P(("grp", "seq"), None)
    return jax.shard_map(
        on_device, mesh=mesh, in_specs=(spec,) * 4, out_specs=(spec,) * 3, check_vma=False
    )
```

```python
import functools
import math

import jax
import jax.numpy as jnp
import numpy as np
from jax import lax
from jax.experimental import pallas as pl
from jax.experimental.pallas import tpu as pltpu
from jax.sharding import PartitionSpec as P

ROWS = 2048
HEAD = 128
UNIT = 256
ORDER = (0, 4, 2, 6, 1, 3, 5, 7)
SCALE = HEAD**-0.5
SCALE2 = SCALE * math.log2(math.e)
NEG = -1e30
VMEM = 60 << 20
QUADS = 4
FAR = 64
BLOCK = 512


def unit_level(unit):
    return 3 if unit == 0 else 2 if unit == 1 else 1 if unit < 4 else 0


def own_bias():
    table = np.zeros((8, ROWS), np.float32)
    for key_unit in range(8):
        for query_unit in range(8):
            shared = 1 + min(unit_level(key_unit), unit_level(query_unit))
            table[key_unit, query_unit * UNIT : (query_unit + 1) * UNIT] = math.log2(shared)
    return table


def far_bias():
    table = np.zeros((8, 1024), np.float32)
    for query_unit in range(4):
        lanes = slice(query_unit * UNIT, (query_unit + 1) * UNIT)
        level = unit_level(query_unit)
        table[0, lanes] = math.log2(min(3, level))
        table[1, lanes] = math.log2(min(2, level))
        if level >= 2:
            table[2, lanes] = math.log2(level - 1)
    table[3, 8:] = NEG
    return table


def dot_nt(left, right):
    return lax.dot_general(left, right, (((1,), (1,)), ((), ())), preferred_element_type=jnp.float32)


def dot_nn(left, right):
    return lax.dot_general(left, right, (((1,), (0,)), ((), ())), preferred_element_type=jnp.float32)


def dot_tn(left, right):
    return lax.dot_general(left, right, (((0,), (0,)), ((), ())), preferred_element_type=jnp.float32)


def call(kernel, outs, args, scratch=(), scalars=0):
    return pl.pallas_call(
        kernel,
        out_shape=[jax.ShapeDtypeStruct(shape, dtype) for shape, dtype in outs],
        in_specs=[
            pl.BlockSpec(memory_space=pltpu.SMEM if at < scalars else pltpu.VMEM) for at in range(len(args))
        ],
        out_specs=[pl.BlockSpec(memory_space=pltpu.VMEM)] * len(outs),
        scratch_shapes=list(scratch),
        compiler_params=pltpu.CompilerParams(vmem_limit_bytes=VMEM),
        cost_estimate=pl.CostEstimate(flops=0, bytes_accessed=0, transcendentals=0),
    )(*args)


def sort_rows(source, target, lane, wide):
    wide[...] = source[...].astype(jnp.float32)
    for unit, residue in enumerate(ORDER):
        for pair in range(16):
            parts = [
                wide[pl.ds(8 * (2 * pair + half) + residue, 8, stride=256), :] for half in range(2)
            ]
            rows = slice(unit * UNIT + 16 * pair, unit * UNIT + 16 * pair + 16)
            target[rows, lane : lane + HEAD] = jnp.concatenate(parts, 0).astype(jnp.bfloat16)


def repeat_first(source, target, lane):
    first = source[:16, :].astype(jnp.float32)[:8]
    pair = jnp.concatenate([first, first], 0).astype(jnp.bfloat16)
    for at in range(0, target.shape[0], 16):
        target[at : at + 16, lane : lane + pair.shape[1]] = pair


def prepare_keys_kernel(k_ref, v_ref, q_ref, g_ref, kv_ref, s1_ref, s2_ref, s3_ref, far_ref, wide):
    sort_rows(k_ref, kv_ref, 0, wide)
    sort_rows(v_ref, kv_ref, HEAD, wide)
    s1_ref[:1024] = kv_ref[:1024]
    s2_ref[:512] = kv_ref[:512]
    s3_ref[...] = kv_ref[:256]
    repeat_first(kv_ref, far_ref, 0)
    for lane, ref in ((0, q_ref), (HEAD, g_ref)):
        rows = [ref[at : at + 16, :].astype(jnp.float32)[:1] for at in range(0, ROWS, 256)]
        block = jnp.concatenate(rows + rows, 0).astype(jnp.bfloat16)
        s1_ref[1024:, lane : lane + HEAD] = block
        s2_ref[512:, lane : lane + HEAD] = block


def prepare_queries_kernel(q_ref, g_ref, after_ref, qp_ref, gp_ref, wide):
    sort_rows(q_ref, qp_ref, 0, wide)
    sort_rows(g_ref, gp_ref, 0, wide)


def add_bias(block, rows):
    if all(row is None for row in rows):
        return block
    parts = []
    for at, row in enumerate(rows):
        part = block[at * UNIT : (at + 1) * UNIT]
        parts.append(part if row is None else part + row)
    return jnp.concatenate(parts, 0)


def attend(query, keys, values, biases):
    scores = [add_bias(dot_nt(key, query) * SCALE2, bias) for key, bias in zip(keys, biases)]
    peak = functools.reduce(jnp.maximum, [jnp.max(block, 0, keepdims=True) for block in scores])
    probs = [jnp.exp2(block - peak) for block in scores]
    total = sum([jnp.sum(block, 0, keepdims=True) for block in probs])
    out = sum([value(block.astype(jnp.bfloat16)) for value, block in zip(values, probs)])
    return peak, total, out


def own_forward_kernel(q_ref, kv_ref, bias_ref, stat_ref, out_ref, vt_ref):
    stat_ref[...] = jnp.zeros_like(stat_ref)
    for unit in range(8):
        rows = slice(unit * UNIT, (unit + 1) * UNIT)
        vt_ref[:, rows] = kv_ref[rows, HEAD:].astype(jnp.float32).T.astype(jnp.bfloat16)
    for start in (0, 1024):
        lanes = slice(start, start + 1024)
        keys, values, biases = [], [], []
        for at in range(0, ROWS, BLOCK):
            rows = slice(at, at + BLOCK)
            keys.append(kv_ref[rows, :HEAD])
            values.append(lambda prob, rows=rows: dot_nn(vt_ref[:, rows], prob))
            unit = at // UNIT
            counted = start == 0 and at < 1024
            biases.append([bias_ref[unit + half : unit + half + 1, lanes] if counted else None for half in (0, 1)])
        peak, total, out = attend(q_ref[lanes, :], keys, values, biases)
        stat_ref[0:1, lanes] = peak
        stat_ref[1:2, lanes] = total
        out_ref[:, lanes] = out


def bias_rows(bias_ref, picks, count):
    return [None if pick is None else bias_ref[pick : pick + 1, :count] for pick in picks]


PARTNER, PARTNER_REST, SECOND, THIRD = (0, 1), (None, None), (2, None), (None, None)


def far_blocks(r1, r2, r3):
    return (
        (1024, [((r1, 0), PARTNER), ((r1, BLOCK), PARTNER_REST)]),
        (512, [((ref, 0), SECOND) for ref in r2]),
        (256, [(r3[0:2], THIRD), (r3[2:4], THIRD)]),
    )


def read_block(place, lanes):
    ref, first = place
    if isinstance(first, int):
        return ref[first : first + BLOCK, lanes]
    return jnp.concatenate([ref[:, lanes], first[:, lanes]], 0)


def write_block(place, block):
    ref, first = place
    if isinstance(first, int):
        ref[first : first + BLOCK, :] = block
    else:
        ref[...] = block[:UNIT]
        first[...] = block[UNIT:]


def join_state(sums, acc, lanes, far_peak, far_total, far_out):
    peak = sums[0:1, lanes]
    top = jnp.maximum(peak, far_peak)
    near, far = jnp.exp2(peak - top), jnp.exp2(far_peak - top)
    sums[0:1, lanes] = top
    sums[1:2, lanes] = near * sums[1:2, lanes] + far * far_total
    acc[:, lanes] = near * acc[:, lanes] + far * far_out


def middle_forward_kernel(q_ref, bias_ref, stat_ref, out_ref, *rest):
    r1, r2, r3, (sums, acc) = rest[0], rest[1:3], rest[3:7], rest[7:]
    sums[...] = stat_ref[...]
    acc[...] = out_ref[...]
    for count, blocks in far_blocks(r1, r2, r3):
        lanes = slice(0, count)
        state = attend(
            q_ref[lanes, :],
            [read_block(place, slice(0, HEAD)) for place, _ in blocks],
            [lambda prob, place=place: dot_tn(read_block(place, slice(HEAD, 256)), prob) for place, _ in blocks],
            [bias_rows(bias_ref, picks, count) for _, picks in blocks],
        )
        join_state(sums, acc, lanes, *state)


def whole_forward_kernel(me_ref, own, r1, r2, r3, far_ref, part_ref, quad_ref, rows_ref):
    for mask, ref in enumerate((own, r1, r2, r3)):
        count = ref.shape[0]
        place = pl.multiple_of((me_ref[0] ^ mask) * 8, 8)
        rows_ref[pl.ds(place, 8), :] = ref[count - 16 :, :].astype(jnp.float32)[:8]
    quad_ref[...] = rows_ref[...].astype(jnp.bfloat16)
    scores = dot_nt(quad_ref[:, :HEAD], far_ref[:, :HEAD]) * SCALE2
    peak = jnp.max(scores, 1, keepdims=True)
    prob = jnp.exp2(scores - peak)
    part_ref[:, :HEAD] = dot_nn(prob.astype(jnp.bfloat16), far_ref[:, HEAD:])
    part_ref[:, HEAD : 2 * HEAD] = jnp.broadcast_to(peak, (8 * QUADS, HEAD))
    part_ref[:, 2 * HEAD :] = jnp.broadcast_to(jnp.sum(prob, 1, keepdims=True), (8 * QUADS, HEAD))


def turn(block, fill):
    return jnp.concatenate([block, jnp.full((HEAD - 8, HEAD), fill, jnp.float32)], 0).T


def finish_kernel(g_ref, stat_ref, out_ref, part_ref, row_ref, tall_ref, sums, acc):
    lanes = slice(0, HEAD)
    sums[...] = stat_ref[:, lanes]
    acc[...] = out_ref[:, lanes]
    for at in range(0, 8 * QUADS, 8):
        part = part_ref[at : at + 8, :]
        far_out = turn(part[:, :HEAD], 0.0)
        far_peak = turn(part[:, HEAD : 2 * HEAD], NEG)[0:1]
        far_total = turn(part[:, 2 * HEAD :], 0.0)[0:1]
        join_state(sums, acc, lanes, far_peak, far_total, far_out)
    row_ref[...] = jnp.zeros_like(row_ref)
    for first in range(0, ROWS, HEAD):
        lanes = slice(first, first + HEAD)
        stat, out = (sums[...], acc[...]) if first == 0 else (stat_ref[:, lanes], out_ref[:, lanes])
        total = stat[1:2]
        row_ref[0:1, lanes] = stat[0:1] + jnp.log2(total)
        grad = g_ref[lanes, :].astype(jnp.float32).T
        row_ref[1:2, lanes] = jnp.sum(grad * out, axis=0, keepdims=True) / total
    tall = jnp.concatenate([row_ref[:, :HEAD], jnp.zeros((HEAD - 8, HEAD), jnp.float32)], 0).T
    for at in range(0, 8 * QUADS, 8):
        tall_ref[at : at + 8, :] = tall[:8]


def remote_backward_kernel(q_ref, g_ref, bias_ref, row_ref, *rest):
    far, outs, dq_ref = rest[:7], rest[7:14], rest[14]
    dq_ref[...] = jnp.zeros_like(dq_ref)
    sources, targets = (far_blocks(refs[0], refs[1:3], refs[3:7]) for refs in (far, outs))
    for (count, blocks), (_, places) in zip(sources, targets):
        for (place, picks), (target, _) in zip(blocks, places):
            bias = bias_rows(bias_ref, picks, count)
            both = backward_block(read_block(place, slice(0, 256)), q_ref, g_ref, row_ref, bias, count, dq_ref)
            write_block(target, jnp.concatenate(both, 1).astype(jnp.bfloat16))


def whole_backward_kernel(quad_ref, far_ref, tall_ref, dq_ref, out_ref):
    query, grad = quad_ref[:, :HEAD], quad_ref[:, HEAD:]
    key, value = far_ref[:, :HEAD], far_ref[:, HEAD:]
    weights = jnp.exp2(dot_nt(query, key) * SCALE2 - tall_ref[:, 0:1])
    grad_scores = (weights * (dot_nt(grad, value) - tall_ref[:, 1:2])).astype(jnp.bfloat16)
    dq_ref[...] = dot_nn(grad_scores, key)
    out_ref[:, :HEAD] = (SCALE * dot_tn(grad_scores, query)).astype(jnp.bfloat16)
    out_ref[:, HEAD:] = dot_tn(weights.astype(jnp.bfloat16), grad).astype(jnp.bfloat16)


def backward_block(kv_block, q_ref, g_ref, row_ref, bias, count, dq_ref):
    key, value = kv_block[:, :HEAD], kv_block[:, HEAD:]
    lanes = slice(0, count)
    query, grad = q_ref[lanes, :], g_ref[lanes, :]
    scores = add_bias(dot_nt(key, query) * SCALE2, bias)
    weights = jnp.exp2(scores - row_ref[0:1, lanes])
    grad_probs = dot_nt(value, grad)
    grad_scores = (weights * (grad_probs - row_ref[1:2, lanes])).astype(jnp.bfloat16)
    grad_value = dot_nn(weights.astype(jnp.bfloat16), grad)
    grad_key = dot_nn(grad_scores, query)
    dq_ref[:, lanes] += dot_tn(key, grad_scores)
    return SCALE * grad_key, grad_value


def own_backward_kernel(q_ref, g_ref, bias_ref, row_ref, kv_ref, far_ref, quad_ref, dq_ref, dkv_ref, acc_ref, tall_ref):
    acc_ref[:, :1024] = far_ref[...]
    acc_ref[:, 1024:] = jnp.zeros((HEAD, 1024), jnp.float32)

    def one(at, carry):
        rows = pl.ds(pl.multiple_of(at * BLOCK, BLOCK), BLOCK)
        bias = [bias_ref[pl.ds(2 * at + half, 1), :] for half in (0, 1)]
        grad_key, grad_value = backward_block(kv_ref[rows, :], q_ref, g_ref, row_ref, bias, ROWS, acc_ref)
        dkv_ref[rows, :HEAD] = grad_key
        dkv_ref[rows, HEAD:] = grad_value
        return carry

    lax.fori_loop(0, ROWS // BLOCK, one, 0)
    for unit in range(8):
        lanes = slice(unit * UNIT, (unit + 1) * UNIT)
        tall_ref[lanes, :] = acc_ref[:, lanes].T * SCALE
    for at in range(0, 8 * QUADS, 8):
        tall_ref[:8, :] += SCALE * quad_ref[at : at + 8, :]
    restore_rows(lambda rows: tall_ref[rows, :], dq_ref)


def restore_rows(read, target):
    for unit, residue in enumerate(ORDER):
        for block in range(32):
            start = unit * UNIT + 8 * block
            target[pl.ds(8 * block + residue, 8, stride=256), :] = read(slice(start, start + 8))


def join_kernel(dkv_ref, b1, b2, b3, b4, b5, b6, b7, far_ref, dk_ref, dv_ref, sum_ref):
    def wide(ref, rows=slice(None)):
        return ref[rows, :].astype(jnp.float32)

    top, mid, low = slice(0, 256), slice(256, 512), slice(512, 1024)
    near = wide(b1, top) + wide(b2, top) + wide(b3, top)
    sum_ref[top, :] = dkv_ref[top, :] + near + wide(b4) + wide(b5) + wide(b6) + wide(b7)
    sum_ref[mid, :] = dkv_ref[mid, :] + wide(b1, mid) + wide(b2, mid) + wide(b3, mid)
    sum_ref[low, :] = dkv_ref[low, :] + wide(b1, low)
    sum_ref[1024:, :] = dkv_ref[1024:, :]
    sum_ref[:8, :] += jnp.sum(wide(far_ref).reshape(FAR, 8, 256), 0)
    restore_rows(lambda rows: sum_ref[rows, :HEAD], dk_ref)
    restore_rows(lambda rows: sum_ref[rows, HEAD:], dv_ref)


def swap(block, mask):
    return lax.ppermute(block, ("z", "y"), [(at, at ^ mask) for at in range(16)])


def swap_all(sends):
    near = [swap(block, mask) for block, mask in zip(sends[:5], (1, 2, 3, 4, 5))]
    last = []
    for at, (block, mask) in enumerate(zip(sends[5:], (6, 7))):
        near[3 + at], block = lax.optimization_barrier((near[3 + at], block))
        last.append(swap(block, mask))
    return near + last


def swap_quad(block):
    parts = block.reshape(QUADS, 8, block.shape[1])
    return lax.all_to_all(parts, "y", 0, 0).reshape(block.shape)


def swap_far(block):
    parts = block.reshape(FAR, 8, block.shape[1])
    return lax.all_to_all(parts, ("grp", "x", "z"), 0, 0).reshape(block.shape)


def on_device(queries, keys, values, cotangent):
    f32, bf16 = jnp.float32, jnp.bfloat16
    near_bias, other_bias = jnp.asarray(own_bias()), jnp.asarray(far_bias())
    sizes = (1024, 512, 512, 256, 256, 256, 256)

    def both(*rows):
        return [((count, 256), bf16) for count in rows]

    wide = [pltpu.VMEM((ROWS, HEAD), f32)]
    kv, s1, s2, s3, far = call(
        prepare_keys_kernel, both(ROWS, 1040, 528, 256, 8 * FAR), (keys, values, queries, cotangent), wide
    )
    peers = swap_all([s1, s2, s2, s3, s3, s3, s3])
    far = swap_far(far)
    q, g = call(prepare_queries_kernel, [((ROWS, HEAD), bf16)] * 2, (queries, cotangent, s3), wide)
    state = [((8, ROWS), f32), ((HEAD, ROWS), f32)]
    stat, out = call(own_forward_kernel, state, (q, kv, near_bias), [pltpu.VMEM((HEAD, ROWS), bf16)])
    stat, far = lax.optimization_barrier((stat, far))
    me = lax.axis_index("y").astype(jnp.int32).reshape(1)
    part, quad = call(
        whole_forward_kernel,
        [((8 * QUADS, 3 * HEAD), f32), *both(8 * QUADS)],
        (me, s2, *peers[:3], far),
        [pltpu.VMEM((8 * QUADS, 256), f32)],
        scalars=1,
    )
    part = swap_quad(part)
    stat, out = call(middle_forward_kernel, state, (q, other_bias, stat, out, *peers))
    row, tall = call(
        finish_kernel,
        [((8, ROWS), f32), ((8 * QUADS, HEAD), f32)],
        (g, stat, out, part),
        [pltpu.VMEM((8, HEAD), f32), pltpu.VMEM((HEAD, HEAD), f32)],
    )
    tall = swap_quad(tall)
    *sends, far_dq = call(
        remote_backward_kernel, [*both(*sizes), ((HEAD, 1024), f32)], (q, g, other_bias, row, *peers)
    )
    back = swap_all(sends)
    far_dq, tall = lax.optimization_barrier((far_dq, tall))
    quad_dq, far_dkv = call(
        whole_backward_kernel, [((8 * QUADS, HEAD), f32), *both(8 * FAR)], (quad, far, tall)
    )
    quad_dq = swap_quad(quad_dq)
    far_dkv = swap_far(far_dkv)
    dq, dkv = call(
        own_backward_kernel,
        [((ROWS, HEAD), f32), ((ROWS, 256), f32)],
        (q, g, near_bias, row, kv, far_dq, quad_dq),
        [pltpu.VMEM((HEAD, ROWS), f32), pltpu.VMEM((ROWS, HEAD), f32)],
    )
    dk, dv = call(join_kernel, [((ROWS, HEAD), f32)] * 2, (dkv, *back, far_dkv), [pltpu.VMEM((ROWS, 256), f32)])
    return dq, dk, dv


def solution(mesh):
    axes = ("grp", "x", "z", "y")
    split = jax.sharding.Mesh(mesh.devices.reshape(4, 4, 4, 4), axes)
    spec = P(axes, None)
    return jax.shard_map(
        on_device, mesh=split, in_specs=(spec,) * 4, out_specs=(spec,) * 3, check_vma=False
    )
```

```python
import functools
import math

import jax
import jax.numpy as jnp
import numpy as np
from jax import lax
from jax.experimental import pallas as pl
from jax.experimental.pallas import tpu as pltpu
from jax.sharding import PartitionSpec as P

ROWS = 2048
HEAD = 128
UNIT = 256
ORDER = (0, 4, 2, 6, 1, 3, 5, 7)
SCALE = HEAD**-0.5
SCALE2 = SCALE * math.log2(math.e)
NEG = -1e30
VMEM = 60 << 20
QUADS = 4
FAR = 64
BLOCK = 512
HALF = 1024


def unit_level(unit):
    return 3 if unit == 0 else 2 if unit == 1 else 1 if unit < 4 else 0


def own_bias():
    table = np.zeros((8, ROWS), np.float32)
    for key_unit in range(8):
        for query_unit in range(8):
            shared = 1 + min(unit_level(key_unit), unit_level(query_unit))
            table[key_unit, query_unit * UNIT : (query_unit + 1) * UNIT] = math.log2(shared)
    return table


def far_bias():
    table = np.zeros((8, 1024), np.float32)
    for query_unit in range(4):
        lanes = slice(query_unit * UNIT, (query_unit + 1) * UNIT)
        level = unit_level(query_unit)
        table[0, lanes] = math.log2(min(3, level))
        table[1, lanes] = math.log2(min(2, level))
        if level >= 2:
            table[2, lanes] = math.log2(level - 1)
    table[3, 8:] = NEG
    return table


def dot_nt(left, right):
    return lax.dot_general(left, right, (((1,), (1,)), ((), ())), preferred_element_type=jnp.float32)


def dot_nn(left, right):
    return lax.dot_general(left, right, (((1,), (0,)), ((), ())), preferred_element_type=jnp.float32)


def dot_tn(left, right):
    return lax.dot_general(left, right, (((0,), (0,)), ((), ())), preferred_element_type=jnp.float32)


def call(kernel, outs, args, scratch=(), scalars=0, steps=(), in_steps=(), out_steps=(), in_place=None):
    def spec(shape, stepped, at_rest, scalar=False):
        if at_rest:
            return pl.BlockSpec(memory_space=pl.ANY)
        if scalar:
            return pl.BlockSpec(memory_space=pltpu.SMEM)
        if not steps:
            return pl.BlockSpec(memory_space=pltpu.VMEM)
        if stepped:
            return pl.BlockSpec((BLOCK, shape[1]), lambda at: (at, 0))
        return pl.BlockSpec(shape, lambda at: (0, 0))

    return pl.pallas_call(
        kernel,
        grid=steps,
        out_shape=[jax.ShapeDtypeStruct(shape, dtype) for shape, dtype in outs],
        in_specs=[spec(arg.shape, at in in_steps, at == in_place, at < scalars) for at, arg in enumerate(args)],
        out_specs=[
            spec(shape, at in out_steps, in_place is not None and at == 0) for at, (shape, _) in enumerate(outs)
        ],
        scratch_shapes=list(scratch),
        input_output_aliases={} if in_place is None else {in_place: 0},
        compiler_params=pltpu.CompilerParams(vmem_limit_bytes=VMEM),
        cost_estimate=pl.CostEstimate(flops=0, bytes_accessed=0, transcendentals=0),
    )(*args)


def sort_rows(source, target, lane, wide):
    wide[...] = source[...].astype(jnp.float32)
    for unit, residue in enumerate(ORDER):
        for pair in range(16):
            parts = [
                wide[pl.ds(8 * (2 * pair + half) + residue, 8, stride=256), :] for half in range(2)
            ]
            rows = slice(unit * UNIT + 16 * pair, unit * UNIT + 16 * pair + 16)
            target[rows, lane : lane + HEAD] = jnp.concatenate(parts, 0).astype(jnp.bfloat16)


def repeat_first(source, target, lane):
    first = source[:16, :].astype(jnp.float32)[:8]
    pair = jnp.concatenate([first, first], 0).astype(jnp.bfloat16)
    for at in range(0, target.shape[0], 16):
        target[at : at + 16, lane : lane + pair.shape[1]] = pair


def prepare_keys_kernel(k_ref, v_ref, q_ref, g_ref, kv_ref, s1_ref, s2_ref, s3_ref, far_ref, wide):
    sort_rows(k_ref, kv_ref, 0, wide)
    sort_rows(v_ref, kv_ref, HEAD, wide)
    s1_ref[:1024] = kv_ref[:1024]
    s2_ref[:512] = kv_ref[:512]
    s3_ref[...] = kv_ref[:256]
    repeat_first(kv_ref, far_ref, 0)
    for lane, ref in ((0, q_ref), (HEAD, g_ref)):
        rows = [ref[at : at + 16, :].astype(jnp.float32)[:1] for at in range(0, ROWS, 256)]
        block = jnp.concatenate(rows + rows, 0).astype(jnp.bfloat16)
        s1_ref[1024:, lane : lane + HEAD] = block
        s2_ref[512:, lane : lane + HEAD] = block


def prepare_queries_kernel(q_ref, g_ref, after_ref, qp_ref, gp_ref, wide):
    sort_rows(q_ref, qp_ref, 0, wide)
    sort_rows(g_ref, gp_ref, 0, wide)


def add_bias(block, rows):
    if all(row is None for row in rows):
        return block
    parts = []
    for at, row in enumerate(rows):
        part = block[at * UNIT : (at + 1) * UNIT]
        parts.append(part if row is None else part + row)
    return jnp.concatenate(parts, 0)


def attend(query, keys, values, biases):
    scores = [add_bias(dot_nt(key, query) * SCALE2, bias) for key, bias in zip(keys, biases)]
    peak = functools.reduce(jnp.maximum, [jnp.max(block, 0, keepdims=True) for block in scores])
    probs = [jnp.exp2(block - peak) for block in scores]
    total = sum([jnp.sum(block, 0, keepdims=True) for block in probs])
    out = sum([value(block.astype(jnp.bfloat16)) for value, block in zip(values, probs)])
    return peak, total, out


def finish_rows(row_ref, target, stat, out, grad):
    total = stat[1:2]
    row_ref[0:1, target] = stat[0:1] + jnp.log2(total)
    row_ref[1:2, target] = jnp.sum(grad.astype(jnp.float32).T * out, axis=0, keepdims=True) / total


def own_forward_kernel(q_ref, kv_ref, g_ref, bias_ref, stat_ref, out_ref, odd_ref, vt_ref):
    stat_ref[...] = jnp.zeros_like(stat_ref)
    odd_ref[...] = jnp.zeros_like(odd_ref)
    for unit in range(8):
        rows = slice(unit * UNIT, (unit + 1) * UNIT)
        vt_ref[:, rows] = kv_ref[rows, HEAD:].astype(jnp.float32).T.astype(jnp.bfloat16)
    for start in (0, HALF):
        lanes = slice(start, start + HALF)
        keys, values, biases = [], [], []
        for at in range(0, ROWS, BLOCK):
            rows = slice(at, at + BLOCK)
            keys.append(kv_ref[rows, :HEAD])
            values.append(lambda prob, rows=rows: dot_nn(vt_ref[:, rows], prob))
            unit = at // UNIT
            counted = start == 0 and at < HALF
            biases.append([bias_ref[unit + half : unit + half + 1, lanes] if counted else None for half in (0, 1)])
        peak, total, out = attend(q_ref[lanes, :], keys, values, biases)
        if start == 0:
            stat_ref[0:1, :] = peak
            stat_ref[1:2, :] = total
            out_ref[...] = out
        else:
            stat = jnp.concatenate([peak, total], 0)
            for first in range(0, HALF, UNIT):
                part = slice(first, first + UNIT)
                grad = g_ref[HALF + first : HALF + first + UNIT, :]
                finish_rows(odd_ref, part, stat[:, part], out[:, part], grad)


def bias_rows(bias_ref, picks, count):
    return [None if pick is None else bias_ref[pick : pick + 1, :count] for pick in picks]


PARTNER, PARTNER_REST, SECOND, THIRD = (0, 1), (None, None), (2, None), (None, None)


def far_blocks(r1, r2, r3):
    return (
        (1024, [((r1, 0), PARTNER), ((r1, BLOCK), PARTNER_REST)]),
        (512, [((ref, 0), SECOND) for ref in r2]),
        (256, [(r3[0:2], THIRD), (r3[2:4], THIRD)]),
    )


def read_block(place, lanes):
    ref, first = place
    if isinstance(first, int):
        return ref[first : first + BLOCK, lanes]
    return jnp.concatenate([ref[:, lanes], first[:, lanes]], 0)


def write_block(place, block):
    ref, first = place
    if isinstance(first, int):
        ref[first : first + BLOCK, :] = block
    else:
        ref[...] = block[:UNIT]
        first[...] = block[UNIT:]


def join_state(sums, acc, lanes, far_peak, far_total, far_out):
    peak = sums[0:1, lanes]
    top = jnp.maximum(peak, far_peak)
    near, far = jnp.exp2(peak - top), jnp.exp2(far_peak - top)
    sums[0:1, lanes] = top
    sums[1:2, lanes] = near * sums[1:2, lanes] + far * far_total
    acc[:, lanes] = near * acc[:, lanes] + far * far_out


def middle_forward_kernel(q_ref, bias_ref, stat_ref, out_ref, *rest):
    r1, r2, r3, (sums, acc) = rest[0], rest[1:3], rest[3:7], rest[7:]
    sums[...] = stat_ref[...]
    acc[...] = out_ref[...]
    for count, blocks in far_blocks(r1, r2, r3):
        lanes = slice(0, count)
        state = attend(
            q_ref[lanes, :],
            [read_block(place, slice(0, HEAD)) for place, _ in blocks],
            [lambda prob, place=place: dot_tn(read_block(place, slice(HEAD, 256)), prob) for place, _ in blocks],
            [bias_rows(bias_ref, picks, count) for _, picks in blocks],
        )
        join_state(sums, acc, lanes, *state)


def whole_forward_kernel(me_ref, own, r1, r2, r3, far_ref, part_ref, quad_ref, rows_ref):
    for mask, ref in enumerate((own, r1, r2, r3)):
        count = ref.shape[0]
        place = pl.multiple_of((me_ref[0] ^ mask) * 8, 8)
        rows_ref[pl.ds(place, 8), :] = ref[count - 16 :, :].astype(jnp.float32)[:8]
    quad_ref[...] = rows_ref[...].astype(jnp.bfloat16)
    scores = dot_nt(quad_ref[:, :HEAD], far_ref[:, :HEAD]) * SCALE2
    peak = jnp.max(scores, 1, keepdims=True)
    prob = jnp.exp2(scores - peak)
    part_ref[:, :HEAD] = dot_nn(prob.astype(jnp.bfloat16), far_ref[:, HEAD:])
    part_ref[:, HEAD : 2 * HEAD] = jnp.broadcast_to(peak, (8 * QUADS, HEAD))
    part_ref[:, 2 * HEAD :] = jnp.broadcast_to(jnp.sum(prob, 1, keepdims=True), (8 * QUADS, HEAD))


def turn(block, fill):
    return jnp.concatenate([block, jnp.full((HEAD - 8, HEAD), fill, jnp.float32)], 0).T


def finish_kernel(g_ref, stat_ref, out_ref, odd_ref, part_ref, row_ref, tall_ref, sums, acc):
    lanes = slice(0, HEAD)
    sums[...] = stat_ref[:, lanes]
    acc[...] = out_ref[:, lanes]
    for at in range(0, 8 * QUADS, 8):
        part = part_ref[at : at + 8, :]
        far_out = turn(part[:, :HEAD], 0.0)
        far_peak = turn(part[:, HEAD : 2 * HEAD], NEG)[0:1]
        far_total = turn(part[:, 2 * HEAD :], 0.0)[0:1]
        join_state(sums, acc, lanes, far_peak, far_total, far_out)
    row_ref[...] = jnp.zeros_like(row_ref)
    row_ref[:, HALF:] = odd_ref[...]
    for first in range(0, HALF, HEAD):
        lanes = slice(first, first + HEAD)
        stat, out = (sums[...], acc[...]) if first == 0 else (stat_ref[:, lanes], out_ref[:, lanes])
        finish_rows(row_ref, lanes, stat, out, g_ref[lanes, :])
    tall = jnp.concatenate([row_ref[:, :HEAD], jnp.zeros((HEAD - 8, HEAD), jnp.float32)], 0).T
    for at in range(0, 8 * QUADS, 8):
        tall_ref[at : at + 8, :] = tall[:8]


def remote_backward_kernel(me_ref, q_ref, g_ref, bias_ref, row_ref, quad_ref, far_ref, tall_ref, *rest):
    far, outs, (dkv_ref, dq_ref, mine_ref, quad_dq) = rest[:7], rest[7:14], rest[14:]
    query, grad = quad_ref[:, :HEAD], quad_ref[:, HEAD:]
    key, value = far_ref[:, :HEAD], far_ref[:, HEAD:]
    weights = jnp.exp2(dot_nt(query, key) * SCALE2 - tall_ref[:, 0:1])
    grad_scores = (weights * (dot_nt(grad, value) - tall_ref[:, 1:2])).astype(jnp.bfloat16)
    dkv_ref[:, :HEAD] = (SCALE * dot_tn(grad_scores, query)).astype(jnp.bfloat16)
    dkv_ref[:, HEAD:] = dot_tn(weights.astype(jnp.bfloat16), grad).astype(jnp.bfloat16)
    quad_dq[...] = dot_nn(grad_scores, key)
    for mask in range(QUADS):
        place = pl.multiple_of((me_ref[0] ^ mask) * 8, 8)
        block = quad_dq[pl.ds(place, 8), :]
        if mask == 0:
            mine_ref[...] = block
        else:
            block = jnp.concatenate([block, jnp.zeros_like(block)], 0)
            block = jnp.concatenate([block, jnp.zeros_like(block)], 1).astype(jnp.bfloat16)
            rows = outs[mask - 1].shape[0]
            outs[mask - 1][rows - 16 :, :] = block
    dq_ref[...] = jnp.zeros_like(dq_ref)
    sources, targets = (far_blocks(refs[0], refs[1:3], refs[3:7]) for refs in (far, outs))
    for (count, blocks), (_, places) in zip(sources, targets):
        for (place, picks), (target, _) in zip(blocks, places):
            bias = bias_rows(bias_ref, picks, count)
            both = backward_block(read_block(place, slice(0, 256)), q_ref, g_ref, row_ref, bias, count, dq_ref)
            write_block(target, jnp.concatenate(both, 1).astype(jnp.bfloat16))


def backward_block(kv_block, q_ref, g_ref, row_ref, bias, count, dq_ref):
    key, value = kv_block[:, :HEAD], kv_block[:, HEAD:]
    lanes = slice(0, count)
    query, grad = q_ref[lanes, :], g_ref[lanes, :]
    scores = add_bias(dot_nt(key, query) * SCALE2, bias)
    weights = jnp.exp2(scores - row_ref[0:1, lanes])
    grad_probs = dot_nt(value, grad)
    grad_scores = (weights * (grad_probs - row_ref[1:2, lanes])).astype(jnp.bfloat16)
    grad_value = dot_nn(weights.astype(jnp.bfloat16), grad)
    grad_key = dot_nn(grad_scores, query)
    dq_ref[:, lanes] += dot_tn(key, grad_scores)
    return SCALE * grad_key, grad_value


def own_backward_kernel(q_ref, g_ref, bias_ref, row_ref, kv_ref, far_ref, dq_ref, dkv_ref, acc_ref, tall_ref):
    at = pl.program_id(0)

    @pl.when(at == 0)
    def _():
        acc_ref[:, :HALF] = far_ref[...]
        acc_ref[:, HALF:] = jnp.zeros((HEAD, HALF), jnp.float32)

    bias = [bias_ref[pl.ds(2 * at + half, 1), :] for half in (0, 1)]
    grad_key, grad_value = backward_block(kv_ref[...], q_ref, g_ref, row_ref, bias, ROWS, acc_ref)
    dkv_ref[:, :HEAD] = grad_key
    dkv_ref[:, HEAD:] = grad_value

    @pl.when(at == ROWS // BLOCK - 1)
    def _():
        for unit in range(8):
            lanes = slice(unit * UNIT, (unit + 1) * UNIT)
            tall_ref[lanes, :] = acc_ref[:, lanes].T * SCALE
        restore_rows(lambda rows: tall_ref[rows, :], dq_ref)


def restore_rows(read, target):
    for unit, residue in enumerate(ORDER):
        for block in range(32):
            start = unit * UNIT + 8 * block
            target[pl.ds(8 * block + residue, 8, stride=256), :] = read(slice(start, start + 8))


def join_kernel(dkv_ref, mine_ref, b1, b2, b3, b4, b5, b6, b7, far_ref, dq_in, dq_out, dk_ref, dv_ref, sum_ref, tiles, sem):
    def wide(ref, rows=slice(None)):
        return ref[rows, :].astype(jnp.float32)

    places = [(pl.ds(256 * at, 8), pl.ds(8 * at, 8)) for at in range(8)]
    reads = [pltpu.make_async_copy(dq_in.at[rows], tiles.at[spot], sem.at[at]) for at, (rows, spot) in enumerate(places)]
    for copy in reads:
        copy.start()
    mine = mine_ref[...]
    for ref in (b1, b2, b3):
        mine = mine + ref[ref.shape[0] - 16 :, :HEAD].astype(jnp.float32)[:8]
    mine = SCALE * mine
    for copy in reads:
        copy.wait()
    for at in range(8):
        tiles[8 * at : 8 * at + 1, :] += mine[at : at + 1, :]
    writes = [pltpu.make_async_copy(tiles.at[spot], dq_out.at[rows], sem.at[8 + at]) for at, (rows, spot) in enumerate(places)]
    for copy in writes:
        copy.start()
    top, mid, low = slice(0, 256), slice(256, 512), slice(512, 1024)
    near = wide(b1, top) + wide(b2, top) + wide(b3, top)
    sum_ref[top, :] = dkv_ref[top, :] + near + wide(b4) + wide(b5) + wide(b6) + wide(b7)
    sum_ref[mid, :] = dkv_ref[mid, :] + wide(b1, mid) + wide(b2, mid) + wide(b3, mid)
    sum_ref[low, :] = dkv_ref[low, :] + wide(b1, low)
    sum_ref[1024:, :] = dkv_ref[1024:, :]
    sum_ref[:8, :] += jnp.sum(wide(far_ref).reshape(FAR, 8, 256), 0)
    restore_rows(lambda rows: sum_ref[rows, :HEAD], dk_ref)
    restore_rows(lambda rows: sum_ref[rows, HEAD:], dv_ref)
    for copy in writes:
        copy.wait()


def swap(block, mask):
    return lax.ppermute(block, ("z", "y"), [(at, at ^ mask) for at in range(16)])


def swap_all(sends):
    near = [swap(block, mask) for block, mask in zip(sends[:5], (1, 2, 3, 4, 5))]
    last = []
    for at, (block, mask) in enumerate(zip(sends[5:], (6, 7))):
        near[3 + at], block = lax.optimization_barrier((near[3 + at], block))
        last.append(swap(block, mask))
    return near + last


def swap_quad(block):
    parts = block.reshape(QUADS, 8, block.shape[1])
    return lax.all_to_all(parts, "y", 0, 0).reshape(block.shape)


def swap_far(block):
    parts = block.reshape(FAR, 8, block.shape[1])
    return lax.all_to_all(parts, ("grp", "x", "z"), 0, 0).reshape(block.shape)


def on_device(queries, keys, values, cotangent):
    f32, bf16 = jnp.float32, jnp.bfloat16
    near_bias, other_bias = jnp.asarray(own_bias()), jnp.asarray(far_bias())

    def both(*rows):
        return [((count, 256), bf16) for count in rows]

    wide = [pltpu.VMEM((ROWS, HEAD), f32)]
    kv, s1, s2, s3, far = call(
        prepare_keys_kernel, both(ROWS, 1040, 528, 256, 8 * FAR), (keys, values, queries, cotangent), wide
    )
    peers = swap_all([s1, s2, s2, s3, s3, s3, s3])
    q, g = call(prepare_queries_kernel, [((ROWS, HEAD), bf16)] * 2, (queries, cotangent, s3), wide)
    q, far, peers[3], peers[4] = lax.optimization_barrier((q, far, peers[3], peers[4]))
    far = swap_far(far)
    state = [((8, HALF), f32), ((HEAD, HALF), f32)]
    stat, out, odd = call(
        own_forward_kernel, [*state, ((8, HALF), f32)], (q, kv, g, near_bias), [pltpu.VMEM((HEAD, ROWS), bf16)]
    )
    stat, far = lax.optimization_barrier((stat, far))
    me = lax.axis_index("y").astype(jnp.int32).reshape(1)
    part, quad = call(
        whole_forward_kernel,
        [((8 * QUADS, 3 * HEAD), f32), *both(8 * QUADS)],
        (me, s2, *peers[:3], far),
        [pltpu.VMEM((8 * QUADS, 256), f32)],
        scalars=1,
    )
    part = swap_quad(part)
    stat, out = call(middle_forward_kernel, state, (q, other_bias, stat, out, *peers))
    row, tall = call(
        finish_kernel,
        [((8, ROWS), f32), ((8 * QUADS, HEAD), f32)],
        (g, stat, out, odd, part),
        [pltpu.VMEM((8, HEAD), f32), pltpu.VMEM((HEAD, HEAD), f32)],
    )
    tall = swap_quad(tall)
    *sends, far_dkv, far_dq, mine = call(
        remote_backward_kernel,
        [*both(1040, 528, 528, 256, 256, 256, 256, 8 * FAR), ((HEAD, HALF), f32), ((8, HEAD), f32)],
        (me, q, g, other_bias, row, quad, far, tall, *peers),
        [pltpu.VMEM((8 * QUADS, HEAD), f32)],
        scalars=1,
    )
    back = swap_all(sends)
    back[3], back[4], far_dkv = lax.optimization_barrier((back[3], back[4], far_dkv))
    far_dkv = swap_far(far_dkv)
    dq, dkv = call(
        own_backward_kernel,
        [((ROWS, HEAD), f32), ((ROWS, 256), f32)],
        (q, g, near_bias, row, kv, far_dq),
        [pltpu.VMEM((HEAD, ROWS), f32), pltpu.VMEM((ROWS, HEAD), f32)],
        steps=(ROWS // BLOCK,),
        in_steps=(4,),
        out_steps=(1,),
    )
    dq, dk, dv = call(
        join_kernel,
        [((ROWS, HEAD), f32)] * 3,
        (dkv, mine, *back, far_dkv, dq),
        [pltpu.VMEM((ROWS, 256), f32), pltpu.VMEM((64, HEAD), f32), pltpu.SemaphoreType.DMA((16,))],
        in_place=10,
    )
    return dq, dk, dv


def solution(mesh):
    axes = ("grp", "x", "z", "y")
    split = jax.sharding.Mesh(mesh.devices.reshape(4, 4, 4, 4), axes)
    spec = P(axes, None)
    return jax.shard_map(
        on_device, mesh=split, in_specs=(spec,) * 4, out_specs=(spec,) * 3, check_vma=False
    )
```

```python
import functools
import math

import jax
import jax.numpy as jnp
import numpy as np
from jax import lax
from jax.experimental import pallas as pl
from jax.experimental.pallas import tpu as pltpu
from jax.sharding import PartitionSpec as P

ROWS = 2048
HEAD = 128
UNIT = 256
ORDER = (0, 4, 2, 6, 1, 3, 5, 7)
SCALE = HEAD**-0.5
SCALE2 = SCALE * math.log2(math.e)
NEG = -1e30
QUADS = 4
FAR = 64
BLOCK = 512
HALF = 1024


def unit_level(unit):
    return 3 if unit == 0 else 2 if unit == 1 else 1 if unit < 4 else 0


def own_bias():
    table = np.zeros((8, ROWS), np.float32)
    for key_unit in range(8):
        for query_unit in range(8):
            shared = 1 + min(unit_level(key_unit), unit_level(query_unit))
            table[key_unit, query_unit * UNIT : (query_unit + 1) * UNIT] = math.log2(shared)
    return table


def far_bias():
    table = np.zeros((8, 1024), np.float32)
    for query_unit in range(4):
        lanes = slice(query_unit * UNIT, (query_unit + 1) * UNIT)
        level = unit_level(query_unit)
        table[0, lanes] = math.log2(min(3, level))
        table[1, lanes] = math.log2(min(2, level))
        if level >= 2:
            table[2, lanes] = math.log2(level - 1)
    table[3, 8:] = NEG
    return table


def dot_nt(left, right):
    return lax.dot_general(left, right, (((1,), (1,)), ((), ())), preferred_element_type=jnp.float32)


def dot_nn(left, right):
    return lax.dot_general(left, right, (((1,), (0,)), ((), ())), preferred_element_type=jnp.float32)


def dot_tn(left, right):
    return lax.dot_general(left, right, (((0,), (0,)), ((), ())), preferred_element_type=jnp.float32)


def call(kernel, outs, args, scratch=(), scalars=0, steps=(), in_steps=(), out_steps=(), in_place=None, vmem=24):
    def spec(shape, stepped, at_rest, scalar=False):
        if at_rest:
            return pl.BlockSpec(memory_space=pl.ANY)
        if scalar:
            return pl.BlockSpec(memory_space=pltpu.SMEM)
        if not steps:
            return pl.BlockSpec(memory_space=pltpu.VMEM)
        if stepped:
            return pl.BlockSpec((BLOCK, shape[1]), lambda at: (at, 0))
        return pl.BlockSpec(shape, lambda at: (0, 0))

    return pl.pallas_call(
        kernel,
        grid=steps,
        out_shape=[jax.ShapeDtypeStruct(shape, dtype) for shape, dtype in outs],
        in_specs=[spec(arg.shape, at in in_steps, at == in_place, at < scalars) for at, arg in enumerate(args)],
        out_specs=[
            spec(shape, at in out_steps, in_place is not None and at == 0) for at, (shape, _) in enumerate(outs)
        ],
        scratch_shapes=list(scratch),
        input_output_aliases={} if in_place is None else {in_place: 0},
        compiler_params=pltpu.CompilerParams(vmem_limit_bytes=vmem << 20),
        cost_estimate=pl.CostEstimate(flops=0, bytes_accessed=0, transcendentals=0),
    )(*args)


def sort_rows(source, target, lane, wide):
    wide[...] = source[...].astype(jnp.float32)
    for unit, residue in enumerate(ORDER):
        for pair in range(16):
            parts = [
                wide[pl.ds(8 * (2 * pair + half) + residue, 8, stride=256), :] for half in range(2)
            ]
            rows = slice(unit * UNIT + 16 * pair, unit * UNIT + 16 * pair + 16)
            target[rows, lane : lane + HEAD] = jnp.concatenate(parts, 0).astype(jnp.bfloat16)


def repeat_first(source, target, lane):
    first = source[:16, :].astype(jnp.float32)[:8]
    pair = jnp.concatenate([first, first], 0).astype(jnp.bfloat16)
    for at in range(0, target.shape[0], 16):
        target[at : at + 16, lane : lane + pair.shape[1]] = pair


def prepare_keys_kernel(k_ref, v_ref, q_ref, g_ref, kv_ref, s1_ref, s2_ref, s3_ref, far_ref, wide):
    sort_rows(k_ref, kv_ref, 0, wide)
    sort_rows(v_ref, kv_ref, HEAD, wide)
    s1_ref[:1024] = kv_ref[:1024]
    s2_ref[:512] = kv_ref[:512]
    s3_ref[...] = kv_ref[:256]
    repeat_first(kv_ref, far_ref, 0)
    for lane, ref in ((0, q_ref), (HEAD, g_ref)):
        rows = [ref[at : at + 16, :].astype(jnp.float32)[:1] for at in range(0, ROWS, 256)]
        block = jnp.concatenate(rows + rows, 0).astype(jnp.bfloat16)
        s1_ref[1024:, lane : lane + HEAD] = block
        s2_ref[512:, lane : lane + HEAD] = block


def prepare_queries_kernel(q_ref, g_ref, after_ref, qp_ref, gp_ref, wide):
    sort_rows(q_ref, qp_ref, 0, wide)
    sort_rows(g_ref, gp_ref, 0, wide)


def add_bias(block, rows):
    if all(row is None for row in rows):
        return block
    parts = []
    for at, row in enumerate(rows):
        part = block[at * UNIT : (at + 1) * UNIT]
        parts.append(part if row is None else part + row)
    return jnp.concatenate(parts, 0)


def longest(rows):
    wide = rows.astype(jnp.float32)
    squares = dot_nt(jnp.ones((8, HEAD), jnp.bfloat16), (wide * wide).astype(jnp.bfloat16))
    return 1.01 * jnp.max(squares)


def attend(query, keys, values, biases, small=False):
    scores = [add_bias(dot_nt(key, query) * SCALE2, bias) for key, bias in zip(keys, biases)]
    if small:
        peak = jnp.zeros((1, query.shape[0]), jnp.float32)
        probs = [jnp.exp2(block) for block in scores]
    else:
        peak = functools.reduce(jnp.maximum, [jnp.max(block, 0, keepdims=True) for block in scores])
        probs = [jnp.exp2(block - peak) for block in scores]
    total = sum([jnp.sum(block, 0, keepdims=True) for block in probs])
    out = sum([value(block.astype(jnp.bfloat16)) for value, block in zip(values, probs)])
    return peak, total, out


def finish_rows(row_ref, target, stat, out, grad):
    total = stat[1:2]
    row_ref[0:1, target] = stat[0:1] + jnp.log2(total)
    row_ref[1:2, target] = jnp.sum(grad.astype(jnp.float32).T * out, axis=0, keepdims=True) / total


def own_forward_kernel(q_ref, kv_ref, g_ref, bias_ref, stat_ref, out_ref, odd_ref, vt_ref):
    stat_ref[...] = jnp.zeros_like(stat_ref)
    odd_ref[...] = jnp.zeros_like(odd_ref)
    for unit in range(8):
        rows = slice(unit * UNIT, (unit + 1) * UNIT)
        vt_ref[:, rows] = kv_ref[rows, HEAD:].astype(jnp.float32).T.astype(jnp.bfloat16)
    def halves(small):
        for start in (0, HALF):
            lanes = slice(start, start + HALF)
            keys, values, biases = [], [], []
            for at in range(0, ROWS, BLOCK):
                rows = slice(at, at + BLOCK)
                keys.append(kv_ref[rows, :HEAD])
                values.append(lambda prob, rows=rows: dot_nn(vt_ref[:, rows], prob))
                unit = at // UNIT
                counted = start == 0 and at < HALF
                biases.append([bias_ref[unit + half : unit + half + 1, lanes] if counted else None for half in (0, 1)])
            peak, total, out = attend(q_ref[lanes, :], keys, values, biases, small)
            if start == 0:
                stat_ref[0:1, :] = peak
                stat_ref[1:2, :] = total
                out_ref[...] = out
            else:
                stat = jnp.concatenate([peak, total], 0)
                for first in range(0, HALF, UNIT):
                    part = slice(first, first + UNIT)
                    grad = g_ref[HALF + first : HALF + first + UNIT, :]
                    finish_rows(odd_ref, part, stat[:, part], out[:, part], grad)

    small = longest(q_ref[...]) * longest(kv_ref[:, :HEAD]) < (60.0 / SCALE2) ** 2
    pl.when(small)(functools.partial(halves, True))
    pl.when(jnp.logical_not(small))(functools.partial(halves, False))


def bias_rows(bias_ref, picks, count):
    return [None if pick is None else bias_ref[pick : pick + 1, :count] for pick in picks]


PARTNER, PARTNER_REST, SECOND, THIRD = (0, 1), (None, None), (2, None), (None, None)


def far_blocks(refs):
    third = (256, [(refs[-4:-2], THIRD), (refs[-2:], THIRD)])
    if len(refs) == 4:
        return (third,)
    near = (
        (1024, [((refs[0], 0), PARTNER), ((refs[0], BLOCK), PARTNER_REST)]),
        (512, [((ref, 0), SECOND) for ref in refs[1:3]]),
    )
    return near if len(refs) == 3 else (*near, third)


def read_block(place, lanes):
    ref, first = place
    if isinstance(first, int):
        return ref[first : first + BLOCK, lanes]
    return jnp.concatenate([ref[:, lanes], first[:, lanes]], 0)


def write_block(place, block):
    ref, first = place
    if isinstance(first, int):
        ref[first : first + BLOCK, :] = block
    else:
        ref[...] = block[:UNIT]
        first[...] = block[UNIT:]


def join_state(sums, acc, lanes, far_peak, far_total, far_out):
    peak = sums[0:1, lanes]
    top = jnp.maximum(peak, far_peak)
    near, far = jnp.exp2(peak - top), jnp.exp2(far_peak - top)
    sums[0:1, lanes] = top
    sums[1:2, lanes] = near * sums[1:2, lanes] + far * far_total
    acc[:, lanes] = near * acc[:, lanes] + far * far_out


def middle_forward_kernel(q_ref, bias_ref, stat_ref, out_ref, *rest):
    peers, (sums, acc) = rest[:7], rest[7:]
    sums[...] = stat_ref[...]
    acc[...] = out_ref[...]
    for count, blocks in far_blocks(peers):
        lanes = slice(0, count)
        state = attend(
            q_ref[lanes, :],
            [read_block(place, slice(0, HEAD)) for place, _ in blocks],
            [lambda prob, place=place: dot_tn(read_block(place, slice(HEAD, 256)), prob) for place, _ in blocks],
            [bias_rows(bias_ref, picks, count) for _, picks in blocks],
        )
        join_state(sums, acc, lanes, *state)


def whole_forward_kernel(me_ref, own, r1, r2, r3, far_ref, part_ref, quad_ref, rows_ref):
    for mask, ref in enumerate((own, r1, r2, r3)):
        count = ref.shape[0]
        place = pl.multiple_of((me_ref[0] ^ mask) * 8, 8)
        rows_ref[pl.ds(place, 8), :] = ref[count - 16 :, :].astype(jnp.float32)[:8]
    quad_ref[...] = rows_ref[...].astype(jnp.bfloat16)
    scores = dot_nt(quad_ref[:, :HEAD], far_ref[:, :HEAD]) * SCALE2
    peak = jnp.max(scores, 1, keepdims=True)
    prob = jnp.exp2(scores - peak)
    part_ref[:, :HEAD] = dot_nn(prob.astype(jnp.bfloat16), far_ref[:, HEAD:])
    part_ref[:, HEAD : 2 * HEAD] = jnp.broadcast_to(peak, (8 * QUADS, HEAD))
    part_ref[:, 2 * HEAD :] = jnp.broadcast_to(jnp.sum(prob, 1, keepdims=True), (8 * QUADS, HEAD))


def turn(block, fill):
    return jnp.concatenate([block, jnp.full((HEAD - 8, HEAD), fill, jnp.float32)], 0).T


def finish_kernel(g_ref, stat_ref, out_ref, odd_ref, part_ref, row_ref, tall_ref, sums, acc):
    lanes = slice(0, HEAD)
    sums[...] = stat_ref[:, lanes]
    acc[...] = out_ref[:, lanes]
    for at in range(0, 8 * QUADS, 8):
        part = part_ref[at : at + 8, :]
        far_out = turn(part[:, :HEAD], 0.0)
        far_peak = turn(part[:, HEAD : 2 * HEAD], NEG)[0:1]
        far_total = turn(part[:, 2 * HEAD :], 0.0)[0:1]
        join_state(sums, acc, lanes, far_peak, far_total, far_out)
    row_ref[...] = jnp.zeros_like(row_ref)
    row_ref[:, HALF:] = odd_ref[...]
    for first in range(0, HALF, HEAD):
        lanes = slice(first, first + HEAD)
        stat, out = (sums[...], acc[...]) if first == 0 else (stat_ref[:, lanes], out_ref[:, lanes])
        finish_rows(row_ref, lanes, stat, out, g_ref[lanes, :])
    tall = jnp.concatenate([row_ref[:, :HEAD], jnp.zeros((HEAD - 8, HEAD), jnp.float32)], 0).T
    for at in range(0, 8 * QUADS, 8):
        tall_ref[at : at + 8, :] = tall[:8]


def remote_backward_kernel(me_ref, q_ref, g_ref, bias_ref, row_ref, quad_ref, far_ref, tall_ref, *rest):
    third_dq, far, outs, (dkv_ref, dq_ref, mine_ref, quad_dq) = rest[0], rest[1:4], rest[4:7], rest[7:]
    query, grad = quad_ref[:, :HEAD], quad_ref[:, HEAD:]
    key, value = far_ref[:, :HEAD], far_ref[:, HEAD:]
    weights = jnp.exp2(dot_nt(query, key) * SCALE2 - tall_ref[:, 0:1])
    grad_scores = (weights * (dot_nt(grad, value) - tall_ref[:, 1:2])).astype(jnp.bfloat16)
    dkv_ref[:, :HEAD] = (SCALE * dot_tn(grad_scores, query)).astype(jnp.bfloat16)
    dkv_ref[:, HEAD:] = dot_tn(weights.astype(jnp.bfloat16), grad).astype(jnp.bfloat16)
    quad_dq[...] = dot_nn(grad_scores, key)
    for mask in range(QUADS):
        place = pl.multiple_of((me_ref[0] ^ mask) * 8, 8)
        block = quad_dq[pl.ds(place, 8), :]
        if mask == 0:
            mine_ref[...] = block
        else:
            block = jnp.concatenate([block, jnp.zeros_like(block)], 0)
            block = jnp.concatenate([block, jnp.zeros_like(block)], 1).astype(jnp.bfloat16)
            rows = outs[mask - 1].shape[0]
            outs[mask - 1][rows - 16 :, :] = block
    dq_ref[...] = jnp.zeros_like(dq_ref)
    dq_ref[:, :UNIT] = third_dq[...]
    backward_far(far, outs, (q_ref, g_ref, bias_ref, row_ref), dq_ref)


def third_backward_kernel(q_ref, g_ref, bias_ref, row_ref, *rest):
    far, outs, dq_ref = rest[:4], rest[4:8], rest[8]
    dq_ref[...] = jnp.zeros_like(dq_ref)
    backward_far(far, outs, (q_ref, g_ref, bias_ref, row_ref), dq_ref)


def backward_block(kv_block, q_ref, g_ref, row_ref, bias, count, dq_ref):
    key, value = kv_block[:, :HEAD], kv_block[:, HEAD:]
    lanes = slice(0, count)
    query, grad = q_ref[lanes, :], g_ref[lanes, :]
    scores = add_bias(dot_nt(key, query) * SCALE2, bias)
    weights = jnp.exp2(scores - row_ref[0:1, lanes])
    grad_probs = dot_nt(value, grad)
    grad_scores = (weights * (grad_probs - row_ref[1:2, lanes])).astype(jnp.bfloat16)
    grad_value = dot_nn(weights.astype(jnp.bfloat16), grad)
    grad_key = dot_nn(grad_scores, query)
    dq_ref[:, lanes] += dot_tn(key, grad_scores)
    return SCALE * grad_key, grad_value


def backward_far(far, outs, refs, dq_ref):
    q_ref, g_ref, bias_ref, row_ref = refs
    for (count, blocks), (_, places) in zip(far_blocks(far), far_blocks(outs)):
        for (place, picks), (target, _) in zip(blocks, places):
            bias = bias_rows(bias_ref, picks, count)
            both = backward_block(read_block(place, slice(0, 256)), q_ref, g_ref, row_ref, bias, count, dq_ref)
            write_block(target, jnp.concatenate(both, 1).astype(jnp.bfloat16))


def own_backward_kernel(q_ref, g_ref, bias_ref, row_ref, kv_ref, far_ref, dq_ref, dkv_ref, acc_ref, tall_ref):
    at = pl.program_id(0)

    @pl.when(at == 0)
    def _():
        acc_ref[:, :HALF] = far_ref[...]
        acc_ref[:, HALF:] = jnp.zeros((HEAD, HALF), jnp.float32)

    bias = [bias_ref[pl.ds(2 * at + half, 1), :] for half in (0, 1)]
    grad_key, grad_value = backward_block(kv_ref[...], q_ref, g_ref, row_ref, bias, ROWS, acc_ref)
    dkv_ref[:, :HEAD] = grad_key
    dkv_ref[:, HEAD:] = grad_value

    @pl.when(at == ROWS // BLOCK - 1)
    def _():
        for unit in range(8):
            lanes = slice(unit * UNIT, (unit + 1) * UNIT)
            tall_ref[lanes, :] = acc_ref[:, lanes].T * SCALE
        restore_rows(lambda rows: tall_ref[rows, :], dq_ref)


def restore_rows(read, target):
    for unit, residue in enumerate(ORDER):
        for block in range(32):
            start = unit * UNIT + 8 * block
            target[pl.ds(8 * block + residue, 8, stride=256), :] = read(slice(start, start + 8))


def join_kernel(dkv_ref, mine_ref, b1, b2, b3, b4, b5, b6, b7, far_ref, dq_in, dq_out, dk_ref, dv_ref, sum_ref, tiles, sem):
    def wide(ref, rows=slice(None)):
        return ref[rows, :].astype(jnp.float32)

    places = [(pl.ds(256 * at, 8), pl.ds(8 * at, 8)) for at in range(8)]
    reads = [pltpu.make_async_copy(dq_in.at[rows], tiles.at[spot], sem.at[at]) for at, (rows, spot) in enumerate(places)]
    for copy in reads:
        copy.start()
    mine = mine_ref[...]
    for ref in (b1, b2, b3):
        mine = mine + ref[ref.shape[0] - 16 :, :HEAD].astype(jnp.float32)[:8]
    mine = SCALE * mine
    for copy in reads:
        copy.wait()
    for at in range(8):
        tiles[8 * at : 8 * at + 1, :] += mine[at : at + 1, :]
    writes = [pltpu.make_async_copy(tiles.at[spot], dq_out.at[rows], sem.at[8 + at]) for at, (rows, spot) in enumerate(places)]
    for copy in writes:
        copy.start()
    top, mid, low = slice(0, 256), slice(256, 512), slice(512, 1024)
    near = wide(b1, top) + wide(b2, top) + wide(b3, top)
    sum_ref[top, :] = dkv_ref[top, :] + near + wide(b4) + wide(b5) + wide(b6) + wide(b7)
    sum_ref[mid, :] = dkv_ref[mid, :] + wide(b1, mid) + wide(b2, mid) + wide(b3, mid)
    sum_ref[low, :] = dkv_ref[low, :] + wide(b1, low)
    sum_ref[1024:, :] = dkv_ref[1024:, :]
    sum_ref[:8, :] += jnp.sum(wide(far_ref).reshape(FAR, 8, 256), 0)
    restore_rows(lambda rows: sum_ref[rows, :HEAD], dk_ref)
    restore_rows(lambda rows: sum_ref[rows, HEAD:], dv_ref)
    for copy in writes:
        copy.wait()


def swap(block, mask):
    return lax.ppermute(block, ("z", "y"), [(at, at ^ mask) for at in range(16)])


def swap_all(sends):
    near = [swap(block, mask) for block, mask in zip(sends[:5], (1, 2, 3, 4, 5))]
    last = []
    for at, (block, mask) in enumerate(zip(sends[5:], (6, 7))):
        near[3 + at], block = lax.optimization_barrier((near[3 + at], block))
        last.append(swap(block, mask))
    return near + last


def swap_quad(block):
    parts = block.reshape(QUADS, 8, block.shape[1])
    return lax.all_to_all(parts, "y", 0, 0).reshape(block.shape)


def swap_far(block):
    parts = block.reshape(FAR, 8, block.shape[1])
    return lax.all_to_all(parts, ("grp", "x", "z"), 0, 0).reshape(block.shape)


def on_device(queries, keys, values, cotangent):
    f32, bf16 = jnp.float32, jnp.bfloat16
    near_bias, other_bias = jnp.asarray(own_bias()), jnp.asarray(far_bias())

    def both(*rows):
        return [((count, 256), bf16) for count in rows]

    wide = [pltpu.VMEM((ROWS, HEAD), f32)]
    kv, s1, s2, s3, far = call(
        prepare_keys_kernel, both(ROWS, 1040, 528, 256, 8 * FAR), (keys, values, queries, cotangent), wide
    )
    peers = swap_all([s1, s2, s2, s3, s3, s3, s3])
    q, g = call(prepare_queries_kernel, [((ROWS, HEAD), bf16)] * 2, (queries, cotangent, s3), wide)
    q, far, peers[3], peers[4] = lax.optimization_barrier((q, far, peers[3], peers[4]))
    far = swap_far(far)
    state = [((8, HALF), f32), ((HEAD, HALF), f32)]
    stat, out, odd = call(
        own_forward_kernel, [*state, ((8, HALF), f32)], (q, kv, g, near_bias), [pltpu.VMEM((HEAD, ROWS), bf16)], vmem=60
    )
    stat, far = lax.optimization_barrier((stat, far))
    me = lax.axis_index("y").astype(jnp.int32).reshape(1)
    part, quad = call(
        whole_forward_kernel,
        [((8 * QUADS, 3 * HEAD), f32), *both(8 * QUADS)],
        (me, s2, *peers[:3], far),
        [pltpu.VMEM((8 * QUADS, 256), f32)],
        scalars=1,
    )
    part = swap_quad(part)
    stat, out = call(middle_forward_kernel, state, (q, other_bias, stat, out, *peers))
    row, tall = call(
        finish_kernel,
        [((8, ROWS), f32), ((8 * QUADS, HEAD), f32)],
        (g, stat, out, odd, part),
        [pltpu.VMEM((8, HEAD), f32), pltpu.VMEM((HEAD, HEAD), f32)],
    )
    tall = swap_quad(tall)
    *third, third_dq = call(
        third_backward_kernel,
        [*both(256, 256, 256, 256), ((HEAD, UNIT), f32)],
        (q, g, other_bias, row, *peers[3:]),
    )
    back = [swap(block, mask) for block, mask in zip(third, (4, 5, 6, 7))]
    third_dq, tall = lax.optimization_barrier((third_dq, tall))
    *sends, far_dkv, far_dq, mine = call(
        remote_backward_kernel,
        [*both(1040, 528, 528, 8 * FAR), ((HEAD, HALF), f32), ((8, HEAD), f32)],
        (me, q, g, other_bias, row, quad, far, tall, third_dq, *peers[:3]),
        [pltpu.VMEM((8 * QUADS, HEAD), f32)],
        scalars=1,
    )
    far_dkv, *back = lax.optimization_barrier((far_dkv, *back))
    back = [swap(block, mask) for block, mask in zip(sends, (1, 2, 3))] + back
    far_dkv = swap_far(far_dkv)
    dq, dkv = call(
        own_backward_kernel,
        [((ROWS, HEAD), f32), ((ROWS, 256), f32)],
        (q, g, near_bias, row, kv, far_dq),
        [pltpu.VMEM((HEAD, ROWS), f32), pltpu.VMEM((ROWS, HEAD), f32)],
        steps=(ROWS // BLOCK,),
        in_steps=(4,),
        out_steps=(1,),
        vmem=60,
    )
    dq, dk, dv = call(
        join_kernel,
        [((ROWS, HEAD), f32)] * 3,
        (dkv, mine, *back, far_dkv, dq),
        [pltpu.VMEM((ROWS, 256), f32), pltpu.VMEM((64, HEAD), f32), pltpu.SemaphoreType.DMA((16,))],
        in_place=10,
    )
    return dq, dk, dv


def solution(mesh):
    axes = ("grp", "x", "z", "y")
    split = jax.sharding.Mesh(mesh.devices.reshape(4, 4, 4, 4), axes)
    spec = P(axes, None)
    return jax.shard_map(
        on_device, mesh=split, in_specs=(spec,) * 4, out_specs=(spec,) * 3, check_vma=False
    )
```

```python
import functools
import math

import jax
import jax.numpy as jnp
import numpy as np
from jax import lax
from jax.experimental import pallas as pl
from jax.experimental.pallas import tpu as pltpu
from jax.sharding import PartitionSpec as P

ROWS = 2048
HEAD = 128
UNIT = 256
ORDER = (0, 4, 2, 6, 1, 3, 5, 7)
SCALE = HEAD**-0.5
SCALE2 = SCALE * math.log2(math.e)
NEG = -1e30
QUADS = 4
FAR = 64
BLOCK = 512
HALF = 1024


def unit_level(unit):
    return 3 if unit == 0 else 2 if unit == 1 else 1 if unit < 4 else 0


def own_bias():
    table = np.zeros((8, ROWS), np.float32)
    for key_unit in range(8):
        for query_unit in range(8):
            shared = 1 + min(unit_level(key_unit), unit_level(query_unit))
            table[key_unit, query_unit * UNIT : (query_unit + 1) * UNIT] = math.log2(shared)
    return table


def far_bias():
    table = np.zeros((8, 1024), np.float32)
    for query_unit in range(4):
        lanes = slice(query_unit * UNIT, (query_unit + 1) * UNIT)
        level = unit_level(query_unit)
        table[0, lanes] = math.log2(min(3, level))
        table[1, lanes] = math.log2(min(2, level))
        if level >= 2:
            table[2, lanes] = math.log2(level - 1)
    table[3, 8:] = NEG
    return table


def dot_nt(left, right):
    return lax.dot_general(left, right, (((1,), (1,)), ((), ())), preferred_element_type=jnp.float32)


def dot_nn(left, right):
    return lax.dot_general(left, right, (((1,), (0,)), ((), ())), preferred_element_type=jnp.float32)


def dot_tn(left, right):
    return lax.dot_general(left, right, (((0,), (0,)), ((), ())), preferred_element_type=jnp.float32)


def call(kernel, outs, args, scratch=(), scalars=0, steps=(), in_steps=(), out_steps=(), in_place=None, vmem=24):
    def spec(shape, stepped, at_rest, scalar=False):
        if at_rest:
            return pl.BlockSpec(memory_space=pl.ANY)
        if scalar:
            return pl.BlockSpec(memory_space=pltpu.SMEM)
        if not steps:
            return pl.BlockSpec(memory_space=pltpu.VMEM)
        if stepped:
            return pl.BlockSpec((BLOCK, shape[1]), lambda at: (at, 0))
        return pl.BlockSpec(shape, lambda at: (0, 0))

    return pl.pallas_call(
        kernel,
        grid=steps,
        out_shape=[jax.ShapeDtypeStruct(shape, dtype) for shape, dtype in outs],
        in_specs=[spec(arg.shape, at in in_steps, at == in_place, at < scalars) for at, arg in enumerate(args)],
        out_specs=[
            spec(shape, at in out_steps, in_place is not None and at == 0) for at, (shape, _) in enumerate(outs)
        ],
        scratch_shapes=list(scratch),
        input_output_aliases={} if in_place is None else {in_place: 0},
        compiler_params=pltpu.CompilerParams(vmem_limit_bytes=vmem << 20),
        cost_estimate=pl.CostEstimate(flops=0, bytes_accessed=0, transcendentals=0),
    )(*args)


def sort_rows(source, target, lane, wide):
    wide[...] = source[...].astype(jnp.float32)
    for unit, residue in enumerate(ORDER):
        for pair in range(16):
            parts = [
                wide[pl.ds(8 * (2 * pair + half) + residue, 8, stride=256), :] for half in range(2)
            ]
            rows = slice(unit * UNIT + 16 * pair, unit * UNIT + 16 * pair + 16)
            target[rows, lane : lane + HEAD] = jnp.concatenate(parts, 0).astype(jnp.bfloat16)


def repeat_first(source, target, lane):
    first = source[:16, :].astype(jnp.float32)[:8]
    pair = jnp.concatenate([first, first], 0).astype(jnp.bfloat16)
    for at in range(0, target.shape[0], 16):
        target[at : at + 16, lane : lane + pair.shape[1]] = pair


def prepare_keys_kernel(k_ref, v_ref, q_ref, g_ref, kv_ref, s1_ref, s2_ref, s3_ref, far_ref, wide):
    sort_rows(k_ref, kv_ref, 0, wide)
    sort_rows(v_ref, kv_ref, HEAD, wide)
    s1_ref[:1024] = kv_ref[:1024]
    s2_ref[:512] = kv_ref[:512]
    s3_ref[...] = kv_ref[:256]
    repeat_first(kv_ref, far_ref, 0)
    for lane, ref in ((0, q_ref), (HEAD, g_ref)):
        rows = [ref[at : at + 16, :].astype(jnp.float32)[:1] for at in range(0, ROWS, 256)]
        block = jnp.concatenate(rows + rows, 0).astype(jnp.bfloat16)
        s1_ref[1024:, lane : lane + HEAD] = block
        s2_ref[512:, lane : lane + HEAD] = block


def prepare_queries_kernel(q_ref, g_ref, after_ref, qp_ref, gp_ref, wide):
    sort_rows(q_ref, qp_ref, 0, wide)
    sort_rows(g_ref, gp_ref, 0, wide)


def add_bias(block, rows):
    if all(row is None for row in rows):
        return block
    parts = []
    for at, row in enumerate(rows):
        part = block[at * UNIT : (at + 1) * UNIT]
        parts.append(part if row is None else part + row)
    return jnp.concatenate(parts, 0)


def longest(rows):
    wide = rows.astype(jnp.float32)
    squares = dot_nt(jnp.ones((8, HEAD), jnp.bfloat16), (wide * wide).astype(jnp.bfloat16))
    return 1.01 * jnp.max(squares)


def attend(query, keys, values, biases, small=False):
    scores = [add_bias(dot_nt(key, query) * SCALE2, bias) for key, bias in zip(keys, biases)]
    if small:
        peak = jnp.zeros((1, query.shape[0]), jnp.float32)
        probs = [jnp.exp2(block) for block in scores]
    else:
        peak = functools.reduce(jnp.maximum, [jnp.max(block, 0, keepdims=True) for block in scores])
        probs = [jnp.exp2(block - peak) for block in scores]
    total = sum([jnp.sum(block, 0, keepdims=True) for block in probs])
    out = sum([value(block.astype(jnp.bfloat16)) for value, block in zip(values, probs)])
    return peak, total, out


def finish_rows(row_ref, target, stat, out, grad):
    total = stat[1:2]
    row_ref[0:1, target] = stat[0:1] + jnp.log2(total)
    row_ref[1:2, target] = jnp.sum(grad.astype(jnp.float32).T * out, axis=0, keepdims=True) / total


def own_forward_kernel(q_ref, kv_ref, g_ref, bias_ref, stat_ref, out_ref, odd_ref, vt_ref):
    stat_ref[...] = jnp.zeros_like(stat_ref)
    odd_ref[...] = jnp.zeros_like(odd_ref)
    for unit in range(8):
        rows = slice(unit * UNIT, (unit + 1) * UNIT)
        vt_ref[:, rows] = kv_ref[rows, HEAD:].astype(jnp.float32).T.astype(jnp.bfloat16)
    def halves(small):
        for start in (0, HALF):
            lanes = slice(start, start + HALF)
            keys, values, biases = [], [], []
            for at in range(0, ROWS, BLOCK):
                rows = slice(at, at + BLOCK)
                keys.append(kv_ref[rows, :HEAD])
                values.append(lambda prob, rows=rows: dot_nn(vt_ref[:, rows], prob))
                unit = at // UNIT
                counted = start == 0 and at < HALF
                biases.append([bias_ref[unit + half : unit + half + 1, lanes] if counted else None for half in (0, 1)])
            peak, total, out = attend(q_ref[lanes, :], keys, values, biases, small)
            if start == 0:
                stat_ref[0:1, :] = peak
                stat_ref[1:2, :] = total
                out_ref[...] = out
            else:
                stat = jnp.concatenate([peak, total], 0)
                for first in range(0, HALF, UNIT):
                    part = slice(first, first + UNIT)
                    grad = g_ref[HALF + first : HALF + first + UNIT, :]
                    finish_rows(odd_ref, part, stat[:, part], out[:, part], grad)

    small = longest(q_ref[...]) * longest(kv_ref[:, :HEAD]) < (60.0 / SCALE2) ** 2
    pl.when(small)(functools.partial(halves, True))
    pl.when(jnp.logical_not(small))(functools.partial(halves, False))


def bias_rows(bias_ref, picks, count):
    return [None if pick is None else bias_ref[pick : pick + 1, :count] for pick in picks]


PARTNER, PARTNER_REST, SECOND, THIRD = (0, 1), (None, None), (2, None), (None, None)


def far_blocks(refs):
    third = (256, [(refs[-4:-2], THIRD), (refs[-2:], THIRD)])
    if len(refs) == 4:
        return (third,)
    near = (
        (1024, [((refs[0], 0), PARTNER), ((refs[0], BLOCK), PARTNER_REST)]),
        (512, [((ref, 0), SECOND) for ref in refs[1:3]]),
    )
    return near if len(refs) == 3 else (*near, third)


def read_block(place, lanes):
    ref, first = place
    if isinstance(first, int):
        return ref[first : first + BLOCK, lanes]
    return jnp.concatenate([ref[:, lanes], first[:, lanes]], 0)


def write_block(place, block):
    ref, first = place
    if isinstance(first, int):
        ref[first : first + BLOCK, :] = block
    else:
        ref[...] = block[:UNIT]
        first[...] = block[UNIT:]


def join_state(sums, acc, lanes, far_peak, far_total, far_out):
    peak = sums[0:1, lanes]
    top = jnp.maximum(peak, far_peak)
    near, far = jnp.exp2(peak - top), jnp.exp2(far_peak - top)
    sums[0:1, lanes] = top
    sums[1:2, lanes] = near * sums[1:2, lanes] + far * far_total
    acc[:, lanes] = near * acc[:, lanes] + far * far_out


def middle_forward_kernel(q_ref, bias_ref, stat_ref, out_ref, *rest):
    peers, (sums, acc) = rest[:7], rest[7:]
    sums[...] = stat_ref[...]
    acc[...] = out_ref[...]
    for count, blocks in far_blocks(peers):
        lanes = slice(0, count)
        state = attend(
            q_ref[lanes, :],
            [read_block(place, slice(0, HEAD)) for place, _ in blocks],
            [lambda prob, place=place: dot_tn(read_block(place, slice(HEAD, 256)), prob) for place, _ in blocks],
            [bias_rows(bias_ref, picks, count) for _, picks in blocks],
        )
        join_state(sums, acc, lanes, *state)


def whole_forward_kernel(me_ref, own, r1, r2, r3, far_ref, part_ref, quad_ref, rows_ref):
    for mask, ref in enumerate((own, r1, r2, r3)):
        count = ref.shape[0]
        place = pl.multiple_of((me_ref[0] ^ mask) * 8, 8)
        rows_ref[pl.ds(place, 8), :] = ref[count - 16 :, :].astype(jnp.float32)[:8]
    quad_ref[...] = rows_ref[...].astype(jnp.bfloat16)
    scores = dot_nt(quad_ref[:, :HEAD], far_ref[:, :HEAD]) * SCALE2
    peak = jnp.max(scores, 1, keepdims=True)
    prob = jnp.exp2(scores - peak)
    part_ref[:, :HEAD] = dot_nn(prob.astype(jnp.bfloat16), far_ref[:, HEAD:])
    part_ref[:, HEAD : 2 * HEAD] = jnp.broadcast_to(peak, (8 * QUADS, HEAD))
    part_ref[:, 2 * HEAD :] = jnp.broadcast_to(jnp.sum(prob, 1, keepdims=True), (8 * QUADS, HEAD))


def turn(block, fill):
    return jnp.concatenate([block, jnp.full((HEAD - 8, HEAD), fill, jnp.float32)], 0).T


def finish_kernel(g_ref, stat_ref, out_ref, odd_ref, part_ref, row_ref, tall_ref, sums, acc):
    lanes = slice(0, HEAD)
    sums[...] = stat_ref[:, lanes]
    acc[...] = out_ref[:, lanes]
    for at in range(0, 8 * QUADS, 8):
        part = part_ref[at : at + 8, :]
        far_out = turn(part[:, :HEAD], 0.0)
        far_peak = turn(part[:, HEAD : 2 * HEAD], NEG)[0:1]
        far_total = turn(part[:, 2 * HEAD :], 0.0)[0:1]
        join_state(sums, acc, lanes, far_peak, far_total, far_out)
    row_ref[...] = jnp.zeros_like(row_ref)
    row_ref[:, HALF:] = odd_ref[...]
    for first in range(0, HALF, HEAD):
        lanes = slice(first, first + HEAD)
        stat, out = (sums[...], acc[...]) if first == 0 else (stat_ref[:, lanes], out_ref[:, lanes])
        finish_rows(row_ref, lanes, stat, out, g_ref[lanes, :])
    tall = jnp.concatenate([row_ref[:, :HEAD], jnp.zeros((HEAD - 8, HEAD), jnp.float32)], 0).T
    for at in range(0, 8 * QUADS, 8):
        tall_ref[at : at + 8, :] = tall[:8]


def remote_backward_kernel(me_ref, q_ref, g_ref, bias_ref, row_ref, quad_ref, far_ref, tall_ref, *rest):
    third_dq, far, outs, (dkv_ref, dq_ref, mine_ref, quad_dq) = rest[0], rest[1:4], rest[4:7], rest[7:]
    query, grad = quad_ref[:, :HEAD], quad_ref[:, HEAD:]
    key, value = far_ref[:, :HEAD], far_ref[:, HEAD:]
    weights = jnp.exp2(dot_nt(query, key) * SCALE2 - tall_ref[:, 0:1])
    grad_scores = (weights * (dot_nt(grad, value) - tall_ref[:, 1:2])).astype(jnp.bfloat16)
    dkv_ref[:, :HEAD] = (SCALE * dot_tn(grad_scores, query)).astype(jnp.bfloat16)
    dkv_ref[:, HEAD:] = dot_tn(weights.astype(jnp.bfloat16), grad).astype(jnp.bfloat16)
    quad_dq[...] = dot_nn(grad_scores, key)
    for mask in range(QUADS):
        place = pl.multiple_of((me_ref[0] ^ mask) * 8, 8)
        block = quad_dq[pl.ds(place, 8), :]
        if mask == 0:
            mine_ref[...] = block
        else:
            block = jnp.concatenate([block, jnp.zeros_like(block)], 0)
            block = jnp.concatenate([block, jnp.zeros_like(block)], 1).astype(jnp.bfloat16)
            rows = outs[mask - 1].shape[0]
            outs[mask - 1][rows - 16 :, :] = block
    dq_ref[...] = jnp.zeros_like(dq_ref)
    dq_ref[:, :UNIT] = third_dq[...]
    backward_far(far, outs, (q_ref, g_ref, bias_ref, row_ref), dq_ref)


def third_backward_kernel(q_ref, g_ref, bias_ref, row_ref, *rest):
    far, outs, dq_ref = rest[:4], rest[4:8], rest[8]
    dq_ref[...] = jnp.zeros_like(dq_ref)
    backward_far(far, outs, (q_ref, g_ref, bias_ref, row_ref), dq_ref)


def backward_block(kv_block, q_ref, g_ref, row_ref, bias, count, dq_ref):
    key, value = kv_block[:, :HEAD], kv_block[:, HEAD:]
    lanes = slice(0, count)
    query, grad = q_ref[lanes, :], g_ref[lanes, :]
    scores = add_bias(dot_nt(key, query) * SCALE2, bias)
    weights = jnp.exp2(scores - row_ref[0:1, lanes])
    grad_probs = dot_nt(value, grad)
    grad_scores = (weights * (grad_probs - row_ref[1:2, lanes])).astype(jnp.bfloat16)
    grad_value = dot_nn(weights.astype(jnp.bfloat16), grad)
    grad_key = dot_nn(grad_scores, query)
    dq_ref[:, lanes] += dot_tn(key, grad_scores)
    return SCALE * grad_key, grad_value


def backward_far(far, outs, refs, dq_ref):
    q_ref, g_ref, bias_ref, row_ref = refs
    for (count, blocks), (_, places) in zip(far_blocks(far), far_blocks(outs)):
        for (place, picks), (target, _) in zip(blocks, places):
            bias = bias_rows(bias_ref, picks, count)
            both = backward_block(read_block(place, slice(0, 256)), q_ref, g_ref, row_ref, bias, count, dq_ref)
            write_block(target, jnp.concatenate(both, 1).astype(jnp.bfloat16))


def half_backward(lanes, q_ref, g_ref, bias_ref, row_ref, kv_ref, acc_ref):
    at = pl.program_id(0)
    bias = (None, None)
    if bias_ref is not None:
        bias = [bias_ref[pl.ds(2 * at + half, 1), lanes] for half in (0, 1)]
    refs = [ref.at[lanes] for ref in (q_ref, g_ref)]
    return backward_block(kv_ref[...], *refs, row_ref, bias, HALF, acc_ref)


def restore_half(acc_ref, tall_ref, dq_ref, units):
    for unit in units:
        first = (unit % 4) * UNIT
        tall_ref[first : first + UNIT, :] = acc_ref[:, first : first + UNIT].T * SCALE
        for block in range(32):
            start = first + 8 * block
            dq_ref[pl.ds(8 * block + ORDER[unit], 8, stride=256), :] = tall_ref[start : start + 8, :]


def odd_backward_kernel(q_ref, g_ref, row_ref, kv_ref, dkv_ref, dq_ref, acc_ref):
    at = pl.program_id(0)

    @pl.when(at == 0)
    def _():
        acc_ref[...] = jnp.zeros_like(acc_ref)

    both = half_backward(slice(HALF, ROWS), q_ref, g_ref, None, row_ref, kv_ref, acc_ref)
    dkv_ref[:, :HEAD], dkv_ref[:, HEAD:] = both

    @pl.when(at == ROWS // BLOCK - 1)
    def _():
        dq_ref[...] = acc_ref[...]


def even_backward_kernel(q_ref, g_ref, bias_ref, row_ref, kv_ref, far_ref, odd_ref, dkv_odd, dq_ref, dkv_ref, acc_ref, tall_ref):
    at = pl.program_id(0)

    @pl.when(at == 0)
    def _():
        restore_half(odd_ref, tall_ref, dq_ref, range(4, 8))
        acc_ref[...] = far_ref[...]

    both = half_backward(slice(0, HALF), q_ref, g_ref, bias_ref, row_ref, kv_ref, acc_ref)
    dkv_ref[:, :HEAD] = dkv_odd[:, :HEAD] + both[0]
    dkv_ref[:, HEAD:] = dkv_odd[:, HEAD:] + both[1]

    @pl.when(at == ROWS // BLOCK - 1)
    def _():
        restore_half(acc_ref, tall_ref, dq_ref, range(4))


def restore_rows(read, target):
    for unit, residue in enumerate(ORDER):
        for block in range(32):
            start = unit * UNIT + 8 * block
            target[pl.ds(8 * block + residue, 8, stride=256), :] = read(slice(start, start + 8))


def join_kernel(dkv_ref, mine_ref, b1, b2, b3, b4, b5, b6, b7, far_ref, dq_in, dq_out, dk_ref, dv_ref, sum_ref, tiles, sem):
    def wide(ref, rows=slice(None)):
        return ref[rows, :].astype(jnp.float32)

    places = [(pl.ds(256 * at, 8), pl.ds(8 * at, 8)) for at in range(8)]
    reads = [pltpu.make_async_copy(dq_in.at[rows], tiles.at[spot], sem.at[at]) for at, (rows, spot) in enumerate(places)]
    for copy in reads:
        copy.start()
    mine = mine_ref[...]
    for ref in (b1, b2, b3):
        mine = mine + ref[ref.shape[0] - 16 :, :HEAD].astype(jnp.float32)[:8]
    mine = SCALE * mine
    for copy in reads:
        copy.wait()
    for at in range(8):
        tiles[8 * at : 8 * at + 1, :] += mine[at : at + 1, :]
    writes = [pltpu.make_async_copy(tiles.at[spot], dq_out.at[rows], sem.at[8 + at]) for at, (rows, spot) in enumerate(places)]
    for copy in writes:
        copy.start()
    top, mid, low = slice(0, 256), slice(256, 512), slice(512, 1024)
    near = wide(b1, top) + wide(b2, top) + wide(b3, top)
    sum_ref[top, :] = dkv_ref[top, :] + near + wide(b4) + wide(b5) + wide(b6) + wide(b7)
    sum_ref[mid, :] = dkv_ref[mid, :] + wide(b1, mid) + wide(b2, mid) + wide(b3, mid)
    sum_ref[low, :] = dkv_ref[low, :] + wide(b1, low)
    sum_ref[1024:, :] = dkv_ref[1024:, :]
    sum_ref[:8, :] += jnp.sum(wide(far_ref).reshape(FAR, 8, 256), 0)
    restore_rows(lambda rows: sum_ref[rows, :HEAD], dk_ref)
    restore_rows(lambda rows: sum_ref[rows, HEAD:], dv_ref)
    for copy in writes:
        copy.wait()


def swap(block, mask):
    return lax.ppermute(block, ("z", "y"), [(at, at ^ mask) for at in range(16)])


def swap_all(sends):
    near = [swap(block, mask) for block, mask in zip(sends[:5], (1, 2, 3, 4, 5))]
    last = []
    for at, (block, mask) in enumerate(zip(sends[5:], (6, 7))):
        near[3 + at], block = lax.optimization_barrier((near[3 + at], block))
        last.append(swap(block, mask))
    return near + last


def swap_quad(block):
    parts = block.reshape(QUADS, 8, block.shape[1])
    return lax.all_to_all(parts, "y", 0, 0).reshape(block.shape)


def swap_far(block):
    parts = block.reshape(FAR, 8, block.shape[1])
    return lax.all_to_all(parts, ("grp", "x", "z"), 0, 0).reshape(block.shape)


def on_device(queries, keys, values, cotangent):
    f32, bf16 = jnp.float32, jnp.bfloat16
    near_bias, other_bias = jnp.asarray(own_bias()), jnp.asarray(far_bias())

    def both(*rows):
        return [((count, 256), bf16) for count in rows]

    wide = [pltpu.VMEM((ROWS, HEAD), f32)]
    kv, s1, s2, s3, far = call(
        prepare_keys_kernel, both(ROWS, 1040, 528, 256, 8 * FAR), (keys, values, queries, cotangent), wide, vmem=60
    )
    peers = swap_all([s1, s2, s2, s3, s3, s3, s3])
    q, g = call(prepare_queries_kernel, [((ROWS, HEAD), bf16)] * 2, (queries, cotangent, s3), wide)
    state = [((8, HALF), f32), ((HEAD, HALF), f32)]
    stat, out, odd = call(
        own_forward_kernel, [*state, ((8, HALF), f32)], (q, kv, g, near_bias), [pltpu.VMEM((HEAD, ROWS), bf16)], vmem=60
    )
    odd_dkv, odd_dq = call(
        odd_backward_kernel,
        [((ROWS, 256), f32), ((HEAD, HALF), f32)],
        (q, g, odd, kv),
        [pltpu.VMEM((HEAD, HALF), f32)],
        steps=(ROWS // BLOCK,),
        in_steps=(3,),
        out_steps=(0,),
        vmem=60,
    )
    far, odd_dq, *peers[1:5] = lax.optimization_barrier((far, odd_dq, *peers[1:5]))
    far = swap_far(far)
    me = lax.axis_index("y").astype(jnp.int32).reshape(1)
    part, quad = call(
        whole_forward_kernel,
        [((8 * QUADS, 3 * HEAD), f32), *both(8 * QUADS)],
        (me, s2, *peers[:3], far),
        [pltpu.VMEM((8 * QUADS, 256), f32)],
        scalars=1,
    )
    part = swap_quad(part)
    stat, out = call(middle_forward_kernel, state, (q, other_bias, stat, out, *peers))
    row, tall = call(
        finish_kernel,
        [((8, ROWS), f32), ((8 * QUADS, HEAD), f32)],
        (g, stat, out, odd, part),
        [pltpu.VMEM((8, HEAD), f32), pltpu.VMEM((HEAD, HEAD), f32)],
    )
    tall = swap_quad(tall)
    *third, third_dq = call(
        third_backward_kernel,
        [*both(256, 256, 256, 256), ((HEAD, UNIT), f32)],
        (q, g, other_bias, row, *peers[3:]),
    )
    back = [swap(block, mask) for block, mask in zip(third, (4, 5, 6, 7))]
    third_dq, tall = lax.optimization_barrier((third_dq, tall))
    *sends, far_dkv, far_dq, mine = call(
        remote_backward_kernel,
        [*both(1040, 528, 528, 8 * FAR), ((HEAD, HALF), f32), ((8, HEAD), f32)],
        (me, q, g, other_bias, row, quad, far, tall, third_dq, *peers[:3]),
        [pltpu.VMEM((8 * QUADS, HEAD), f32)],
        scalars=1,
    )
    far_dkv, *back = lax.optimization_barrier((far_dkv, *back))
    back = [swap(block, mask) for block, mask in zip(sends, (1, 2, 3))] + back
    far_dkv = swap_far(far_dkv)
    dq, dkv = call(
        even_backward_kernel,
        [((ROWS, HEAD), f32), ((ROWS, 256), f32)],
        (q, g, near_bias, row, kv, far_dq, odd_dq, odd_dkv),
        [pltpu.VMEM((HEAD, HALF), f32), pltpu.VMEM((HALF, HEAD), f32)],
        steps=(ROWS // BLOCK,),
        in_steps=(4, 7),
        out_steps=(1,),
        vmem=60,
    )
    dq, dk, dv = call(
        join_kernel,
        [((ROWS, HEAD), f32)] * 3,
        (dkv, mine, *back, far_dkv, dq),
        [pltpu.VMEM((ROWS, 256), f32), pltpu.VMEM((64, HEAD), f32), pltpu.SemaphoreType.DMA((16,))],
        in_place=10,
    )
    return dq, dk, dv


def solution(mesh):
    axes = ("grp", "x", "z", "y")
    split = jax.sharding.Mesh(mesh.devices.reshape(4, 4, 4, 4), axes)
    spec = P(axes, None)
    return jax.shard_map(
        on_device, mesh=split, in_specs=(spec,) * 4, out_specs=(spec,) * 3, check_vma=False
    )
```

```python
import functools
import math

import jax
import jax.numpy as jnp
import numpy as np
from jax import lax
from jax.experimental import pallas as pl
from jax.experimental.pallas import tpu as pltpu
from jax.sharding import PartitionSpec as P

ROWS = 2048
HEAD = 128
UNIT = 256
ORDER = (0, 4, 2, 6, 1, 3, 5, 7)
SCALE = HEAD**-0.5
SCALE2 = SCALE * math.log2(math.e)
NEG = -1e30
QUADS = 4
FAR = 64
BLOCK = 512
HALF = 1024


def unit_level(unit):
    return 3 if unit == 0 else 2 if unit == 1 else 1 if unit < 4 else 0


def own_bias():
    table = np.zeros((8, ROWS), np.float32)
    for key_unit in range(8):
        for query_unit in range(8):
            shared = 1 + min(unit_level(key_unit), unit_level(query_unit))
            table[key_unit, query_unit * UNIT : (query_unit + 1) * UNIT] = math.log2(shared)
    return table


def far_bias():
    table = np.zeros((8, 1024), np.float32)
    for query_unit in range(4):
        lanes = slice(query_unit * UNIT, (query_unit + 1) * UNIT)
        level = unit_level(query_unit)
        table[0, lanes] = math.log2(min(3, level))
        table[1, lanes] = math.log2(min(2, level))
        if level >= 2:
            table[2, lanes] = math.log2(level - 1)
    table[3, 8:] = NEG
    return table


def dot_nt(left, right):
    return lax.dot_general(left, right, (((1,), (1,)), ((), ())), preferred_element_type=jnp.float32)


def dot_nn(left, right):
    return lax.dot_general(left, right, (((1,), (0,)), ((), ())), preferred_element_type=jnp.float32)


def dot_tn(left, right):
    return lax.dot_general(left, right, (((0,), (0,)), ((), ())), preferred_element_type=jnp.float32)


def call(kernel, outs, args, scratch=(), scalars=0, steps=(), in_steps=(), out_steps=(), in_place=None, first=None, flops=0):
    first = first or {}
    steps = steps or ((1,) if first else ())

    def spec(shape, stepped, at_rest, scalar=False, part=None):
        if at_rest:
            return pl.BlockSpec(memory_space=pl.ANY)
        if scalar:
            return pl.BlockSpec(memory_space=pltpu.SMEM)
        if part is not None:
            return pl.BlockSpec(part, lambda *at: (0, 0))
        if not steps:
            return pl.BlockSpec(memory_space=pltpu.VMEM)
        if stepped:
            return pl.BlockSpec((BLOCK, shape[1]), lambda at: (at, 0))
        return pl.BlockSpec(shape, lambda at: (0, 0))

    return pl.pallas_call(
        kernel,
        grid=steps,
        out_shape=[jax.ShapeDtypeStruct(shape, dtype) for shape, dtype in outs],
        in_specs=[spec(arg.shape, at in in_steps, at == in_place, at < scalars, first.get(at)) for at, arg in enumerate(args)],
        out_specs=[
            spec(shape, at in out_steps, in_place is not None and at == 0) for at, (shape, _) in enumerate(outs)
        ],
        scratch_shapes=list(scratch),
        input_output_aliases={} if in_place is None else {in_place: 0},
        compiler_params=pltpu.CompilerParams(vmem_limit_bytes=60 << 20),
        cost_estimate=pl.CostEstimate(flops=flops, bytes_accessed=0, transcendentals=0),
    )(*args)


def sort_rows(source, target, lane, wide):
    wide[...] = source[...].astype(jnp.float32)
    for unit, residue in enumerate(ORDER):
        for pair in range(16):
            parts = [
                wide[pl.ds(8 * (2 * pair + half) + residue, 8, stride=256), :] for half in range(2)
            ]
            rows = slice(unit * UNIT + 16 * pair, unit * UNIT + 16 * pair + 16)
            target[rows, lane : lane + HEAD] = jnp.concatenate(parts, 0).astype(jnp.bfloat16)


def repeat_first(source, target, lane):
    first = source[:16, :].astype(jnp.float32)[:8]
    pair = jnp.concatenate([first, first], 0).astype(jnp.bfloat16)
    for at in range(0, target.shape[0], 16):
        target[at : at + 16, lane : lane + pair.shape[1]] = pair


def prepare_keys_kernel(k_ref, v_ref, q_ref, g_ref, kv_ref, s1_ref, s2_ref, s3_ref, far_ref, wide):
    sort_rows(k_ref, kv_ref, 0, wide)
    sort_rows(v_ref, kv_ref, HEAD, wide)
    s1_ref[:1024] = kv_ref[:1024]
    s2_ref[:512] = kv_ref[:512]
    s3_ref[...] = kv_ref[:256]
    repeat_first(kv_ref, far_ref, 0)
    for lane, ref in ((0, q_ref), (HEAD, g_ref)):
        rows = [ref[at : at + 16, :].astype(jnp.float32)[:1] for at in range(0, ROWS, 256)]
        block = jnp.concatenate(rows + rows, 0).astype(jnp.bfloat16)
        s1_ref[1024:, lane : lane + HEAD] = block
        s2_ref[512:, lane : lane + HEAD] = block


def prepare_queries_kernel(q_ref, g_ref, after_ref, qp_ref, gp_ref, wide):
    sort_rows(q_ref, qp_ref, 0, wide)
    sort_rows(g_ref, gp_ref, 0, wide)


def add_bias(block, rows):
    if all(row is None for row in rows):
        return block
    parts = []
    for at, row in enumerate(rows):
        part = block[at * UNIT : (at + 1) * UNIT]
        parts.append(part if row is None else part + row)
    return jnp.concatenate(parts, 0)


def longest(rows):
    wide = rows.astype(jnp.float32)
    squares = dot_nt(jnp.ones((8, HEAD), jnp.bfloat16), (wide * wide).astype(jnp.bfloat16))
    return 1.01 * jnp.max(squares)


def attend(query, keys, values, biases, small=False):
    scores = [add_bias(dot_nt(key, query) * SCALE2, bias) for key, bias in zip(keys, biases)]
    if small:
        peak = jnp.zeros((1, query.shape[0]), jnp.float32)
        probs = [jnp.exp2(block) for block in scores]
    else:
        peak = functools.reduce(jnp.maximum, [jnp.max(block, 0, keepdims=True) for block in scores])
        probs = [jnp.exp2(block - peak) for block in scores]
    total = sum([jnp.sum(block, 0, keepdims=True) for block in probs])
    out = sum([value(block.astype(jnp.bfloat16)) for value, block in zip(values, probs)])
    return peak, total, out


def finish_rows(row_ref, target, stat, out, grad):
    total = stat[1:2]
    row_ref[0:1, target] = stat[0:1] + jnp.log2(total)
    row_ref[1:2, target] = jnp.sum(grad.astype(jnp.float32).T * out, axis=0, keepdims=True) / total


def own_forward_kernel(q_ref, kv_ref, g_ref, bias_ref, stat_ref, out_ref, odd_ref, vt_ref):
    stat_ref[...] = jnp.zeros_like(stat_ref)
    odd_ref[...] = jnp.zeros_like(odd_ref)
    for unit in range(8):
        rows = slice(unit * UNIT, (unit + 1) * UNIT)
        vt_ref[:, rows] = kv_ref[rows, HEAD:].astype(jnp.float32).T.astype(jnp.bfloat16)
    def halves(small):
        for start in (0, HALF):
            lanes = slice(start, start + HALF)
            keys, values, biases = [], [], []
            for at in range(0, ROWS, BLOCK):
                rows = slice(at, at + BLOCK)
                keys.append(kv_ref[rows, :HEAD])
                values.append(lambda prob, rows=rows: dot_nn(vt_ref[:, rows], prob))
                unit = at // UNIT
                counted = start == 0 and at < HALF
                biases.append([bias_ref[unit + half : unit + half + 1, lanes] if counted else None for half in (0, 1)])
            peak, total, out = attend(q_ref[lanes, :], keys, values, biases, small)
            if start == 0:
                stat_ref[0:1, :] = peak
                stat_ref[1:2, :] = total
                out_ref[...] = out
            else:
                stat = jnp.concatenate([peak, total], 0)
                for first in range(0, HALF, UNIT):
                    part = slice(first, first + UNIT)
                    grad = g_ref[HALF + first : HALF + first + UNIT, :]
                    finish_rows(odd_ref, part, stat[:, part], out[:, part], grad)

    small = longest(q_ref[...]) * longest(kv_ref[:, :HEAD]) < (60.0 / SCALE2) ** 2
    pl.when(small)(functools.partial(halves, True))
    pl.when(jnp.logical_not(small))(functools.partial(halves, False))


def bias_rows(bias_ref, picks, count):
    return [None if pick is None else bias_ref[pick : pick + 1, :count] for pick in picks]


PARTNER, PARTNER_REST, SECOND, THIRD = (0, 1), (None, None), (2, None), (None, None)


def far_blocks(refs):
    third = (256, [(refs[-4:-2], THIRD), (refs[-2:], THIRD)])
    if len(refs) == 4:
        return (third,)
    near = (
        (1024, [((refs[0], 0), PARTNER), ((refs[0], BLOCK), PARTNER_REST)]),
        (512, [((ref, 0), SECOND) for ref in refs[1:3]]),
    )
    return near if len(refs) == 3 else (*near, third)


def read_block(place, lanes):
    ref, first = place
    if isinstance(first, int):
        return ref[first : first + BLOCK, lanes]
    return jnp.concatenate([ref[:, lanes], first[:, lanes]], 0)


def write_block(place, block):
    ref, first = place
    if isinstance(first, int):
        ref[first : first + BLOCK, :] = block
    else:
        ref[...] = block[:UNIT]
        first[...] = block[UNIT:]


def join_state(sums, acc, lanes, far_peak, far_total, far_out):
    peak = sums[0:1, lanes]
    top = jnp.maximum(peak, far_peak)
    near, far = jnp.exp2(peak - top), jnp.exp2(far_peak - top)
    sums[0:1, lanes] = top
    sums[1:2, lanes] = near * sums[1:2, lanes] + far * far_total
    acc[:, lanes] = near * acc[:, lanes] + far * far_out


def middle_forward_kernel(q_ref, bias_ref, stat_ref, out_ref, *rest):
    peers, (sums, acc) = rest[:7], rest[7:]
    sums[...] = stat_ref[...]
    acc[...] = out_ref[...]
    for count, blocks in far_blocks(peers):
        lanes = slice(0, count)
        state = attend(
            q_ref[lanes, :],
            [read_block(place, slice(0, HEAD)) for place, _ in blocks],
            [lambda prob, place=place: dot_tn(read_block(place, slice(HEAD, 256)), prob) for place, _ in blocks],
            [bias_rows(bias_ref, picks, count) for _, picks in blocks],
        )
        join_state(sums, acc, lanes, *state)


def whole_forward_kernel(me_ref, own, r1, r2, r3, far_ref, part_ref, quad_ref, rows_ref):
    for mask, ref in enumerate((own, r1, r2, r3)):
        count = ref.shape[0]
        place = pl.multiple_of((me_ref[0] ^ mask) * 8, 8)
        rows_ref[pl.ds(place, 8), :] = ref[count - 16 :, :].astype(jnp.float32)[:8]
    quad_ref[...] = rows_ref[...].astype(jnp.bfloat16)
    scores = dot_nt(quad_ref[:, :HEAD], far_ref[:, :HEAD]) * SCALE2
    peak = jnp.max(scores, 1, keepdims=True)
    prob = jnp.exp2(scores - peak)
    part_ref[:, :HEAD] = dot_nn(prob.astype(jnp.bfloat16), far_ref[:, HEAD:])
    part_ref[:, HEAD : 2 * HEAD] = jnp.broadcast_to(peak, (8 * QUADS, HEAD))
    part_ref[:, 2 * HEAD :] = jnp.broadcast_to(jnp.sum(prob, 1, keepdims=True), (8 * QUADS, HEAD))


def turn(block, fill):
    return jnp.concatenate([block, jnp.full((HEAD - 8, HEAD), fill, jnp.float32)], 0).T


def finish_kernel(g_ref, stat_ref, out_ref, odd_ref, part_ref, row_ref, tall_ref, sums, acc):
    lanes = slice(0, HEAD)
    sums[...] = stat_ref[:, lanes]
    acc[...] = out_ref[:, lanes]
    for at in range(0, 8 * QUADS, 8):
        part = part_ref[at : at + 8, :]
        far_out = turn(part[:, :HEAD], 0.0)
        far_peak = turn(part[:, HEAD : 2 * HEAD], NEG)[0:1]
        far_total = turn(part[:, 2 * HEAD :], 0.0)[0:1]
        join_state(sums, acc, lanes, far_peak, far_total, far_out)
    row_ref[...] = jnp.zeros_like(row_ref)
    row_ref[:, HALF:] = odd_ref[...]
    for first in range(0, HALF, HEAD):
        lanes = slice(first, first + HEAD)
        stat, out = (sums[...], acc[...]) if first == 0 else (stat_ref[:, lanes], out_ref[:, lanes])
        finish_rows(row_ref, lanes, stat, out, g_ref[lanes, :])
    tall = jnp.concatenate([row_ref[:, :HEAD], jnp.zeros((HEAD - 8, HEAD), jnp.float32)], 0).T
    for at in range(0, 8 * QUADS, 8):
        tall_ref[at : at + 8, :] = tall[:8]


def remote_backward_kernel(me_ref, q_ref, g_ref, bias_ref, row_ref, quad_ref, far_ref, tall_ref, *rest):
    third_dq, far, outs, (dkv_ref, dq_ref, mine_ref, quad_dq) = rest[0], rest[1:4], rest[4:7], rest[7:]
    query, grad = quad_ref[:, :HEAD], quad_ref[:, HEAD:]
    key, value = far_ref[:, :HEAD], far_ref[:, HEAD:]
    weights = jnp.exp2(dot_nt(query, key) * SCALE2 - tall_ref[:, 0:1])
    grad_scores = (weights * (dot_nt(grad, value) - tall_ref[:, 1:2])).astype(jnp.bfloat16)
    dkv_ref[:, :HEAD] = (SCALE * dot_tn(grad_scores, query)).astype(jnp.bfloat16)
    dkv_ref[:, HEAD:] = dot_tn(weights.astype(jnp.bfloat16), grad).astype(jnp.bfloat16)
    quad_dq[...] = dot_nn(grad_scores, key)
    for mask in range(QUADS):
        place = pl.multiple_of((me_ref[0] ^ mask) * 8, 8)
        block = quad_dq[pl.ds(place, 8), :]
        if mask == 0:
            mine_ref[...] = block
        else:
            block = jnp.concatenate([block, jnp.zeros_like(block)], 0)
            block = jnp.concatenate([block, jnp.zeros_like(block)], 1).astype(jnp.bfloat16)
            rows = outs[mask - 1].shape[0]
            outs[mask - 1][rows - 16 :, :] = block
    dq_ref[...] = jnp.zeros_like(dq_ref)
    dq_ref[:, :UNIT] = third_dq[...]
    backward_far(far, outs, (q_ref, g_ref, bias_ref, row_ref), dq_ref)


def third_backward_kernel(q_ref, g_ref, bias_ref, row_ref, *rest):
    far, outs, dq_ref = rest[:4], rest[4:8], rest[8]
    dq_ref[...] = jnp.zeros_like(dq_ref)
    backward_far(far, outs, (q_ref, g_ref, bias_ref, row_ref), dq_ref)


def backward_block(kv_block, q_ref, g_ref, row_ref, bias, count, dq_ref):
    key, value = kv_block[:, :HEAD], kv_block[:, HEAD:]
    lanes = slice(0, count)
    query, grad = q_ref[lanes, :], g_ref[lanes, :]
    scores = add_bias(dot_nt(key, query) * SCALE2, bias)
    weights = jnp.exp2(scores - row_ref[0:1, lanes])
    grad_probs = dot_nt(value, grad)
    grad_scores = (weights * (grad_probs - row_ref[1:2, lanes])).astype(jnp.bfloat16)
    grad_value = dot_nn(weights.astype(jnp.bfloat16), grad)
    grad_key = dot_nn(grad_scores, query)
    dq_ref[:, lanes] += dot_tn(key, grad_scores)
    return SCALE * grad_key, grad_value


def backward_far(far, outs, refs, dq_ref):
    q_ref, g_ref, bias_ref, row_ref = refs
    for (count, blocks), (_, places) in zip(far_blocks(far), far_blocks(outs)):
        for (place, picks), (target, _) in zip(blocks, places):
            bias = bias_rows(bias_ref, picks, count)
            both = backward_block(read_block(place, slice(0, 256)), q_ref, g_ref, row_ref, bias, count, dq_ref)
            write_block(target, jnp.concatenate(both, 1).astype(jnp.bfloat16))


def own_backward_kernel(q_ref, g_ref, bias_ref, row_ref, kv_ref, far_ref, dq_ref, dkv_ref, acc_ref, tall_ref):
    at = pl.program_id(0)

    @pl.when(at == 0)
    def _():
        acc_ref[:, :HALF] = far_ref[...]
        acc_ref[:, HALF:] = jnp.zeros((HEAD, HALF), jnp.float32)

    bias = [bias_ref[pl.ds(2 * at + half, 1), :] for half in (0, 1)]
    grad_key, grad_value = backward_block(kv_ref[...], q_ref, g_ref, row_ref, bias, ROWS, acc_ref)
    dkv_ref[:, :HEAD] = grad_key
    dkv_ref[:, HEAD:] = grad_value

    @pl.when(at == ROWS // BLOCK - 1)
    def _():
        for unit in range(8):
            lanes = slice(unit * UNIT, (unit + 1) * UNIT)
            tall_ref[lanes, :] = acc_ref[:, lanes].T * SCALE
        restore_rows(lambda rows: tall_ref[rows, :], dq_ref)


def restore_rows(read, target):
    for unit, residue in enumerate(ORDER):
        for block in range(32):
            start = unit * UNIT + 8 * block
            target[pl.ds(8 * block + residue, 8, stride=256), :] = read(slice(start, start + 8))


def join_kernel(dkv_ref, mine_ref, b1, b2, b3, b4, b5, b6, b7, far_ref, dq_in, dq_out, dk_ref, dv_ref, sum_ref, tiles, sem):
    def wide(ref, rows=slice(None)):
        return ref[rows, :].astype(jnp.float32)

    places = [(pl.ds(256 * at, 8), pl.ds(8 * at, 8)) for at in range(8)]
    reads = [pltpu.make_async_copy(dq_in.at[rows], tiles.at[spot], sem.at[at]) for at, (rows, spot) in enumerate(places)]
    for copy in reads:
        copy.start()
    mine = mine_ref[...]
    for ref in (b1, b2, b3):
        mine = mine + ref[ref.shape[0] - 16 :, :HEAD].astype(jnp.float32)[:8]
    mine = SCALE * mine
    for copy in reads:
        copy.wait()
    for at in range(8):
        tiles[8 * at : 8 * at + 1, :] += mine[at : at + 1, :]
    writes = [pltpu.make_async_copy(tiles.at[spot], dq_out.at[rows], sem.at[8 + at]) for at, (rows, spot) in enumerate(places)]
    for copy in writes:
        copy.start()
    top, mid, low = slice(0, 256), slice(256, 512), slice(512, 1024)
    near = wide(b1, top) + wide(b2, top) + wide(b3, top)
    sum_ref[top, :] = dkv_ref[top, :] + near + wide(b4) + wide(b5) + wide(b6) + wide(b7)
    sum_ref[mid, :] = dkv_ref[mid, :] + wide(b1, mid) + wide(b2, mid) + wide(b3, mid)
    sum_ref[low, :] = dkv_ref[low, :] + wide(b1, low)
    sum_ref[1024:, :] = dkv_ref[1024:, :]
    sum_ref[:8, :] += jnp.sum(wide(far_ref).reshape(FAR, 8, 256), 0)
    restore_rows(lambda rows: sum_ref[rows, :HEAD], dk_ref)
    restore_rows(lambda rows: sum_ref[rows, HEAD:], dv_ref)
    for copy in writes:
        copy.wait()


def swap(block, mask):
    return lax.ppermute(block, ("z", "y"), [(at, at ^ mask) for at in range(16)])


def swap_all(sends):
    near = [swap(block, mask) for block, mask in zip(sends[:5], (1, 2, 3, 4, 5))]
    last = []
    for at, (block, mask) in enumerate(zip(sends[5:], (6, 7))):
        near[3 + at], block = lax.optimization_barrier((near[3 + at], block))
        last.append(swap(block, mask))
    return near + last


def swap_quad(block):
    parts = block.reshape(QUADS, 8, block.shape[1])
    return lax.all_to_all(parts, "y", 0, 0).reshape(block.shape)


def swap_far(block):
    parts = block.reshape(FAR, 8, block.shape[1])
    return lax.all_to_all(parts, ("grp", "x", "z"), 0, 0).reshape(block.shape)


def on_device(queries, keys, values, cotangent):
    f32, bf16 = jnp.float32, jnp.bfloat16
    near_bias, other_bias = jnp.asarray(own_bias()), jnp.asarray(far_bias())

    def both(*rows):
        return [((count, 256), bf16) for count in rows]

    wide = [pltpu.VMEM((ROWS, HEAD), f32)]
    kv, s1, s2, s3, far = call(
        prepare_keys_kernel, both(ROWS, 1040, 528, 256, 8 * FAR), (keys, values, queries, cotangent), wide
    )
    peers = swap_all([s1, s2, s2, s3, s3, s3, s3])
    q, g = call(prepare_queries_kernel, [((ROWS, HEAD), bf16)] * 2, (queries, cotangent, s3), wide)
    q, far = lax.optimization_barrier((q, far))
    far = swap_far(far)
    state = [((8, HALF), f32), ((HEAD, HALF), f32)]
    stat, out, odd = call(
        own_forward_kernel, [*state, ((8, HALF), f32)], (q, kv, g, near_bias), [pltpu.VMEM((HEAD, ROWS), bf16)], flops=10000000000
    )
    stat, far = lax.optimization_barrier((stat, far))
    me = lax.axis_index("y").astype(jnp.int32).reshape(1)
    part, quad = call(
        whole_forward_kernel,
        [((8 * QUADS, 3 * HEAD), f32), *both(8 * QUADS)],
        (me, s2, *peers[:3], far),
        [pltpu.VMEM((8 * QUADS, 256), f32)],
        scalars=1,
    )
    part = swap_quad(part)
    stat, out = call(middle_forward_kernel, state, (q, other_bias, stat, out, *peers), first={0: (HALF, HEAD)})
    row, tall = call(
        finish_kernel,
        [((8, ROWS), f32), ((8 * QUADS, HEAD), f32)],
        (g, stat, out, odd, part),
        [pltpu.VMEM((8, HEAD), f32), pltpu.VMEM((HEAD, HEAD), f32)],
        first={0: (HALF, HEAD)},
    )
    tall = swap_quad(tall)
    *third, third_dq = call(
        third_backward_kernel,
        [*both(256, 256, 256, 256), ((HEAD, UNIT), f32)],
        (q, g, other_bias, row, *peers[3:]),
        first={0: (UNIT, HEAD), 1: (UNIT, HEAD), 2: (8, UNIT), 3: (8, UNIT)},
    )
    back = [swap(block, mask) for block, mask in zip(third, (4, 5, 6, 7))]
    third_dq, tall = lax.optimization_barrier((third_dq, tall))
    *sends, far_dkv, far_dq, mine = call(
        remote_backward_kernel,
        [*both(1040, 528, 528, 8 * FAR), ((HEAD, HALF), f32), ((8, HEAD), f32)],
        (me, q, g, other_bias, row, quad, far, tall, third_dq, *peers[:3]),
        [pltpu.VMEM((8 * QUADS, HEAD), f32)],
        scalars=1,
        first={1: (HALF, HEAD), 2: (HALF, HEAD), 4: (8, HALF)},
    )
    back = [swap(block, mask) for block, mask in zip(sends, (1, 2, 3))] + back
    far_dkv = swap_far(far_dkv)
    dq, dkv = call(
        own_backward_kernel,
        [((ROWS, HEAD), f32), ((ROWS, 256), f32)],
        (q, g, near_bias, row, kv, far_dq),
        [pltpu.VMEM((HEAD, ROWS), f32), pltpu.VMEM((ROWS, HEAD), f32)],
        steps=(ROWS // BLOCK,),
        in_steps=(4,),
        out_steps=(1,),
        flops=10000000000,
    )
    dq, dk, dv = call(
        join_kernel,
        [((ROWS, HEAD), f32)] * 3,
        (dkv, mine, *back, far_dkv, dq),
        [pltpu.VMEM((ROWS, 256), f32), pltpu.VMEM((64, HEAD), f32), pltpu.SemaphoreType.DMA((16,))],
        in_place=10,
    )
    return dq, dk, dv


def solution(mesh):
    axes = ("grp", "x", "z", "y")
    split = jax.sharding.Mesh(mesh.devices.reshape(4, 4, 4, 4), axes)
    spec = P(axes, None)
    return jax.shard_map(
        on_device, mesh=split, in_specs=(spec,) * 4, out_specs=(spec,) * 3, check_vma=False
    )
```

```python
import functools
import math

import jax
import jax.numpy as jnp
import numpy as np
from jax import lax
from jax.experimental import pallas as pl
from jax.experimental.pallas import tpu as pltpu
from jax.sharding import PartitionSpec as P

ROWS = 2048
HEAD = 128
UNIT = 256
ORDER = (0, 4, 2, 6, 1, 3, 5, 7)
SCALE = HEAD**-0.5
SCALE2 = SCALE * math.log2(math.e)
NEG = -1e30
QUADS = 4
FAR = 64
BLOCK = 512
HALF = 1024
LARGE = 10**10


def unit_level(unit):
    return 3 if unit == 0 else 2 if unit == 1 else 1 if unit < 4 else 0


def own_bias():
    table = np.zeros((8, ROWS), np.float32)
    for key_unit in range(8):
        for query_unit in range(8):
            shared = 1 + min(unit_level(key_unit), unit_level(query_unit))
            table[key_unit, query_unit * UNIT : (query_unit + 1) * UNIT] = math.log2(shared)
    return table


def far_bias():
    table = np.zeros((8, 1024), np.float32)
    for query_unit in range(4):
        lanes = slice(query_unit * UNIT, (query_unit + 1) * UNIT)
        level = unit_level(query_unit)
        table[0, lanes] = math.log2(min(3, level))
        table[1, lanes] = math.log2(min(2, level))
        if level >= 2:
            table[2, lanes] = math.log2(level - 1)
    table[3, 8:] = NEG
    return table


def dot_nt(left, right):
    return lax.dot_general(left, right, (((1,), (1,)), ((), ())), preferred_element_type=jnp.float32)


def dot_nn(left, right):
    return lax.dot_general(left, right, (((1,), (0,)), ((), ())), preferred_element_type=jnp.float32)


def dot_tn(left, right):
    return lax.dot_general(left, right, (((0,), (0,)), ((), ())), preferred_element_type=jnp.float32)


def call(kernel, outs, args, scratch=(), scalars=0, steps=(), in_steps=(), out_steps=(), lane_steps=(), in_place=None, first=None, flops=0, vmem=60):
    first = first or {}
    steps = steps or ((1,) if first else ())

    def spec(shape, stepped, at_rest, scalar=False, part=None, by_lanes=False):
        if at_rest:
            return pl.BlockSpec(memory_space=pl.ANY)
        if scalar:
            return pl.BlockSpec(memory_space=pltpu.SMEM)
        if by_lanes:
            return pl.BlockSpec((shape[0], HEAD), lambda at: (0, at))
        if part is not None:
            return pl.BlockSpec(part, lambda *at: (0, 0))
        if not steps:
            return pl.BlockSpec(memory_space=pltpu.VMEM)
        if stepped:
            return pl.BlockSpec((BLOCK, shape[1]), lambda at: (at, 0))
        return pl.BlockSpec(shape, lambda at: (0, 0))

    return pl.pallas_call(
        kernel,
        grid=steps,
        out_shape=[jax.ShapeDtypeStruct(shape, dtype) for shape, dtype in outs],
        in_specs=[spec(arg.shape, at in in_steps, at == in_place, at < scalars, first.get(at), at in lane_steps) for at, arg in enumerate(args)],
        out_specs=[
            spec(shape, at in out_steps, bool(lane_steps)) for at, (shape, _) in enumerate(outs)
        ],
        scratch_shapes=list(scratch),
        input_output_aliases={} if in_place is None else {in_place: 0},
        compiler_params=pltpu.CompilerParams(vmem_limit_bytes=vmem << 20),
        cost_estimate=pl.CostEstimate(flops=flops, bytes_accessed=0, transcendentals=0),
    )(*args)


def sort_rows(source, target, lane, wide):
    wide[...] = source[...].astype(jnp.float32)
    for unit, residue in enumerate(ORDER):
        for pair in range(16):
            parts = [
                wide[pl.ds(8 * (2 * pair + half) + residue, 8, stride=256), :] for half in range(2)
            ]
            rows = slice(unit * UNIT + 16 * pair, unit * UNIT + 16 * pair + 16)
            target[rows, lane : lane + HEAD] = jnp.concatenate(parts, 0).astype(jnp.bfloat16)


def repeat_first(source, target, lane):
    first = source[:16, :].astype(jnp.float32)[:8]
    pair = jnp.concatenate([first, first], 0).astype(jnp.bfloat16)
    for at in range(0, target.shape[0], 16):
        target[at : at + 16, lane : lane + pair.shape[1]] = pair


def prepare_keys_kernel(k_ref, v_ref, q_ref, g_ref, kv_ref, s1_ref, s2_ref, s3_ref, far_ref, wide):
    sort_rows(k_ref, kv_ref, 0, wide)
    sort_rows(v_ref, kv_ref, HEAD, wide)
    s1_ref[:1024] = kv_ref[:1024]
    s2_ref[:512] = kv_ref[:512]
    s3_ref[...] = kv_ref[:256]
    repeat_first(kv_ref, far_ref, 0)
    for lane, ref in ((0, q_ref), (HEAD, g_ref)):
        rows = [ref[at : at + 16, :].astype(jnp.float32)[:1] for at in range(0, ROWS, 256)]
        block = jnp.concatenate(rows + rows, 0).astype(jnp.bfloat16)
        s1_ref[1024:, lane : lane + HEAD] = block
        s2_ref[512:, lane : lane + HEAD] = block


def add_bias(block, rows):
    if all(row is None for row in rows):
        return block
    parts = []
    for at, row in enumerate(rows):
        part = block[at * UNIT : (at + 1) * UNIT]
        parts.append(part if row is None else part + row)
    return jnp.concatenate(parts, 0)


def longest(rows):
    wide = rows.astype(jnp.float32)
    squares = dot_nt(jnp.ones((8, HEAD), jnp.bfloat16), (wide * wide).astype(jnp.bfloat16))
    return 1.01 * jnp.max(squares)


def attend(query, keys, values, biases, small=False):
    scores = [add_bias(dot_nt(key, query) * SCALE2, bias) for key, bias in zip(keys, biases)]
    if small:
        peak = jnp.zeros((1, query.shape[0]), jnp.float32)
        probs = [jnp.exp2(block) for block in scores]
    else:
        peak = functools.reduce(jnp.maximum, [jnp.max(block, 0, keepdims=True) for block in scores])
        probs = [jnp.exp2(block - peak) for block in scores]
    total = sum([jnp.sum(block, 0, keepdims=True) for block in probs])
    out = sum([value(block.astype(jnp.bfloat16)) for value, block in zip(values, probs)])
    return peak, total, out


def finish_rows(row_ref, target, stat, out, grad):
    total = stat[1:2]
    row_ref[0:1, target] = stat[0:1] + jnp.log2(total)
    row_ref[1:2, target] = jnp.sum(grad.astype(jnp.float32).T * out, axis=0, keepdims=True) / total


def own_forward_kernel(raw_q, raw_g, kv_ref, bias_ref, stat_ref, out_ref, odd_ref, q_ref, g_ref, vt_ref, wide):
    sort_rows(raw_q, q_ref, 0, wide)
    sort_rows(raw_g, g_ref, 0, wide)
    stat_ref[...] = jnp.zeros_like(stat_ref)
    odd_ref[...] = jnp.zeros_like(odd_ref)
    for unit in range(8):
        rows = slice(unit * UNIT, (unit + 1) * UNIT)
        vt_ref[:, rows] = kv_ref[rows, HEAD:].astype(jnp.float32).T.astype(jnp.bfloat16)
    def halves(small):
        for start in (0, HALF):
            lanes = slice(start, start + HALF)
            keys, values, biases = [], [], []
            for at in range(0, ROWS, BLOCK):
                rows = slice(at, at + BLOCK)
                keys.append(kv_ref[rows, :HEAD])
                values.append(lambda prob, rows=rows: dot_nn(vt_ref[:, rows], prob))
                unit = at // UNIT
                counted = start == 0 and at < HALF
                biases.append([bias_ref[unit + half : unit + half + 1, lanes] if counted else None for half in (0, 1)])
            peak, total, out = attend(q_ref[lanes, :], keys, values, biases, small)
            if start == 0:
                stat_ref[0:1, :] = peak
                stat_ref[1:2, :] = total
                out_ref[...] = out
            else:
                stat = jnp.concatenate([peak, total], 0)
                for first in range(0, HALF, UNIT):
                    part = slice(first, first + UNIT)
                    grad = g_ref[HALF + first : HALF + first + UNIT, :]
                    finish_rows(odd_ref, part, stat[:, part], out[:, part], grad)

    small = longest(q_ref[...]) * longest(kv_ref[:, :HEAD]) < (60.0 / SCALE2) ** 2
    pl.when(small)(functools.partial(halves, True))
    pl.when(jnp.logical_not(small))(functools.partial(halves, False))


def bias_rows(bias_ref, picks, count):
    return [None if pick is None else bias_ref[pick : pick + 1, :count] for pick in picks]


PARTNER, PARTNER_REST, SECOND, THIRD = (0, 1), (None, None), (2, None), (None, None)


def far_blocks(refs):
    third = (256, [(refs[-4:-2], THIRD), (refs[-2:], THIRD)])
    if len(refs) == 4:
        return (third,)
    near = (
        (1024, [((refs[0], 0), PARTNER), ((refs[0], BLOCK), PARTNER_REST)]),
        (512, [((ref, 0), SECOND) for ref in refs[1:3]]),
    )
    return near if len(refs) == 3 else (*near, third)


def read_block(place, lanes):
    ref, first = place
    if isinstance(first, int):
        return ref[first : first + BLOCK, lanes]
    return jnp.concatenate([ref[:, lanes], first[:, lanes]], 0)


def write_block(place, block):
    ref, first = place
    if isinstance(first, int):
        ref[first : first + BLOCK, :] = block
    else:
        ref[...] = block[:UNIT]
        first[...] = block[UNIT:]


def join_state(sums, acc, lanes, far_peak, far_total, far_out):
    peak = sums[0:1, lanes]
    top = jnp.maximum(peak, far_peak)
    near, far = jnp.exp2(peak - top), jnp.exp2(far_peak - top)
    sums[0:1, lanes] = top
    sums[1:2, lanes] = near * sums[1:2, lanes] + far * far_total
    acc[:, lanes] = near * acc[:, lanes] + far * far_out


def middle_forward_kernel(q_ref, bias_ref, stat_ref, out_ref, *rest):
    peers, (sums, acc) = rest[:7], rest[7:]
    sums[...] = stat_ref[...]
    acc[...] = out_ref[...]
    for count, blocks in far_blocks(peers):
        lanes = slice(0, count)
        state = attend(
            q_ref[lanes, :],
            [read_block(place, slice(0, HEAD)) for place, _ in blocks],
            [lambda prob, place=place: dot_tn(read_block(place, slice(HEAD, 256)), prob) for place, _ in blocks],
            [bias_rows(bias_ref, picks, count) for _, picks in blocks],
        )
        join_state(sums, acc, lanes, *state)


def whole_forward_kernel(me_ref, own, r1, r2, r3, far_ref, part_ref, quad_ref, rows_ref):
    for mask, ref in enumerate((own, r1, r2, r3)):
        count = ref.shape[0]
        place = pl.multiple_of((me_ref[0] ^ mask) * 8, 8)
        rows_ref[pl.ds(place, 8), :] = ref[count - 16 :, :].astype(jnp.float32)[:8]
    quad_ref[...] = rows_ref[...].astype(jnp.bfloat16)
    scores = dot_nt(quad_ref[:, :HEAD], far_ref[:, :HEAD]) * SCALE2
    peak = jnp.max(scores, 1, keepdims=True)
    prob = jnp.exp2(scores - peak)
    part_ref[:, :HEAD] = dot_nn(prob.astype(jnp.bfloat16), far_ref[:, HEAD:])
    part_ref[:, HEAD : 2 * HEAD] = jnp.broadcast_to(peak, (8 * QUADS, HEAD))
    part_ref[:, 2 * HEAD :] = jnp.broadcast_to(jnp.sum(prob, 1, keepdims=True), (8 * QUADS, HEAD))


def turn(block, fill):
    return jnp.concatenate([block, jnp.full((HEAD - 8, HEAD), fill, jnp.float32)], 0).T


def finish_kernel(q_ref, g_ref, bias_ref, stat_ref, out_ref, odd_ref, part_ref, *rest):
    far, third, (dq_ref, row_ref, tall_ref, sums, acc) = rest[:4], rest[4:8], rest[8:]
    lanes = slice(0, HEAD)
    sums[...] = stat_ref[:, lanes]
    acc[...] = out_ref[:, lanes]
    for at in range(0, 8 * QUADS, 8):
        part = part_ref[at : at + 8, :]
        far_out = turn(part[:, :HEAD], 0.0)
        far_peak = turn(part[:, HEAD : 2 * HEAD], NEG)[0:1]
        far_total = turn(part[:, 2 * HEAD :], 0.0)[0:1]
        join_state(sums, acc, lanes, far_peak, far_total, far_out)
    row_ref[...] = jnp.zeros_like(row_ref)
    row_ref[:, HALF:] = odd_ref[...]
    for first in range(0, HALF, HEAD):
        lanes = slice(first, first + HEAD)
        stat, out = (sums[...], acc[...]) if first == 0 else (stat_ref[:, lanes], out_ref[:, lanes])
        finish_rows(row_ref, lanes, stat, out, g_ref[lanes, :])
    tall = jnp.concatenate([row_ref[:, :HEAD], jnp.zeros((HEAD - 8, HEAD), jnp.float32)], 0).T
    for at in range(0, 8 * QUADS, 8):
        tall_ref[at : at + 8, :] = tall[:8]
    dq_ref[...] = jnp.zeros_like(dq_ref)
    backward_far(far, third, (q_ref, g_ref, bias_ref, row_ref), dq_ref)


def remote_backward_kernel(me_ref, q_ref, g_ref, bias_ref, row_ref, quad_ref, far_ref, tall_ref, *rest):
    third_dq, far, outs, (dkv_ref, dq_ref, mine_ref, quad_dq) = rest[0], rest[1:4], rest[4:7], rest[7:]
    query, grad = quad_ref[:, :HEAD], quad_ref[:, HEAD:]
    key, value = far_ref[:, :HEAD], far_ref[:, HEAD:]
    weights = jnp.exp2(dot_nt(query, key) * SCALE2 - tall_ref[:, 0:1])
    grad_scores = (weights * (dot_nt(grad, value) - tall_ref[:, 1:2])).astype(jnp.bfloat16)
    dkv_ref[:, :HEAD] = (SCALE * dot_tn(grad_scores, query)).astype(jnp.bfloat16)
    dkv_ref[:, HEAD:] = dot_tn(weights.astype(jnp.bfloat16), grad).astype(jnp.bfloat16)
    quad_dq[...] = dot_nn(grad_scores, key)
    for mask in range(QUADS):
        place = pl.multiple_of((me_ref[0] ^ mask) * 8, 8)
        block = quad_dq[pl.ds(place, 8), :]
        if mask == 0:
            mine_ref[...] = block
        else:
            block = jnp.concatenate([block, jnp.zeros_like(block)], 0)
            block = jnp.concatenate([block, jnp.zeros_like(block)], 1).astype(jnp.bfloat16)
            rows = outs[mask - 1].shape[0]
            outs[mask - 1][rows - 16 :, :] = block
    dq_ref[...] = jnp.zeros_like(dq_ref)
    dq_ref[:, :UNIT] = third_dq[...]
    backward_far(far, outs, (q_ref, g_ref, bias_ref, row_ref), dq_ref)


def backward_block(kv_block, q_ref, g_ref, row_ref, bias, count, dq_ref):
    key, value = kv_block[:, :HEAD], kv_block[:, HEAD:]
    lanes = slice(0, count)
    query, grad = q_ref[lanes, :], g_ref[lanes, :]
    scores = add_bias(dot_nt(key, query) * SCALE2, bias)
    weights = jnp.exp2(scores - row_ref[0:1, lanes])
    grad_probs = dot_nt(value, grad)
    grad_scores = (weights * (grad_probs - row_ref[1:2, lanes])).astype(jnp.bfloat16)
    grad_value = dot_nn(weights.astype(jnp.bfloat16), grad)
    grad_key = dot_nn(grad_scores, query)
    dq_ref[:, lanes] += dot_tn(key, grad_scores)
    return SCALE * grad_key, grad_value


def backward_far(far, outs, refs, dq_ref):
    q_ref, g_ref, bias_ref, row_ref = refs
    for (count, blocks), (_, places) in zip(far_blocks(far), far_blocks(outs)):
        for (place, picks), (target, _) in zip(blocks, places):
            bias = bias_rows(bias_ref, picks, count)
            both = backward_block(read_block(place, slice(0, 256)), q_ref, g_ref, row_ref, bias, count, dq_ref)
            write_block(target, jnp.concatenate(both, 1).astype(jnp.bfloat16))


def own_backward_kernel(q_ref, g_ref, bias_ref, row_ref, kv_ref, far_ref, dq_ref, dkv_ref, acc_ref, tall_ref):
    at = pl.program_id(0)

    @pl.when(at == 0)
    def _():
        acc_ref[:, :HALF] = far_ref[...]
        acc_ref[:, HALF:] = jnp.zeros((HEAD, HALF), jnp.float32)

    bias = [bias_ref[pl.ds(2 * at + half, 1), :] for half in (0, 1)]
    grad_key, grad_value = backward_block(kv_ref[...], q_ref, g_ref, row_ref, bias, ROWS, acc_ref)
    dkv_ref[:, :HEAD] = grad_key
    dkv_ref[:, HEAD:] = grad_value

    @pl.when(at == ROWS // BLOCK - 1)
    def _():
        for unit in range(8):
            lanes = slice(unit * UNIT, (unit + 1) * UNIT)
            tall_ref[lanes, :] = acc_ref[:, lanes].T * SCALE
        restore_rows(lambda rows: tall_ref[rows, :], dq_ref)


def restore_rows(read, target):
    for unit, residue in enumerate(ORDER):
        for block in range(32):
            start = unit * UNIT + 8 * block
            target[pl.ds(8 * block + residue, 8, stride=256), :] = read(slice(start, start + 8))


def join_kernel(dkv_ref, mine_ref, b1, b2, b3, b4, b5, b6, b7, far_ref, dq_in, dq_out, dk_out, dv_out, sum_ref, done_ref, tiles, sem):
    at = pl.program_id(0)

    def wide(ref, rows=slice(None)):
        return ref[rows, :].astype(jnp.float32)

    places = [(pl.ds(256 * step, 8), pl.ds(8 * step, 8)) for step in range(8)]
    reads = [pltpu.make_async_copy(dq_in.at[rows], tiles.at[spot], sem.at[n]) for n, (rows, spot) in enumerate(places)]
    writes = [pltpu.make_async_copy(tiles.at[spot], dq_out.at[rows], sem.at[8 + n]) for n, (rows, spot) in enumerate(places)]
    sends = [pltpu.make_async_copy(done_ref.at[n], out, sem.at[16 + n]) for n, out in enumerate((dk_out, dv_out))]

    @pl.when(at == 0)
    def _():
        for copy in reads:
            copy.start()

    top, mid, low = slice(0, 256), slice(256, 512), slice(512, 1024)
    near = wide(b1, top) + wide(b2, top) + wide(b3, top)
    sum_ref[top, :] = dkv_ref[top, :] + near + wide(b4) + wide(b5) + wide(b6) + wide(b7)
    sum_ref[mid, :] = dkv_ref[mid, :] + wide(b1, mid) + wide(b2, mid) + wide(b3, mid)
    sum_ref[low, :] = dkv_ref[low, :] + wide(b1, low)
    sum_ref[HALF:, :] = dkv_ref[HALF:, :]
    sum_ref[:8, :] += jnp.sum(wide(far_ref).reshape(FAR, 8, HEAD), 0)

    @pl.when(at == 0)
    def _():
        restore_rows(lambda rows: sum_ref[rows, :], done_ref.at[0])
        sends[0].start()
        mine = mine_ref[...]
        for ref in (b1, b2, b3):
            mine = mine + ref[ref.shape[0] - 16 :, :].astype(jnp.float32)[:8]
        mine = SCALE * mine
        for copy in reads:
            copy.wait()
        for step in range(8):
            tiles[8 * step : 8 * step + 1, :] += mine[step : step + 1, :]
        for copy in writes:
            copy.start()

    @pl.when(at == 1)
    def _():
        restore_rows(lambda rows: sum_ref[rows, :], done_ref.at[1])
        sends[1].start()
        for copy in writes + sends:
            copy.wait()


def swap(block, mask):
    return lax.ppermute(block, ("z", "y"), [(at, at ^ mask) for at in range(16)])


def swap_all(sends):
    near = [swap(block, mask) for block, mask in zip(sends[:5], (1, 2, 3, 4, 5))]
    last = []
    for at, (block, mask) in enumerate(zip(sends[5:], (6, 7))):
        near[3 + at], block = lax.optimization_barrier((near[3 + at], block))
        last.append(swap(block, mask))
    return near + last


def swap_quad(block):
    parts = block.reshape(QUADS, 8, block.shape[1])
    return lax.all_to_all(parts, "y", 0, 0).reshape(block.shape)


def swap_far(block):
    parts = block.reshape(FAR, 8, block.shape[1])
    return lax.all_to_all(parts, ("grp", "x", "z"), 0, 0).reshape(block.shape)


def on_device(queries, keys, values, cotangent):
    f32, bf16 = jnp.float32, jnp.bfloat16
    near_bias, other_bias = jnp.asarray(own_bias()), jnp.asarray(far_bias())

    def both(*rows):
        return [((count, 256), bf16) for count in rows]

    wide = [pltpu.VMEM((ROWS, HEAD), f32)]
    kv, s1, s2, s3, far = call(
        prepare_keys_kernel, both(ROWS, 1040, 528, 256, 8 * FAR), (keys, values, queries, cotangent), wide
    )
    peers = swap_all([s1, s2, s2, s3, s3, s3, s3])
    far = swap_far(far)
    state = [((8, HALF), f32), ((HEAD, HALF), f32)]
    stat, out, odd, q, g = call(
        own_forward_kernel,
        [*state, ((8, HALF), f32), ((ROWS, HEAD), bf16), ((ROWS, HEAD), bf16)],
        (queries, cotangent, kv, near_bias),
        [pltpu.VMEM((HEAD, ROWS), bf16), *wide],
        flops=LARGE,
    )
    stat, far = lax.optimization_barrier((stat, far))
    me = lax.axis_index("y").astype(jnp.int32).reshape(1)
    part, quad = call(
        whole_forward_kernel,
        [((8 * QUADS, 3 * HEAD), f32), *both(8 * QUADS)],
        (me, s2, *peers[:3], far),
        [pltpu.VMEM((8 * QUADS, 256), f32)],
        scalars=1,
        vmem=24,
    )
    part = swap_quad(part)
    stat, out = call(middle_forward_kernel, state, (q, other_bias, stat, out, *peers), first={0: (HALF, HEAD)})
    *third, third_dq, row, tall = call(
        finish_kernel,
        [*both(256, 256, 256, 256), ((HEAD, UNIT), f32), ((8, ROWS), f32), ((8 * QUADS, HEAD), f32)],
        (q, g, other_bias, stat, out, odd, part, *peers[3:]),
        [pltpu.VMEM((8, HEAD), f32), pltpu.VMEM((HEAD, HEAD), f32)],
        first={0: (UNIT, HEAD), 1: (HALF, HEAD), 2: (8, UNIT)},
    )
    tall = swap_quad(tall)
    back = [swap(block, mask) for block, mask in zip(third, (4, 5, 6, 7))]
    third_dq, tall = lax.optimization_barrier((third_dq, tall))
    *sends, far_dkv, far_dq, mine = call(
        remote_backward_kernel,
        [*both(1040, 528, 528, 8 * FAR), ((HEAD, HALF), f32), ((8, HEAD), f32)],
        (me, q, g, other_bias, row, quad, far, tall, third_dq, *peers[:3]),
        [pltpu.VMEM((8 * QUADS, HEAD), f32)],
        scalars=1,
        first={1: (HALF, HEAD), 2: (HALF, HEAD), 4: (8, HALF)},
    )
    back = [swap(block, mask) for block, mask in zip(sends, (1, 2, 3))] + back
    far_dkv = swap_far(far_dkv)
    dq, dkv = call(
        own_backward_kernel,
        [((ROWS, HEAD), f32), ((ROWS, 256), f32)],
        (q, g, near_bias, row, kv, far_dq),
        [pltpu.VMEM((HEAD, ROWS), f32), pltpu.VMEM((ROWS, HEAD), f32)],
        steps=(ROWS // BLOCK,),
        in_steps=(4,),
        out_steps=(1,),
        flops=LARGE,
    )
    dq, dk, dv = call(
        join_kernel,
        [((ROWS, HEAD), f32)] * 3,
        (dkv, mine, *back, far_dkv, dq),
        [
            pltpu.VMEM((ROWS, HEAD), f32),
            pltpu.VMEM((2, ROWS, HEAD), f32),
            pltpu.VMEM((64, HEAD), f32),
            pltpu.SemaphoreType.DMA((18,)),
        ],
        steps=(2,),
        lane_steps=(0, *range(2, 10)),
        in_place=10,
    )
    return dq, dk, dv


def solution(mesh):
    axes = ("grp", "x", "z", "y")
    split = jax.sharding.Mesh(mesh.devices.reshape(4, 4, 4, 4), axes)
    spec = P(axes, None)
    return jax.shard_map(
        on_device, mesh=split, in_specs=(spec,) * 4, out_specs=(spec,) * 3, check_vma=False
    )
```

```python
import functools
import math

import jax
import jax.numpy as jnp
import numpy as np
from jax import lax
from jax.experimental import pallas as pl
from jax.experimental.pallas import tpu as pltpu
from jax.sharding import PartitionSpec as P

ROWS = 2048
HEAD = 128
UNIT = 256
ORDER = (0, 4, 2, 6, 1, 3, 5, 7)
SCALE = HEAD**-0.5
SCALE2 = SCALE * math.log2(math.e)
NEG = -1e30
QUADS = 4
FAR = 64
BLOCK = 512
HALF = 1024
LARGE = 10**10


def unit_level(unit):
    return 3 if unit == 0 else 2 if unit == 1 else 1 if unit < 4 else 0


def own_bias():
    table = np.zeros((8, ROWS), np.float32)
    for key_unit in range(8):
        for query_unit in range(8):
            shared = 1 + min(unit_level(key_unit), unit_level(query_unit))
            table[key_unit, query_unit * UNIT : (query_unit + 1) * UNIT] = math.log2(shared)
    return table


def far_bias():
    table = np.zeros((8, 1024), np.float32)
    for query_unit in range(4):
        lanes = slice(query_unit * UNIT, (query_unit + 1) * UNIT)
        level = unit_level(query_unit)
        table[0, lanes] = math.log2(min(3, level))
        table[1, lanes] = math.log2(min(2, level))
        if level >= 2:
            table[2, lanes] = math.log2(level - 1)
    table[3, 8:] = NEG
    return table


def dot_nt(left, right):
    return lax.dot_general(left, right, (((1,), (1,)), ((), ())), preferred_element_type=jnp.float32)


def dot_nn(left, right):
    return lax.dot_general(left, right, (((1,), (0,)), ((), ())), preferred_element_type=jnp.float32)


def dot_tn(left, right):
    return lax.dot_general(left, right, (((0,), (0,)), ((), ())), preferred_element_type=jnp.float32)


def call(kernel, outs, args, scratch=(), scalars=0, steps=(), in_steps=(), out_steps=(), lane_steps=(), in_place=None, first=None, flops=0, vmem=60):
    first = first or {}
    steps = steps or ((1,) if first else ())

    def spec(shape, stepped, at_rest, scalar=False, part=None, by_lanes=False):
        if at_rest:
            return pl.BlockSpec(memory_space=pl.ANY)
        if scalar:
            return pl.BlockSpec(memory_space=pltpu.SMEM)
        if by_lanes:
            return pl.BlockSpec((shape[0], HEAD), lambda at: (0, at))
        if part is not None:
            return pl.BlockSpec(part, lambda *at: (0, 0))
        if not steps:
            return pl.BlockSpec(memory_space=pltpu.VMEM)
        if stepped:
            return pl.BlockSpec((BLOCK, shape[1]), lambda at: (at, 0))
        return pl.BlockSpec(shape, lambda at: (0, 0))

    return pl.pallas_call(
        kernel,
        grid=steps,
        out_shape=[jax.ShapeDtypeStruct(shape, dtype) for shape, dtype in outs],
        in_specs=[spec(arg.shape, at in in_steps, at == in_place, at < scalars, first.get(at), at in lane_steps) for at, arg in enumerate(args)],
        out_specs=[
            spec(shape, at in out_steps, bool(lane_steps)) for at, (shape, _) in enumerate(outs)
        ],
        scratch_shapes=list(scratch),
        input_output_aliases={} if in_place is None else {in_place: 0},
        compiler_params=pltpu.CompilerParams(vmem_limit_bytes=vmem << 20),
        cost_estimate=pl.CostEstimate(flops=flops, bytes_accessed=0, transcendentals=0),
    )(*args)


def sort_rows(source, target, lane, wide):
    wide[...] = source[...].astype(jnp.float32)
    for unit, residue in enumerate(ORDER):
        for pair in range(16):
            parts = [
                wide[pl.ds(8 * (2 * pair + half) + residue, 8, stride=256), :] for half in range(2)
            ]
            rows = slice(unit * UNIT + 16 * pair, unit * UNIT + 16 * pair + 16)
            target[rows, lane : lane + HEAD] = jnp.concatenate(parts, 0).astype(jnp.bfloat16)


def repeat_first(source, target, lane):
    first = source[:16, :].astype(jnp.float32)[:8]
    pair = jnp.concatenate([first, first], 0).astype(jnp.bfloat16)
    for at in range(0, target.shape[0], 16):
        target[at : at + 16, lane : lane + pair.shape[1]] = pair


def prepare_keys_kernel(k_ref, v_ref, q_ref, g_ref, kv_ref, s1_ref, s2_ref, s3_ref, far_ref, wide):
    sort_rows(k_ref, kv_ref, 0, wide)
    sort_rows(v_ref, kv_ref, HEAD, wide)
    s1_ref[:1024] = kv_ref[:1024]
    s2_ref[:512] = kv_ref[:512]
    s3_ref[...] = kv_ref[:256]
    repeat_first(kv_ref, far_ref, 0)
    for lane, ref in ((0, q_ref), (HEAD, g_ref)):
        rows = [ref[at : at + 16, :].astype(jnp.float32)[:1] for at in range(0, ROWS, 256)]
        block = jnp.concatenate(rows + rows, 0).astype(jnp.bfloat16)
        s1_ref[1024:, lane : lane + HEAD] = block
        s2_ref[512:, lane : lane + HEAD] = block


def add_bias(block, rows):
    if all(row is None for row in rows):
        return block
    parts = []
    for at, row in enumerate(rows):
        part = block[at * UNIT : (at + 1) * UNIT]
        parts.append(part if row is None else part + row)
    return jnp.concatenate(parts, 0)


def longest(rows):
    wide = rows.astype(jnp.float32)
    squares = dot_nt(jnp.ones((8, HEAD), jnp.bfloat16), (wide * wide).astype(jnp.bfloat16))
    return 1.01 * jnp.max(squares)


def attend(query, keys, values, biases, small=False):
    scores = [add_bias(dot_nt(key, query) * SCALE2, bias) for key, bias in zip(keys, biases)]
    if small:
        peak = jnp.zeros((1, query.shape[0]), jnp.float32)
        probs = [jnp.exp2(block) for block in scores]
    else:
        peak = functools.reduce(jnp.maximum, [jnp.max(block, 0, keepdims=True) for block in scores])
        probs = [jnp.exp2(block - peak) for block in scores]
    total = sum([jnp.sum(block, 0, keepdims=True) for block in probs])
    out = sum([value(block.astype(jnp.bfloat16)) for value, block in zip(values, probs)])
    return peak, total, out


def finish_rows(row_ref, target, stat, out, grad):
    total = stat[1:2]
    row_ref[0:1, target] = stat[0:1] + jnp.log2(total)
    row_ref[1:2, target] = jnp.sum(grad.astype(jnp.float32).T * out, axis=0, keepdims=True) / total


def own_forward_kernel(raw_q, raw_g, kv_ref, bias_ref, stat_ref, out_ref, odd_ref, q_ref, g_ref, vt_ref, wide):
    sort_rows(raw_q, q_ref, 0, wide)
    sort_rows(raw_g, g_ref, 0, wide)
    stat_ref[...] = jnp.zeros_like(stat_ref)
    odd_ref[...] = jnp.zeros_like(odd_ref)
    for unit in range(8):
        rows = slice(unit * UNIT, (unit + 1) * UNIT)
        vt_ref[:, rows] = kv_ref[rows, HEAD:].astype(jnp.float32).T.astype(jnp.bfloat16)
    def halves(small):
        for start in (0, HALF):
            lanes = slice(start, start + HALF)
            keys, values, biases = [], [], []
            for at in range(0, ROWS, BLOCK):
                rows = slice(at, at + BLOCK)
                keys.append(kv_ref[rows, :HEAD])
                values.append(lambda prob, rows=rows: dot_nn(vt_ref[:, rows], prob))
                unit = at // UNIT
                counted = start == 0 and at < HALF
                biases.append([bias_ref[unit + half : unit + half + 1, lanes] if counted else None for half in (0, 1)])
            peak, total, out = attend(q_ref[lanes, :], keys, values, biases, small)
            if start == 0:
                stat_ref[0:1, :] = peak
                stat_ref[1:2, :] = total
                out_ref[...] = out
            else:
                stat = jnp.concatenate([peak, total], 0)
                for first in range(0, HALF, UNIT):
                    part = slice(first, first + UNIT)
                    grad = g_ref[HALF + first : HALF + first + UNIT, :]
                    finish_rows(odd_ref, part, stat[:, part], out[:, part], grad)

    small = longest(q_ref[...]) * longest(kv_ref[:, :HEAD]) < (60.0 / SCALE2) ** 2
    pl.when(small)(functools.partial(halves, True))
    pl.when(jnp.logical_not(small))(functools.partial(halves, False))


def bias_rows(bias_ref, picks, count):
    return [None if pick is None else bias_ref[pick : pick + 1, :count] for pick in picks]


PARTNER, PARTNER_REST, SECOND, THIRD = (0, 1), (None, None), (2, None), (None, None)


def far_blocks(refs):
    third = (256, [(refs[-4:-2], THIRD), (refs[-2:], THIRD)])
    if len(refs) == 4:
        return (third,)
    near = (
        (1024, [((refs[0], 0), PARTNER), ((refs[0], BLOCK), PARTNER_REST)]),
        (512, [((ref, 0), SECOND) for ref in refs[1:3]]),
    )
    return near if len(refs) == 3 else (*near, third)


def read_block(place, lanes):
    ref, first = place
    if isinstance(first, int):
        return ref[first : first + BLOCK, lanes]
    return jnp.concatenate([ref[:, lanes], first[:, lanes]], 0)


def write_block(place, block):
    ref, first = place
    if isinstance(first, int):
        ref[first : first + BLOCK, :] = block
    else:
        ref[...] = block[:UNIT]
        first[...] = block[UNIT:]


def join_state(sums, acc, lanes, far_peak, far_total, far_out):
    peak = sums[0:1, lanes]
    top = jnp.maximum(peak, far_peak)
    near, far = jnp.exp2(peak - top), jnp.exp2(far_peak - top)
    sums[0:1, lanes] = top
    sums[1:2, lanes] = near * sums[1:2, lanes] + far * far_total
    acc[:, lanes] = near * acc[:, lanes] + far * far_out


def middle_forward_kernel(q_ref, bias_ref, stat_ref, out_ref, *rest):
    peers, (sums, acc) = rest[:7], rest[7:]
    sums[...] = stat_ref[...]
    acc[...] = out_ref[...]
    for count, blocks in far_blocks(peers):
        lanes = slice(0, count)
        state = attend(
            q_ref[lanes, :],
            [read_block(place, slice(0, HEAD)) for place, _ in blocks],
            [lambda prob, place=place: dot_tn(read_block(place, slice(HEAD, 256)), prob) for place, _ in blocks],
            [bias_rows(bias_ref, picks, count) for _, picks in blocks],
        )
        join_state(sums, acc, lanes, *state)


def whole_forward_kernel(me_ref, own, r1, r2, r3, far_ref, part_ref, quad_ref, rows_ref):
    for mask, ref in enumerate((own, r1, r2, r3)):
        count = ref.shape[0]
        place = pl.multiple_of((me_ref[0] ^ mask) * 8, 8)
        rows_ref[pl.ds(place, 8), :] = ref[count - 16 :, :].astype(jnp.float32)[:8]
    quad_ref[...] = rows_ref[...].astype(jnp.bfloat16)
    scores = dot_nt(quad_ref[:, :HEAD], far_ref[:, :HEAD]) * SCALE2
    peak = jnp.max(scores, 1, keepdims=True)
    prob = jnp.exp2(scores - peak)
    part_ref[:, :HEAD] = dot_nn(prob.astype(jnp.bfloat16), far_ref[:, HEAD:])
    part_ref[:, HEAD : 2 * HEAD] = jnp.broadcast_to(peak, (8 * QUADS, HEAD))
    part_ref[:, 2 * HEAD :] = jnp.broadcast_to(jnp.sum(prob, 1, keepdims=True), (8 * QUADS, HEAD))


def turn(block, fill):
    return jnp.concatenate([block, jnp.full((HEAD - 8, HEAD), fill, jnp.float32)], 0).T


def finish_kernel(q_ref, g_ref, bias_ref, stat_ref, out_ref, odd_ref, part_ref, *rest):
    far, third, (dq_ref, row_ref, tall_ref, sums, acc) = rest[:4], rest[4:8], rest[8:]
    lanes = slice(0, HEAD)
    sums[...] = stat_ref[:, lanes]
    acc[...] = out_ref[:, lanes]
    for at in range(0, 8 * QUADS, 8):
        part = part_ref[at : at + 8, :]
        far_out = turn(part[:, :HEAD], 0.0)
        far_peak = turn(part[:, HEAD : 2 * HEAD], NEG)[0:1]
        far_total = turn(part[:, 2 * HEAD :], 0.0)[0:1]
        join_state(sums, acc, lanes, far_peak, far_total, far_out)
    row_ref[...] = jnp.zeros_like(row_ref)
    row_ref[:, HALF:] = odd_ref[...]
    for first in range(0, HALF, HEAD):
        lanes = slice(first, first + HEAD)
        stat, out = (sums[...], acc[...]) if first == 0 else (stat_ref[:, lanes], out_ref[:, lanes])
        finish_rows(row_ref, lanes, stat, out, g_ref[lanes, :])
    tall = jnp.concatenate([row_ref[:, :HEAD], jnp.zeros((HEAD - 8, HEAD), jnp.float32)], 0).T
    for at in range(0, 8 * QUADS, 8):
        tall_ref[at : at + 8, :] = tall[:8]
    dq_ref[...] = jnp.zeros_like(dq_ref)
    backward_far(far, third, (q_ref, g_ref, bias_ref, row_ref), dq_ref)


def remote_backward_kernel(me_ref, q_ref, g_ref, bias_ref, row_ref, quad_ref, far_ref, tall_ref, *rest):
    third_dq, far, outs, (dkv_ref, dq_ref, mine_ref, quad_dq) = rest[0], rest[1:4], rest[4:7], rest[7:]
    query, grad = quad_ref[:, :HEAD], quad_ref[:, HEAD:]
    key, value = far_ref[:, :HEAD], far_ref[:, HEAD:]
    weights = jnp.exp2(dot_nt(query, key) * SCALE2 - tall_ref[:, 0:1])
    grad_scores = (weights * (dot_nt(grad, value) - tall_ref[:, 1:2])).astype(jnp.bfloat16)
    dkv_ref[:, :HEAD] = (SCALE * dot_tn(grad_scores, query)).astype(jnp.bfloat16)
    dkv_ref[:, HEAD:] = dot_tn(weights.astype(jnp.bfloat16), grad).astype(jnp.bfloat16)
    quad_dq[...] = dot_nn(grad_scores, key)
    for mask in range(QUADS):
        place = pl.multiple_of((me_ref[0] ^ mask) * 8, 8)
        block = quad_dq[pl.ds(place, 8), :]
        if mask == 0:
            mine_ref[...] = block
        else:
            block = jnp.concatenate([block, jnp.zeros_like(block)], 0)
            block = jnp.concatenate([block, jnp.zeros_like(block)], 1).astype(jnp.bfloat16)
            rows = outs[mask - 1].shape[0]
            outs[mask - 1][rows - 16 :, :] = block
    dq_ref[...] = jnp.zeros_like(dq_ref)
    dq_ref[:, :UNIT] = third_dq[...]
    backward_far(far, outs, (q_ref, g_ref, bias_ref, row_ref), dq_ref)


def backward_block(kv_block, q_ref, g_ref, row_ref, bias, count, dq_ref):
    key, value = kv_block[:, :HEAD], kv_block[:, HEAD:]
    lanes = slice(0, count)
    query, grad = q_ref[lanes, :], g_ref[lanes, :]
    scores = add_bias(dot_nt(key, query) * SCALE2, bias)
    weights = jnp.exp2(scores - row_ref[0:1, lanes])
    grad_probs = dot_nt(value, grad)
    grad_scores = (weights * (grad_probs - row_ref[1:2, lanes])).astype(jnp.bfloat16)
    grad_value = dot_nn(weights.astype(jnp.bfloat16), grad)
    grad_key = dot_nn(grad_scores, query)
    dq_ref[:, lanes] += dot_tn(key, grad_scores)
    return SCALE * grad_key, grad_value


def backward_far(far, outs, refs, dq_ref):
    q_ref, g_ref, bias_ref, row_ref = refs
    for (count, blocks), (_, places) in zip(far_blocks(far), far_blocks(outs)):
        for (place, picks), (target, _) in zip(blocks, places):
            bias = bias_rows(bias_ref, picks, count)
            both = backward_block(read_block(place, slice(0, 256)), q_ref, g_ref, row_ref, bias, count, dq_ref)
            write_block(target, jnp.concatenate(both, 1).astype(jnp.bfloat16))


def own_backward_kernel(q_ref, g_ref, bias_ref, row_ref, kv_ref, far_ref, dq_ref, dkv_ref, acc_ref, tall_ref):
    at = pl.program_id(0)

    @pl.when(at == 0)
    def _():
        acc_ref[:, :HALF] = far_ref[...]
        acc_ref[:, HALF:] = jnp.zeros((HEAD, HALF), jnp.float32)

    bias = [bias_ref[pl.ds(2 * at + half, 1), :] for half in (0, 1)]
    grad_key, grad_value = backward_block(kv_ref[...], q_ref, g_ref, row_ref, bias, ROWS, acc_ref)
    dkv_ref[:, :HEAD] = grad_key
    dkv_ref[:, HEAD:] = grad_value

    @pl.when(at == ROWS // BLOCK - 1)
    def _():
        for unit in range(8):
            lanes = slice(unit * UNIT, (unit + 1) * UNIT)
            tall_ref[lanes, :] = acc_ref[:, lanes].T * SCALE
        restore_rows(lambda rows: tall_ref[rows, :], dq_ref)


def restore_rows(read, target):
    for unit, residue in enumerate(ORDER):
        for block in range(32):
            start = unit * UNIT + 8 * block
            target[pl.ds(8 * block + residue, 8, stride=256), :] = read(slice(start, start + 8))


def join_kernel(dkv_ref, mine_ref, b1, b2, b3, b4, b5, b6, b7, far_ref, dq_in, dq_out, dk_out, dv_out, sum_ref, done_ref, tiles, sem):
    at = pl.program_id(0)

    def wide(ref, rows=slice(None)):
        return ref[rows, :].astype(jnp.float32)

    places = [(pl.ds(256 * step, 8), pl.ds(8 * step, 8)) for step in range(8)]
    reads = [pltpu.make_async_copy(dq_in.at[rows], tiles.at[spot], sem.at[n]) for n, (rows, spot) in enumerate(places)]
    writes = [pltpu.make_async_copy(tiles.at[spot], dq_out.at[rows], sem.at[8 + n]) for n, (rows, spot) in enumerate(places)]
    sends = [pltpu.make_async_copy(done_ref.at[n], out, sem.at[16 + n]) for n, out in enumerate((dk_out, dv_out))]

    @pl.when(at == 0)
    def _():
        for copy in reads:
            copy.start()

    top, mid, low = slice(0, 256), slice(256, 512), slice(512, 1024)
    near = wide(b1, top) + wide(b2, top) + wide(b3, top)
    sum_ref[top, :] = dkv_ref[top, :] + near + wide(b4) + wide(b5) + wide(b6) + wide(b7)
    sum_ref[mid, :] = dkv_ref[mid, :] + wide(b1, mid) + wide(b2, mid) + wide(b3, mid)
    sum_ref[low, :] = dkv_ref[low, :] + wide(b1, low)
    sum_ref[HALF:, :] = dkv_ref[HALF:, :]
    sum_ref[:8, :] += jnp.sum(wide(far_ref).reshape(FAR, 8, HEAD), 0)

    @pl.when(at == 0)
    def _():
        restore_rows(lambda rows: sum_ref[rows, :], done_ref.at[0])
        sends[0].start()
        mine = mine_ref[...]
        for ref in (b1, b2, b3):
            mine = mine + ref[ref.shape[0] - 16 :, :].astype(jnp.float32)[:8]
        mine = SCALE * mine
        for copy in reads:
            copy.wait()
        for step in range(8):
            tiles[8 * step : 8 * step + 1, :] += mine[step : step + 1, :]
        for copy in writes:
            copy.start()

    @pl.when(at == 1)
    def _():
        restore_rows(lambda rows: sum_ref[rows, :], done_ref.at[1])
        sends[1].start()
        for copy in writes + sends:
            copy.wait()


def swap(block, mask):
    return lax.ppermute(block, ("z", "y"), [(at, at ^ mask) for at in range(16)])


def swap_quad(block):
    parts = block.reshape(QUADS, 8, block.shape[1])
    return lax.all_to_all(parts, "y", 0, 0).reshape(block.shape)


def swap_far(block):
    parts = block.reshape(FAR, 8, block.shape[1])
    return lax.all_to_all(parts, ("grp", "x", "z"), 0, 0).reshape(block.shape)


def on_device(queries, keys, values, cotangent):
    f32, bf16 = jnp.float32, jnp.bfloat16
    near_bias, other_bias = jnp.asarray(own_bias()), jnp.asarray(far_bias())

    def both(*rows):
        return [((count, 256), bf16) for count in rows]

    wide = [pltpu.VMEM((ROWS, HEAD), f32)]
    kv, s1, s2, s3, far = call(
        prepare_keys_kernel, both(ROWS, 1040, 528, 256, 8 * FAR), (keys, values, queries, cotangent), wide
    )
    peers = [swap(block, mask) for block, mask in zip((s1, s2, s2, s3, s3), (1, 2, 3, 4, 5))]
    far = swap_far(far)
    state = [((8, HALF), f32), ((HEAD, HALF), f32)]
    stat, out, odd, q, g = call(
        own_forward_kernel,
        [*state, ((8, HALF), f32), ((ROWS, HEAD), bf16), ((ROWS, HEAD), bf16)],
        (queries, cotangent, kv, near_bias),
        [pltpu.VMEM((HEAD, ROWS), bf16), *wide],
        flops=LARGE,
    )
    stat, far, s3, peers[3], peers[4] = lax.optimization_barrier((stat, far, s3, peers[3], peers[4]))
    peers += [swap(s3, mask) for mask in (6, 7)]
    me = lax.axis_index("y").astype(jnp.int32).reshape(1)
    part, quad = call(
        whole_forward_kernel,
        [((8 * QUADS, 3 * HEAD), f32), *both(8 * QUADS)],
        (me, s2, *peers[:3], far),
        [pltpu.VMEM((8 * QUADS, 256), f32)],
        scalars=1,
        vmem=24,
    )
    part = swap_quad(part)
    stat, out = call(middle_forward_kernel, state, (q, other_bias, stat, out, *peers), first={0: (HALF, HEAD)})
    *third, third_dq, row, tall = call(
        finish_kernel,
        [*both(256, 256, 256, 256), ((HEAD, UNIT), f32), ((8, ROWS), f32), ((8 * QUADS, HEAD), f32)],
        (q, g, other_bias, stat, out, odd, part, *peers[3:]),
        [pltpu.VMEM((8, HEAD), f32), pltpu.VMEM((HEAD, HEAD), f32)],
        first={0: (UNIT, HEAD), 1: (HALF, HEAD), 2: (8, UNIT)},
    )
    tall = swap_quad(tall)
    back = [swap(block, mask) for block, mask in zip(third, (4, 5, 6, 7))]
    third_dq, tall = lax.optimization_barrier((third_dq, tall))
    *sends, far_dkv, far_dq, mine = call(
        remote_backward_kernel,
        [*both(1040, 528, 528, 8 * FAR), ((HEAD, HALF), f32), ((8, HEAD), f32)],
        (me, q, g, other_bias, row, quad, far, tall, third_dq, *peers[:3]),
        [pltpu.VMEM((8 * QUADS, HEAD), f32)],
        scalars=1,
        first={1: (HALF, HEAD), 2: (HALF, HEAD), 4: (8, HALF)},
    )
    back = [swap(block, mask) for block, mask in zip(sends, (1, 2, 3))] + back
    far_dkv = swap_far(far_dkv)
    dq, dkv = call(
        own_backward_kernel,
        [((ROWS, HEAD), f32), ((ROWS, 256), f32)],
        (q, g, near_bias, row, kv, far_dq),
        [pltpu.VMEM((HEAD, ROWS), f32), pltpu.VMEM((ROWS, HEAD), f32)],
        steps=(ROWS // BLOCK,),
        in_steps=(4,),
        out_steps=(1,),
        flops=LARGE,
    )
    dq, dk, dv = call(
        join_kernel,
        [((ROWS, HEAD), f32)] * 3,
        (dkv, mine, *back, far_dkv, dq),
        [
            pltpu.VMEM((ROWS, HEAD), f32),
            pltpu.VMEM((2, ROWS, HEAD), f32),
            pltpu.VMEM((64, HEAD), f32),
            pltpu.SemaphoreType.DMA((18,)),
        ],
        steps=(2,),
        lane_steps=(0, *range(2, 10)),
        in_place=10,
    )
    return dq, dk, dv


def solution(mesh):
    axes = ("grp", "x", "z", "y")
    split = jax.sharding.Mesh(mesh.devices.reshape(4, 4, 4, 4), axes)
    spec = P(axes, None)
    return jax.shard_map(
        on_device, mesh=split, in_specs=(spec,) * 4, out_specs=(spec,) * 3, check_vma=False
    )
```

```python
import functools
import math

import jax
import jax.numpy as jnp
import numpy as np
from jax import lax
from jax.experimental import pallas as pl
from jax.experimental.pallas import tpu as pltpu
from jax.sharding import PartitionSpec as P

ROWS = 2048
HEAD = 128
UNIT = 256
ORDER = (0, 4, 2, 6, 1, 3, 5, 7)
SCALE = HEAD**-0.5
SCALE2 = SCALE * math.log2(math.e)
NEG = -1e30
QUADS = 4
FAR = 64
BLOCK = 512
HALF = 1024
LARGE = 10**10


def unit_level(unit):
    return 3 if unit == 0 else 2 if unit == 1 else 1 if unit < 4 else 0


def own_bias():
    table = np.zeros((8, ROWS), np.float32)
    for key_unit in range(8):
        for query_unit in range(8):
            shared = 1 + min(unit_level(key_unit), unit_level(query_unit))
            table[key_unit, query_unit * UNIT : (query_unit + 1) * UNIT] = math.log2(shared)
    return table


def far_bias():
    table = np.zeros((8, 1024), np.float32)
    for query_unit in range(4):
        lanes = slice(query_unit * UNIT, (query_unit + 1) * UNIT)
        level = unit_level(query_unit)
        table[0, lanes] = math.log2(min(3, level))
        table[1, lanes] = math.log2(min(2, level))
        if level >= 2:
            table[2, lanes] = math.log2(level - 1)
    table[3, 8:] = NEG
    return table


def dot_nt(left, right):
    return lax.dot_general(left, right, (((1,), (1,)), ((), ())), preferred_element_type=jnp.float32)


def dot_nn(left, right):
    return lax.dot_general(left, right, (((1,), (0,)), ((), ())), preferred_element_type=jnp.float32)


def dot_tn(left, right):
    return lax.dot_general(left, right, (((0,), (0,)), ((), ())), preferred_element_type=jnp.float32)


def call(kernel, outs, args, scratch=(), scalars=0, steps=(), in_steps=(), out_steps=(), lane_steps=(), in_place=None, at_home=(), first=None, flops=0, vmem=60):
    first = first or {}
    steps = steps or ((1,) if first else ())

    def spec(shape, stepped, at_rest, scalar=False, part=None, by_lanes=False):
        if at_rest:
            return pl.BlockSpec(memory_space=pl.ANY)
        if scalar:
            return pl.BlockSpec(memory_space=pltpu.SMEM)
        if by_lanes:
            return pl.BlockSpec((shape[0], HEAD), lambda at: (0, at))
        if part is not None:
            return pl.BlockSpec(part, lambda *at: (0, 0))
        if not steps:
            return pl.BlockSpec(memory_space=pltpu.VMEM)
        if stepped:
            return pl.BlockSpec((BLOCK, shape[1]), lambda at: (at, 0))
        return pl.BlockSpec(shape, lambda at: (0, 0))

    return pl.pallas_call(
        kernel,
        grid=steps,
        out_shape=[jax.ShapeDtypeStruct(shape, dtype) for shape, dtype in outs],
        in_specs=[spec(arg.shape, at in in_steps, at == in_place or at in at_home, at < scalars, first.get(at), at in lane_steps) for at, arg in enumerate(args)],
        out_specs=[
            spec(shape, at in out_steps, bool(lane_steps)) for at, (shape, _) in enumerate(outs)
        ],
        scratch_shapes=list(scratch),
        input_output_aliases={} if in_place is None else {in_place: 0},
        compiler_params=pltpu.CompilerParams(vmem_limit_bytes=vmem << 20),
        cost_estimate=pl.CostEstimate(flops=flops, bytes_accessed=0, transcendentals=0),
    )(*args)


def sort_rows(source, target, lane, wide):
    wide[...] = source[...].astype(jnp.float32)
    for unit, residue in enumerate(ORDER):
        for pair in range(16):
            parts = [
                wide[pl.ds(8 * (2 * pair + half) + residue, 8, stride=256), :] for half in range(2)
            ]
            rows = slice(unit * UNIT + 16 * pair, unit * UNIT + 16 * pair + 16)
            target[rows, lane : lane + HEAD] = jnp.concatenate(parts, 0).astype(jnp.bfloat16)


def repeat_first(source, target, lane):
    first = source[:16, :].astype(jnp.float32)[:8]
    pair = jnp.concatenate([first, first], 0).astype(jnp.bfloat16)
    for at in range(0, target.shape[0], 16):
        target[at : at + 16, lane : lane + pair.shape[1]] = pair


def prepare_keys_kernel(k_ref, v_ref, q_ref, g_ref, kv_ref, s1_ref, s2_ref, s3_ref, far_ref, wide, tiles, sem):
    copies = []
    for index, ref in enumerate((q_ref, g_ref)):
        for at in range(8):
            source, target = ref.at[pl.ds(256 * at, 16)], tiles.at[index, pl.ds(16 * at, 16)]
            copies.append(pltpu.make_async_copy(source, target, sem.at[8 * index + at]))
    for copy in copies:
        copy.start()
    sort_rows(k_ref, kv_ref, 0, wide)
    sort_rows(v_ref, kv_ref, HEAD, wide)
    s1_ref[:1024] = kv_ref[:1024]
    s2_ref[:512] = kv_ref[:512]
    s3_ref[...] = kv_ref[:256]
    repeat_first(kv_ref, far_ref, 0)
    for copy in copies:
        copy.wait()
    for index, lane in enumerate((0, HEAD)):
        rows = [tiles[index, at : at + 16, :].astype(jnp.float32)[:1] for at in range(0, 128, 16)]
        block = jnp.concatenate(rows + rows, 0).astype(jnp.bfloat16)
        s1_ref[1024:, lane : lane + HEAD] = block
        s2_ref[512:, lane : lane + HEAD] = block


def add_bias(block, rows):
    if all(row is None for row in rows):
        return block
    parts = []
    for at, row in enumerate(rows):
        part = block[at * UNIT : (at + 1) * UNIT]
        parts.append(part if row is None else part + row)
    return jnp.concatenate(parts, 0)


def longest(rows):
    wide = rows.astype(jnp.float32)
    squares = dot_nt(jnp.ones((8, HEAD), jnp.bfloat16), (wide * wide).astype(jnp.bfloat16))
    return 1.01 * jnp.max(squares)


def attend(query, keys, values, biases, small=False):
    scores = [add_bias(dot_nt(key, query) * SCALE2, bias) for key, bias in zip(keys, biases)]
    if small:
        peak = jnp.zeros((1, query.shape[0]), jnp.float32)
        probs = [jnp.exp2(block) for block in scores]
    else:
        peak = functools.reduce(jnp.maximum, [jnp.max(block, 0, keepdims=True) for block in scores])
        probs = [jnp.exp2(block - peak) for block in scores]
    total = sum([jnp.sum(block, 0, keepdims=True) for block in probs])
    out = sum([value(block.astype(jnp.bfloat16)) for value, block in zip(values, probs)])
    return peak, total, out


def finish_rows(row_ref, target, stat, out, grad):
    total = stat[1:2]
    row_ref[0:1, target] = stat[0:1] + jnp.log2(total)
    row_ref[1:2, target] = jnp.sum(grad.astype(jnp.float32).T * out, axis=0, keepdims=True) / total


def own_forward_kernel(raw_q, raw_g, kv_ref, bias_ref, stat_ref, out_ref, odd_ref, q_ref, g_ref, vt_ref, wide):
    sort_rows(raw_q, q_ref, 0, wide)
    sort_rows(raw_g, g_ref, 0, wide)
    stat_ref[...] = jnp.zeros_like(stat_ref)
    odd_ref[...] = jnp.zeros_like(odd_ref)
    for unit in range(8):
        rows = slice(unit * UNIT, (unit + 1) * UNIT)
        vt_ref[:, rows] = kv_ref[rows, HEAD:].astype(jnp.float32).T.astype(jnp.bfloat16)
    def halves(small):
        for start in (0, HALF):
            lanes = slice(start, start + HALF)
            keys, values, biases = [], [], []
            for at in range(0, ROWS, BLOCK):
                rows = slice(at, at + BLOCK)
                keys.append(kv_ref[rows, :HEAD])
                values.append(lambda prob, rows=rows: dot_nn(vt_ref[:, rows], prob))
                unit = at // UNIT
                counted = start == 0 and at < HALF
                biases.append([bias_ref[unit + half : unit + half + 1, lanes] if counted else None for half in (0, 1)])
            peak, total, out = attend(q_ref[lanes, :], keys, values, biases, small)
            if start == 0:
                stat_ref[0:1, :] = peak
                stat_ref[1:2, :] = total
                out_ref[...] = out
            else:
                stat = jnp.concatenate([peak, total], 0)
                for first in range(0, HALF, UNIT):
                    part = slice(first, first + UNIT)
                    grad = g_ref[HALF + first : HALF + first + UNIT, :]
                    finish_rows(odd_ref, part, stat[:, part], out[:, part], grad)

    small = longest(q_ref[...]) * longest(kv_ref[:, :HEAD]) < (60.0 / SCALE2) ** 2
    pl.when(small)(functools.partial(halves, True))
    pl.when(jnp.logical_not(small))(functools.partial(halves, False))


def bias_rows(bias_ref, picks, count):
    return [None if pick is None else bias_ref[pick : pick + 1, :count] for pick in picks]


PARTNER, PARTNER_REST, SECOND, THIRD = (0, 1), (None, None), (2, None), (None, None)


def far_blocks(refs):
    third = (256, [(refs[-4:-2], THIRD), (refs[-2:], THIRD)])
    if len(refs) == 4:
        return (third,)
    near = (
        (1024, [((refs[0], 0), PARTNER), ((refs[0], BLOCK), PARTNER_REST)]),
        (512, [((ref, 0), SECOND) for ref in refs[1:3]]),
    )
    return near if len(refs) == 3 else (*near, third)


def read_block(place, lanes):
    ref, first = place
    if isinstance(first, int):
        return ref[first : first + BLOCK, lanes]
    return jnp.concatenate([ref[:, lanes], first[:, lanes]], 0)


def write_block(place, block):
    ref, first = place
    if isinstance(first, int):
        ref[first : first + BLOCK, :] = block
    else:
        ref[...] = block[:UNIT]
        first[...] = block[UNIT:]


def join_state(sums, acc, lanes, far_peak, far_total, far_out):
    peak = sums[0:1, lanes]
    top = jnp.maximum(peak, far_peak)
    near, far = jnp.exp2(peak - top), jnp.exp2(far_peak - top)
    sums[0:1, lanes] = top
    sums[1:2, lanes] = near * sums[1:2, lanes] + far * far_total
    acc[:, lanes] = near * acc[:, lanes] + far * far_out


def middle_forward_kernel(q_ref, bias_ref, stat_ref, out_ref, *rest):
    peers, (sums, acc) = rest[:7], rest[7:]
    sums[...] = stat_ref[...]
    acc[...] = out_ref[...]
    for count, blocks in far_blocks(peers):
        lanes = slice(0, count)
        state = attend(
            q_ref[lanes, :],
            [read_block(place, slice(0, HEAD)) for place, _ in blocks],
            [lambda prob, place=place: dot_tn(read_block(place, slice(HEAD, 256)), prob) for place, _ in blocks],
            [bias_rows(bias_ref, picks, count) for _, picks in blocks],
        )
        join_state(sums, acc, lanes, *state)


def whole_forward_kernel(me_ref, own, r1, r2, r3, far_ref, part_ref, quad_ref, rows_ref):
    for mask, ref in enumerate((own, r1, r2, r3)):
        count = ref.shape[0]
        place = pl.multiple_of((me_ref[0] ^ mask) * 8, 8)
        rows_ref[pl.ds(place, 8), :] = ref[count - 16 :, :].astype(jnp.float32)[:8]
    quad_ref[...] = rows_ref[...].astype(jnp.bfloat16)
    scores = dot_nt(quad_ref[:, :HEAD], far_ref[:, :HEAD]) * SCALE2
    peak = jnp.max(scores, 1, keepdims=True)
    prob = jnp.exp2(scores - peak)
    part_ref[:, :HEAD] = dot_nn(prob.astype(jnp.bfloat16), far_ref[:, HEAD:])
    part_ref[:, HEAD : 2 * HEAD] = jnp.broadcast_to(peak, (8 * QUADS, HEAD))
    part_ref[:, 2 * HEAD :] = jnp.broadcast_to(jnp.sum(prob, 1, keepdims=True), (8 * QUADS, HEAD))


def turn(block, fill):
    return jnp.concatenate([block, jnp.full((HEAD - 8, HEAD), fill, jnp.float32)], 0).T


def finish_kernel(q_ref, g_ref, bias_ref, stat_ref, out_ref, odd_ref, part_ref, *rest):
    far, third, (dq_ref, row_ref, tall_ref, sums, acc) = rest[:4], rest[4:8], rest[8:]
    lanes = slice(0, HEAD)
    sums[...] = stat_ref[:, lanes]
    acc[...] = out_ref[:, lanes]
    for at in range(0, 8 * QUADS, 8):
        part = part_ref[at : at + 8, :]
        far_out = turn(part[:, :HEAD], 0.0)
        far_peak = turn(part[:, HEAD : 2 * HEAD], NEG)[0:1]
        far_total = turn(part[:, 2 * HEAD :], 0.0)[0:1]
        join_state(sums, acc, lanes, far_peak, far_total, far_out)
    row_ref[...] = jnp.zeros_like(row_ref)
    row_ref[:, HALF:] = odd_ref[...]
    for first in range(0, HALF, HEAD):
        lanes = slice(first, first + HEAD)
        stat, out = (sums[...], acc[...]) if first == 0 else (stat_ref[:, lanes], out_ref[:, lanes])
        finish_rows(row_ref, lanes, stat, out, g_ref[lanes, :])
    tall = jnp.concatenate([row_ref[:, :HEAD], jnp.zeros((HEAD - 8, HEAD), jnp.float32)], 0).T
    for at in range(0, 8 * QUADS, 8):
        tall_ref[at : at + 8, :] = tall[:8]
    dq_ref[...] = jnp.zeros_like(dq_ref)
    backward_far(far, third, (q_ref, g_ref, bias_ref, row_ref), dq_ref)


def remote_backward_kernel(me_ref, q_ref, g_ref, bias_ref, row_ref, quad_ref, far_ref, tall_ref, *rest):
    third_dq, far, outs, (dkv_ref, dq_ref, mine_ref, quad_dq) = rest[0], rest[1:4], rest[4:7], rest[7:]
    query, grad = quad_ref[:, :HEAD], quad_ref[:, HEAD:]
    key, value = far_ref[:, :HEAD], far_ref[:, HEAD:]
    weights = jnp.exp2(dot_nt(query, key) * SCALE2 - tall_ref[:, 0:1])
    grad_scores = (weights * (dot_nt(grad, value) - tall_ref[:, 1:2])).astype(jnp.bfloat16)
    dkv_ref[:, :HEAD] = (SCALE * dot_tn(grad_scores, query)).astype(jnp.bfloat16)
    dkv_ref[:, HEAD:] = dot_tn(weights.astype(jnp.bfloat16), grad).astype(jnp.bfloat16)
    quad_dq[...] = dot_nn(grad_scores, key)
    for mask in range(QUADS):
        place = pl.multiple_of((me_ref[0] ^ mask) * 8, 8)
        block = quad_dq[pl.ds(place, 8), :]
        if mask == 0:
            mine_ref[...] = block
        else:
            block = jnp.concatenate([block, jnp.zeros_like(block)], 0)
            block = jnp.concatenate([block, jnp.zeros_like(block)], 1).astype(jnp.bfloat16)
            rows = outs[mask - 1].shape[0]
            outs[mask - 1][rows - 16 :, :] = block
    dq_ref[...] = jnp.zeros_like(dq_ref)
    dq_ref[:, :UNIT] = third_dq[...]
    backward_far(far, outs, (q_ref, g_ref, bias_ref, row_ref), dq_ref)


def backward_block(kv_block, q_ref, g_ref, row_ref, bias, count, dq_ref):
    key, value = kv_block[:, :HEAD], kv_block[:, HEAD:]
    lanes = slice(0, count)
    query, grad = q_ref[lanes, :], g_ref[lanes, :]
    scores = add_bias(dot_nt(key, query) * SCALE2, bias)
    weights = jnp.exp2(scores - row_ref[0:1, lanes])
    grad_probs = dot_nt(value, grad)
    grad_scores = (weights * (grad_probs - row_ref[1:2, lanes])).astype(jnp.bfloat16)
    grad_value = dot_nn(weights.astype(jnp.bfloat16), grad)
    grad_key = dot_nn(grad_scores, query)
    dq_ref[:, lanes] += dot_tn(key, grad_scores)
    return SCALE * grad_key, grad_value


def backward_far(far, outs, refs, dq_ref):
    q_ref, g_ref, bias_ref, row_ref = refs
    for (count, blocks), (_, places) in zip(far_blocks(far), far_blocks(outs)):
        for (place, picks), (target, _) in zip(blocks, places):
            bias = bias_rows(bias_ref, picks, count)
            both = backward_block(read_block(place, slice(0, 256)), q_ref, g_ref, row_ref, bias, count, dq_ref)
            write_block(target, jnp.concatenate(both, 1).astype(jnp.bfloat16))


def own_backward_kernel(q_ref, g_ref, bias_ref, row_ref, kv_ref, far_ref, dq_ref, dkv_ref, acc_ref, tall_ref):
    at = pl.program_id(0)

    @pl.when(at == 0)
    def _():
        acc_ref[:, :HALF] = far_ref[...]
        acc_ref[:, HALF:] = jnp.zeros((HEAD, HALF), jnp.float32)

    bias = [bias_ref[pl.ds(2 * at + half, 1), :] for half in (0, 1)]
    grad_key, grad_value = backward_block(kv_ref[...], q_ref, g_ref, row_ref, bias, ROWS, acc_ref)
    dkv_ref[:, :HEAD] = grad_key
    dkv_ref[:, HEAD:] = grad_value

    @pl.when(at == ROWS // BLOCK - 1)
    def _():
        for unit in range(8):
            lanes = slice(unit * UNIT, (unit + 1) * UNIT)
            tall_ref[lanes, :] = acc_ref[:, lanes].T * SCALE
        restore_rows(lambda rows: tall_ref[rows, :], dq_ref)


def restore_rows(read, target):
    for unit, residue in enumerate(ORDER):
        for block in range(32):
            start = unit * UNIT + 8 * block
            target[pl.ds(8 * block + residue, 8, stride=256), :] = read(slice(start, start + 8))


def join_kernel(dkv_ref, mine_ref, b1, b2, b3, b4, b5, b6, b7, far_ref, dq_in, dq_out, dk_out, dv_out, sum_ref, done_ref, tiles, sem):
    at = pl.program_id(0)

    def wide(ref, rows=slice(None)):
        return ref[rows, :].astype(jnp.float32)

    places = [(pl.ds(256 * step, 8), pl.ds(8 * step, 8)) for step in range(8)]
    reads = [pltpu.make_async_copy(dq_in.at[rows], tiles.at[spot], sem.at[n]) for n, (rows, spot) in enumerate(places)]
    writes = [pltpu.make_async_copy(tiles.at[spot], dq_out.at[rows], sem.at[8 + n]) for n, (rows, spot) in enumerate(places)]
    sends = [pltpu.make_async_copy(done_ref.at[n], out, sem.at[16 + n]) for n, out in enumerate((dk_out, dv_out))]

    @pl.when(at == 0)
    def _():
        for copy in reads:
            copy.start()

    top, mid, low = slice(0, 256), slice(256, 512), slice(512, 1024)
    near = wide(b1, top) + wide(b2, top) + wide(b3, top)
    sum_ref[top, :] = dkv_ref[top, :] + near + wide(b4) + wide(b5) + wide(b6) + wide(b7)
    sum_ref[mid, :] = dkv_ref[mid, :] + wide(b1, mid) + wide(b2, mid) + wide(b3, mid)
    sum_ref[low, :] = dkv_ref[low, :] + wide(b1, low)
    sum_ref[HALF:, :] = dkv_ref[HALF:, :]
    sum_ref[:8, :] += jnp.sum(wide(far_ref).reshape(FAR, 8, HEAD), 0)

    @pl.when(at == 0)
    def _():
        restore_rows(lambda rows: sum_ref[rows, :], done_ref.at[0])
        sends[0].start()
        mine = mine_ref[...]
        for ref in (b1, b2, b3):
            mine = mine + ref[ref.shape[0] - 16 :, :].astype(jnp.float32)[:8]
        mine = SCALE * mine
        for copy in reads:
            copy.wait()
        for step in range(8):
            tiles[8 * step : 8 * step + 1, :] += mine[step : step + 1, :]
        for copy in writes:
            copy.start()

    @pl.when(at == 1)
    def _():
        restore_rows(lambda rows: sum_ref[rows, :], done_ref.at[1])
        sends[1].start()
        for copy in writes + sends:
            copy.wait()


def swap(block, mask):
    return lax.ppermute(block, ("z", "y"), [(at, at ^ mask) for at in range(16)])


def swap_quad(block):
    parts = block.reshape(QUADS, 8, block.shape[1])
    return lax.all_to_all(parts, "y", 0, 0).reshape(block.shape)


def swap_far(block):
    parts = block.reshape(FAR, 8, block.shape[1])
    return lax.all_to_all(parts, ("grp", "x", "z"), 0, 0).reshape(block.shape)


def on_device(queries, keys, values, cotangent):
    f32, bf16 = jnp.float32, jnp.bfloat16
    near_bias, other_bias = jnp.asarray(own_bias()), jnp.asarray(far_bias())

    def both(*rows):
        return [((count, 256), bf16) for count in rows]

    wide = [pltpu.VMEM((ROWS, HEAD), f32)]
    kv, s1, s2, s3, far = call(
        prepare_keys_kernel, both(ROWS, 1040, 528, 256, 8 * FAR), (keys, values, queries, cotangent),
        [*wide, pltpu.VMEM((2, 128, HEAD), bf16), pltpu.SemaphoreType.DMA((16,))],
        at_home=(2, 3),
    )
    peers = [swap(block, mask) for block, mask in zip((s1, s2, s2, s3, s3), (1, 2, 3, 4, 5))]
    far = swap_far(far)
    state = [((8, HALF), f32), ((HEAD, HALF), f32)]
    stat, out, odd, q, g = call(
        own_forward_kernel,
        [*state, ((8, HALF), f32), ((ROWS, HEAD), bf16), ((ROWS, HEAD), bf16)],
        (queries, cotangent, kv, near_bias),
        [pltpu.VMEM((HEAD, ROWS), bf16), *wide],
        flops=LARGE,
    )
    stat, far, s3, peers[3], peers[4] = lax.optimization_barrier((stat, far, s3, peers[3], peers[4]))
    peers += [swap(s3, mask) for mask in (6, 7)]
    me = lax.axis_index("y").astype(jnp.int32).reshape(1)
    part, quad = call(
        whole_forward_kernel,
        [((8 * QUADS, 3 * HEAD), f32), *both(8 * QUADS)],
        (me, s2, *peers[:3], far),
        [pltpu.VMEM((8 * QUADS, 256), f32)],
        scalars=1,
        vmem=24,
    )
    part = swap_quad(part)
    stat, out = call(middle_forward_kernel, state, (q, other_bias, stat, out, *peers), first={0: (HALF, HEAD)})
    *third, third_dq, row, tall = call(
        finish_kernel,
        [*both(256, 256, 256, 256), ((HEAD, UNIT), f32), ((8, ROWS), f32), ((8 * QUADS, HEAD), f32)],
        (q, g, other_bias, stat, out, odd, part, *peers[3:]),
        [pltpu.VMEM((8, HEAD), f32), pltpu.VMEM((HEAD, HEAD), f32)],
        first={0: (UNIT, HEAD), 1: (HALF, HEAD), 2: (8, UNIT)},
    )
    tall = swap_quad(tall)
    back = [swap(block, mask) for block, mask in zip(third, (4, 5, 6, 7))]
    third_dq, tall = lax.optimization_barrier((third_dq, tall))
    *sends, far_dkv, far_dq, mine = call(
        remote_backward_kernel,
        [*both(1040, 528, 528, 8 * FAR), ((HEAD, HALF), f32), ((8, HEAD), f32)],
        (me, q, g, other_bias, row, quad, far, tall, third_dq, *peers[:3]),
        [pltpu.VMEM((8 * QUADS, HEAD), f32)],
        scalars=1,
        first={1: (HALF, HEAD), 2: (HALF, HEAD), 4: (8, HALF)},
    )
    back = [swap(block, mask) for block, mask in zip(sends, (1, 2, 3))] + back
    far_dkv = swap_far(far_dkv)
    dq, dkv = call(
        own_backward_kernel,
        [((ROWS, HEAD), f32), ((ROWS, 256), f32)],
        (q, g, near_bias, row, kv, far_dq),
        [pltpu.VMEM((HEAD, ROWS), f32), pltpu.VMEM((ROWS, HEAD), f32)],
        steps=(ROWS // BLOCK,),
        in_steps=(4,),
        out_steps=(1,),
        flops=LARGE,
    )
    dq, dk, dv = call(
        join_kernel,
        [((ROWS, HEAD), f32)] * 3,
        (dkv, mine, *back, far_dkv, dq),
        [
            pltpu.VMEM((ROWS, HEAD), f32),
            pltpu.VMEM((2, ROWS, HEAD), f32),
            pltpu.VMEM((64, HEAD), f32),
            pltpu.SemaphoreType.DMA((18,)),
        ],
        steps=(2,),
        lane_steps=(0, *range(2, 10)),
        in_place=10,
    )
    return dq, dk, dv


def solution(mesh):
    axes = ("grp", "x", "z", "y")
    split = jax.sharding.Mesh(mesh.devices.reshape(4, 4, 4, 4), axes)
    spec = P(axes, None)
    return jax.shard_map(
        on_device, mesh=split, in_specs=(spec,) * 4, out_specs=(spec,) * 3, check_vma=False
    )
```
